256 devices in a mesh: ctx: 16 (over z_hi, y, core), head: 16 (over z_lo, x).
Axes of the slice: x: 4, y: 4, z: 8 (z_hi: 2, z_lo: 4; z = z_hi * 4 + z_lo), core: 2. Of those that a mesh axis runs over, the one named last changes fastest.
Arguments:
- queries: bfloat16 [32768, 2048], P(('ctx', 'head')), may hold values from -10 to 10
- keys: bfloat16 [32768, 2048], P(('ctx', 'head')), may hold values from -10 to 10
- values: bfloat16 [32768, 2048], P(('ctx', 'head')), may hold values from -6 to 6
- out_grad: bfloat16 [32768, 2048], P(('ctx', 'head')), may hold values from -6 to 6
- key_lists: int32 [256, 4], replicated, may hold values from 0 to 255, as said below
Outputs:
- attended: bfloat16 [32768, 2048], P(('ctx', 'head'))
- query_grad: bfloat16 [32768, 2048], P(('ctx', 'head'))
- key_grad: bfloat16 [32768, 2048], P(('ctx', 'head'))
- value_grad: bfloat16 [32768, 2048], P(('ctx', 'head'))
The draws below stay inside these ranges and needn't reach their ends.
Inputs may be any that keep to these rules, and one draw needn't show every extreme that they name: `key_lists`: row n lists block n in slot 0 and block (n - 1) mod 256 in slot 1; slots 2 and 3 name blocks of slabs other than n's own slab of 16 blocks. Over the 32 entries in slots 2 and 3 of one slab's rows, each other slab is named floor or ceil of 2 * 16 / 15 times, some slab exactly 3 times.
All inputs are finite; a program needn't handle non-finite values.
Results may differ from the reference program's by a relative error of at most 0.029.
Values may be sent and summed in bfloat16 or wider, within the bound.
No kernel may reach another device: no remote copies, remote signals or barrier semaphores. Data moves between devices by JAX's collectives and lax.ppermute only.
A program may use at most 128 MiB of HBM per device.

```python
import jax
import jax.numpy as jnp
from jax import lax

HEADS = 16
HEAD_DIM = 128
BLOCK = 128
SLOTS = 4
SEQ = 32768
QB = 16
NBLK = 256
N_CTX = 16


def draw_queries(key, part):
    key = jax.random.fold_in(key, 1)
    return jnp.clip(jax.random.normal(key, (SEQ, HEADS * HEAD_DIM), jnp.float32), -6.0, 6.0).astype(jnp.bfloat16)


def draw_keys(key, part):
    key = jax.random.fold_in(key, 2)
    return jnp.clip(jax.random.normal(key, (SEQ, HEADS * HEAD_DIM), jnp.float32), -6.0, 6.0).astype(jnp.bfloat16)


def draw_key_lists(key, part):
    key = jax.random.fold_in(key, 7)
    requests = 2 * QB
    request_order = jax.vmap(lambda subkey: jax.random.permutation(subkey, requests))(jax.random.split(jax.random.fold_in(key, 1), N_CTX))
    shuffle = jax.vmap(lambda subkey: jax.random.permutation(subkey, N_CTX - 1))(jax.random.split(jax.random.fold_in(key, 2), N_CTX))
    offset = 1 + jnp.take_along_axis(shuffle, request_order % (N_CTX - 1), axis=1)
    far_slab = (jnp.arange(N_CTX)[:, None] + offset) % N_CTX
    inside = jax.random.randint(jax.random.fold_in(key, 3), (N_CTX, requests), 0, QB)
    far_blocks = (far_slab * QB + inside).reshape(NBLK, 2)
    own_block = jnp.arange(NBLK)
    prev_block = (own_block + NBLK - 1) % NBLK
    return jnp.concatenate([own_block[:, None], prev_block[:, None], far_blocks], axis=1).astype(jnp.int32)


def shard_levels(rng, dims, shards, low, largest):
    factor_of = 1.0
    for axis_at, parts in shards:
        heights = jax.random.uniform(jax.random.fold_in(jax.random.fold_in(rng, 6), axis_at), (parts,), jnp.float32, low / len(shards), largest / len(shards))
        factor_of = factor_of * jnp.repeat(jnp.exp(heights), dims[axis_at] // parts).reshape((-1,) + (1,) * (len(dims) - 1 - axis_at))
    return factor_of


def scatter_about(stream_key, dims, width, most, cuts=(), held_as=jnp.bfloat16):
    factor_of = shard_levels(stream_key, dims, cuts, -0.22, 0.18) if cuts else 1.0
    entries = jax.random.normal(stream_key, dims, jnp.float32) * width * factor_of
    return jnp.minimum(jnp.maximum(entries, -most), most).astype(held_as)


def setup_inputs(seed: int = 0) -> dict:
    arg_keys = jax.random.split(jax.random.key(seed), 6)
    return {
        "queries": draw_queries(jax.random.fold_in(arg_keys[5], 71), 0),
        "keys": draw_keys(jax.random.fold_in(arg_keys[5], 71), 0),
        "values": scatter_about(arg_keys[2], (SEQ, HEADS * HEAD_DIM), 1.0, 6.0, ((0, 256),)),
        "out_grad": scatter_about(arg_keys[3], (SEQ, HEADS * HEAD_DIM), 1.0, 6.0, ((0, 256),)),
        "key_lists": draw_key_lists(jax.random.fold_in(arg_keys[5], 71), 0),
    }


def reference(queries, keys, values, out_grad, key_lists):
    score_scale = HEAD_DIM ** -0.5
    flat_list = key_lists.reshape(-1)
    highest = lax.Precision.HIGHEST

    def split_heads(array):
        return array.reshape(NBLK, BLOCK, HEADS, HEAD_DIM).transpose(2, 0, 1, 3)

    def one_head(head_data):
        query_h, key_h, value_h, grad_h = head_data
        listed_keys = key_h[key_lists].reshape(NBLK, SLOTS * BLOCK, HEAD_DIM).astype(jnp.float32)
        listed_values = value_h[key_lists].reshape(NBLK, SLOTS * BLOCK, HEAD_DIM).astype(jnp.float32)
        query_f = query_h.astype(jnp.float32)
        grad_f = grad_h.astype(jnp.float32)
        scores = jnp.einsum("nbd,nkd->nbk", query_f, listed_keys, precision=highest) * score_scale
        row_max = jnp.max(scores, axis=-1, keepdims=True)
        weights = jnp.exp(scores - row_max)
        probs = weights / jnp.sum(weights, axis=-1, keepdims=True)
        probs_low = lax.optimization_barrier(probs.astype(jnp.bfloat16)).astype(jnp.float32)
        attended = jnp.einsum("nbk,nkd->nbd", probs_low, listed_values, precision=highest).astype(jnp.bfloat16)
        attended_f = lax.optimization_barrier(attended).astype(jnp.float32)
        row_delta = jnp.sum(grad_f * attended_f, axis=-1)
        dprob = jnp.einsum("nbd,nkd->nbk", grad_f, listed_values, precision=highest)
        dscore = (probs * (dprob - row_delta[..., None]) * score_scale).astype(jnp.bfloat16)
        dscore_f = lax.optimization_barrier(dscore).astype(jnp.float32)
        query_grad = jnp.einsum("nbk,nkd->nbd", dscore_f, listed_keys, precision=highest).astype(jnp.bfloat16)
        key_parts = jnp.einsum("nbk,nbd->nkd", dscore_f, query_f, precision=highest).reshape(NBLK * SLOTS, BLOCK, HEAD_DIM)
        value_parts = jnp.einsum("nbk,nbd->nkd", probs_low, grad_f, precision=highest).reshape(NBLK * SLOTS, BLOCK, HEAD_DIM)
        key_grad = jax.ops.segment_sum(key_parts, flat_list, num_segments=NBLK).astype(jnp.bfloat16)
        value_grad = jax.ops.segment_sum(value_parts, flat_list, num_segments=NBLK).astype(jnp.bfloat16)
        return attended, query_grad, key_grad, value_grad

    results = lax.map(one_head, (split_heads(queries), split_heads(keys), split_heads(values), split_heads(out_grad)))

    def join_heads(array):
        return array.transpose(1, 2, 0, 3).reshape(SEQ, HEADS * HEAD_DIM)

    return (join_heads(results[0]), join_heads(results[1]), join_heads(results[2]), join_heads(results[3]))
```

```python
import functools

import jax
import jax.numpy as jnp
from jax import lax
from jax.experimental import pallas as pl
from jax.experimental.pallas import tpu as pltpu
from jax.sharding import PartitionSpec as P

HEAD_DIM = 128
BLOCK = 128
VMEM_LIMIT = 48 * 1024 * 1024
ANY = pl.BlockSpec(memory_space=pl.ANY)
VMEM = pl.BlockSpec(memory_space=pltpu.VMEM)
SMEM = pl.BlockSpec(memory_space=pltpu.SMEM)


def params():
    return pltpu.CompilerParams(vmem_limit_bytes=VMEM_LIMIT)


def cost(flops, nbytes):
    return pl.CostEstimate(flops=flops, bytes_accessed=nbytes, transcendentals=0)


def split_kernel(heads, first_ref, second_ref, out_ref, sems):
    copies = []
    for which, ref in enumerate((first_ref, second_ref)):
        for head in range(heads):
            copies.append(
                pltpu.make_async_copy(
                    ref.at[:, pl.ds(head * HEAD_DIM, HEAD_DIM)],
                    out_ref.at[head, which],
                    sems.at[which * heads + head],
                )
            )
    for copy in copies:
        copy.start()
    for copy in copies:
        copy.wait()


def split_heads(first, second):
    rows, features = first.shape
    heads = features // HEAD_DIM
    return pl.pallas_call(
        functools.partial(split_kernel, heads),
        out_shape=jax.ShapeDtypeStruct((heads, 2, rows, HEAD_DIM), first.dtype),
        in_specs=[ANY, ANY],
        out_specs=ANY,
        scratch_shapes=[pltpu.SemaphoreType.DMA((2 * heads,))],
        compiler_params=params(),
        cost_estimate=cost(0, 4 * first.size * 2),
        name="split_heads",
    )(first, second)


def join_kernel(heads, in_ref, first_ref, second_ref, sems):
    copies = []
    for which, ref in enumerate((first_ref, second_ref)):
        for head in range(heads):
            copies.append(
                pltpu.make_async_copy(
                    in_ref.at[head, which],
                    ref.at[:, pl.ds(head * HEAD_DIM, HEAD_DIM)],
                    sems.at[which * heads + head],
                )
            )
    for copy in copies:
        copy.start()
    for copy in copies:
        copy.wait()


def join_heads(both):
    heads, _, rows, depth = both.shape
    shape = jax.ShapeDtypeStruct((rows, heads * depth), both.dtype)
    return pl.pallas_call(
        functools.partial(join_kernel, heads),
        out_shape=(shape, shape),
        in_specs=[ANY],
        out_specs=(ANY, ANY),
        scratch_shapes=[pltpu.SemaphoreType.DMA((2 * heads,))],
        compiler_params=params(),
        cost_estimate=cost(0, 2 * both.size * 2),
        name="join_heads",
    )(both)


def pick_kernel(slots, index_ref, in_ref, out_ref, sems):
    copies = [
        pltpu.make_async_copy(in_ref.at[index_ref[slot]], out_ref.at[slot], sems.at[slot])
        for slot in range(slots)
    ]
    for copy in copies:
        copy.start()
    for copy in copies:
        copy.wait()


def pick_blocks(index, blocks):
    slots = index.shape[0]
    return pl.pallas_call(
        functools.partial(pick_kernel, slots),
        out_shape=jax.ShapeDtypeStruct((slots,) + blocks.shape[1:], blocks.dtype),
        in_specs=[SMEM, VMEM],
        out_specs=ANY,
        scratch_shapes=[pltpu.SemaphoreType.DMA((slots,))],
        compiler_params=params(),
        cost_estimate=cost(0, 2 * slots * blocks[0].size * 2),
        name="pick_blocks",
    )(index, blocks)


def attend_kernel(blocks, slot_ref, qg_ref, kv_ref, edge_ref, far_ref, out_ref, far_out_ref, edge_out_ref, sum_ref):
    scale = HEAD_DIM ** (-0.5)
    f32, bf16 = jnp.float32, jnp.bfloat16

    def dot(a, b, dims):
        return lax.dot_general(a, b, (dims, ((), ())), preferred_element_type=f32)

    def one(n, first):
        q, g = qg_ref[n, 0], qg_ref[n, 1]
        s2, s3 = slot_ref[2 * n], slot_ref[2 * n + 1]
        if first:
            prev_k, prev_v = edge_ref[0], edge_ref[1]
        else:
            prev_k, prev_v = kv_ref[n - 1, 0], kv_ref[n - 1, 1]
        k = jnp.concatenate([kv_ref[n, 0], prev_k, far_ref[s2, 0], far_ref[s3, 0]], axis=0)
        v = jnp.concatenate([kv_ref[n, 1], prev_v, far_ref[s2, 1], far_ref[s3, 1]], axis=0)
        s = dot(k, q, ((1,), (1,))) * scale
        dp = dot(v, g, ((1,), (1,)))
        w = jnp.exp(s - jnp.max(s, axis=0, keepdims=True))
        p = w * (1.0 / jnp.sum(w, axis=0, keepdims=True))
        p_low = p.astype(bf16)
        delta = jnp.sum(p_low.astype(f32) * dp, axis=0, keepdims=True)
        ds = (p * (dp - delta) * scale).astype(bf16)
        out_ref[n, 0] = dot(p_low, v, ((0,), (0,))).astype(bf16)
        out_ref[n, 1] = dot(ds, k, ((0,), (0,))).astype(bf16)
        dk = dot(ds, q, ((1,), (0,)))
        dv = dot(p_low, g, ((1,), (0,)))
        for which, d in enumerate((dk, dv)):
            sum_ref[n, which] = d[:BLOCK]
            if first:
                edge_out_ref[which] = d[BLOCK : 2 * BLOCK].astype(bf16)
            else:
                sum_ref[n - 1, which] += d[BLOCK : 2 * BLOCK]
            far_out_ref[s2, which] = d[2 * BLOCK : 3 * BLOCK].astype(bf16)
            far_out_ref[s3, which] = d[3 * BLOCK :].astype(bf16)

    far_out_ref[...] = jnp.zeros_like(far_out_ref)
    one(0, True)
    lax.fori_loop(1, blocks, lambda n, _: one(n, False), None)


def attend(slot, qg, kv, edge, far):
    blocks = qg.shape[0]
    bf16 = jnp.bfloat16
    return pl.pallas_call(
        functools.partial(attend_kernel, blocks),
        out_shape=(
            jax.ShapeDtypeStruct(qg.shape, bf16),
            jax.ShapeDtypeStruct(far.shape, bf16),
            jax.ShapeDtypeStruct(edge.shape, bf16),
            jax.ShapeDtypeStruct(kv.shape, jnp.float32),
        ),
        in_specs=[SMEM, VMEM, VMEM, VMEM, VMEM],
        out_specs=(VMEM, VMEM, VMEM, VMEM),
        compiler_params=params(),
        cost_estimate=cost(
            5 * 2 * blocks * 4 * BLOCK * BLOCK * HEAD_DIM, 2 * (2 * qg.size + 3 * kv.size + 2 * far.size)
        ),
        name="attend",
    )(slot, qg, kv, edge, far)


def land_kernel(slots, blocks, index_ref, valid_ref, sum_ref, back_ref, home_ref, out_ref, total):
    total[...] = sum_ref[...]
    total[blocks - 1] += back_ref[...].astype(jnp.float32)

    def one(slot, _):
        @pl.when(valid_ref[slot] != 0)
        def _():
            total[index_ref[slot]] += home_ref[slot].astype(jnp.float32)

    lax.fori_loop(0, slots, one, None)
    out_ref[...] = total[...].astype(out_ref.dtype)


def land(index, valid, sums, back, home):
    slots = index.shape[0]
    blocks = sums.shape[0]
    return pl.pallas_call(
        functools.partial(land_kernel, slots, blocks),
        out_shape=jax.ShapeDtypeStruct(sums.shape, jnp.bfloat16),
        in_specs=[SMEM, SMEM, VMEM, VMEM, VMEM],
        out_specs=VMEM,
        scratch_shapes=[pltpu.VMEM(sums.shape, jnp.float32)],
        compiler_params=params(),
        cost_estimate=cost(sums.size * 4, 6 * sums.size + 2 * home.size),
        name="land",
    )(index, valid, sums, back, home)


def body(queries, keys, values, out_grad, key_lists):
    ctx_count = lax.axis_size("ctx")
    ctx_rank = lax.axis_index("ctx")
    blocks = lax.axis_size("head")
    requests = 2 * blocks
    capacity = (requests + ctx_count - 2) // (ctx_count - 1)

    far_all = key_lists[:, 2:].reshape(ctx_count, requests)
    source = far_all // blocks
    earlier = jnp.arange(requests)[None, :] < jnp.arange(requests)[:, None]
    rank = jnp.sum(
        ((source[:, None, :] == source[:, :, None]) & earlier[None]).astype(jnp.int32), axis=2
    )
    slot_of = source * capacity + rank
    is_mine = jnp.arange(ctx_count) == ctx_rank
    my_slot = jnp.sum(jnp.where(is_mine[:, None], slot_of, 0), axis=0)
    wanted = (
        slot_of[:, None, :] == ctx_rank * capacity + jnp.arange(capacity, dtype=jnp.int32)[None, :, None]
    )
    send_index = jnp.sum(jnp.where(wanted, far_all[:, None, :] % blocks, 0), axis=2).reshape(-1)
    send_valid = jnp.sum(wanted.astype(jnp.int32), axis=2).reshape(-1)

    def head_exchange(array):
        return lax.all_to_all(array, "head", split_axis=0, concat_axis=0, tiled=True)

    def ctx_exchange(array):
        return lax.all_to_all(array, "ctx", split_axis=0, concat_axis=0, tiled=True)

    def shift(array, by):
        return lax.ppermute(
            array, "ctx", [(i, (i + by) % ctx_count) for i in range(ctx_count)]
        )

    kv = head_exchange(split_heads(keys, values))
    qg = head_exchange(split_heads(queries, out_grad))
    edge = shift(kv[blocks - 1], 1)
    far = ctx_exchange(pick_blocks(send_index, kv))
    out, far_grad, edge_grad, sums = attend(my_slot, qg, kv, edge, far)
    home = ctx_exchange(far_grad)
    back = shift(edge_grad, -1)
    attended, query_grad = join_heads(head_exchange(out))
    key_grad, value_grad = join_heads(head_exchange(land(send_index, send_valid, sums, back, home)))
    return attended, query_grad, key_grad, value_grad


def solution(mesh):
    tokens = P(("ctx", "head"), None)
    return jax.shard_map(
        body,
        mesh=mesh,
        in_specs=(tokens, tokens, tokens, tokens, P()),
        out_specs=(tokens, tokens, tokens, tokens),
        check_vma=False,
    )
```

```python
import functools

import jax
import jax.numpy as jnp
from jax import lax
from jax.experimental import pallas as pl
from jax.experimental.pallas import tpu as pltpu
from jax.sharding import PartitionSpec as P

HEAD_DIM = 128
BLOCK = 128
VMEM_LIMIT = 48 * 1024 * 1024
ANY = pl.BlockSpec(memory_space=pl.ANY)
HBM = pl.BlockSpec(memory_space=pltpu.HBM)
VMEM = pl.BlockSpec(memory_space=pltpu.VMEM)
SMEM = pl.BlockSpec(memory_space=pltpu.SMEM)


def params():
    return pltpu.CompilerParams(vmem_limit_bytes=VMEM_LIMIT)


def cost(flops, nbytes):
    return pl.CostEstimate(flops=flops, bytes_accessed=nbytes, transcendentals=0)


def split_kernel(heads, first_ref, second_ref, out_ref, sems):
    copies = []
    for which, ref in enumerate((first_ref, second_ref)):
        for head in range(heads):
            copies.append(
                pltpu.make_async_copy(
                    ref.at[:, pl.ds(head * HEAD_DIM, HEAD_DIM)],
                    out_ref.at[head, which],
                    sems.at[which * heads + head],
                )
            )
    for copy in copies:
        copy.start()
    for copy in copies:
        copy.wait()


def split_heads(first, second):
    rows, features = first.shape
    heads = features // HEAD_DIM
    return pl.pallas_call(
        functools.partial(split_kernel, heads),
        out_shape=jax.ShapeDtypeStruct((heads, 2, rows, HEAD_DIM), first.dtype),
        in_specs=[HBM, HBM],
        out_specs=ANY,
        scratch_shapes=[pltpu.SemaphoreType.DMA((2 * heads,))],
        compiler_params=params(),
        cost_estimate=cost(0, 4 * first.size * 2),
        name="split_heads",
    )(first, second)


def join_kernel(heads, in_ref, first_ref, second_ref, sems):
    copies = []
    for which, ref in enumerate((first_ref, second_ref)):
        for head in range(heads):
            copies.append(
                pltpu.make_async_copy(
                    in_ref.at[head, which],
                    ref.at[:, pl.ds(head * HEAD_DIM, HEAD_DIM)],
                    sems.at[which * heads + head],
                )
            )
    for copy in copies:
        copy.start()
    for copy in copies:
        copy.wait()


def join_heads(both):
    heads, _, rows, depth = both.shape
    shape = jax.ShapeDtypeStruct((rows, heads * depth), both.dtype)
    return pl.pallas_call(
        functools.partial(join_kernel, heads),
        out_shape=(shape, shape),
        in_specs=[ANY],
        out_specs=(ANY, ANY),
        scratch_shapes=[pltpu.SemaphoreType.DMA((2 * heads,))],
        compiler_params=params(),
        cost_estimate=cost(0, 2 * both.size * 2),
        name="join_heads",
    )(both)


def start_all(copies):
    for copy in copies:
        copy.start()


def wait_all(copies):
    for copy in copies:
        copy.wait()


def pick_kernel(slots, index_ref, in_ref, out_ref, sems):
    copies = [
        pltpu.make_async_copy(in_ref.at[index_ref[slot]], out_ref.at[slot], sems.at[slot])
        for slot in range(slots)
    ]
    start_all(copies)
    wait_all(copies)


def pick_blocks(index, blocks):
    slots = index.shape[0]
    return pl.pallas_call(
        functools.partial(pick_kernel, slots),
        out_shape=jax.ShapeDtypeStruct((slots,) + blocks.shape[1:], blocks.dtype),
        in_specs=[SMEM, VMEM],
        out_specs=ANY,
        scratch_shapes=[pltpu.SemaphoreType.DMA((slots,))],
        compiler_params=params(),
        cost_estimate=cost(0, 2 * slots * blocks[0].size * 2),
        name="pick_blocks",
    )(index, blocks)


def pick_third_kernel(lanes, index_ref, in_ref, *refs):
    outs, sems = refs[:lanes], refs[lanes]
    copies = [
        pltpu.make_async_copy(
            in_ref.at[index_ref[2 * step + half]], outs[step].at[half], sems.at[2 * step + half]
        )
        for step in range(lanes)
        for half in range(2)
    ]
    start_all(copies)
    wait_all(copies)


def pick_third(index, blocks):
    lanes = index.shape[0] // 2
    shape = jax.ShapeDtypeStruct((2,) + blocks.shape[1:], blocks.dtype)
    return pl.pallas_call(
        functools.partial(pick_third_kernel, lanes),
        out_shape=(shape,) * lanes,
        in_specs=[SMEM, VMEM],
        out_specs=(ANY,) * lanes,
        scratch_shapes=[pltpu.SemaphoreType.DMA((2 * lanes,))],
        compiler_params=params(),
        cost_estimate=cost(0, 4 * lanes * blocks[0].size * 2),
        name="pick_third",
    )(index, blocks)


def pick_cross_kernel(lanes, step_ref, *refs):
    ins, out_ref, sems = refs[:lanes], refs[lanes], refs[lanes + 1]
    for j in range(2):
        for step in range(lanes):

            @pl.when(step_ref[j] == step)
            def _():
                pltpu.make_async_copy(ins[step].at[1], out_ref.at[j], sems.at[j]).start()

    for j in range(2):

        @pl.when(step_ref[j] >= 0)
        def _():
            pltpu.make_async_copy(ins[0].at[1], out_ref.at[j], sems.at[j]).wait()


def pick_cross(steps, thirds):
    lanes = len(thirds)
    return pl.pallas_call(
        functools.partial(pick_cross_kernel, lanes),
        out_shape=jax.ShapeDtypeStruct(thirds[0].shape, thirds[0].dtype),
        in_specs=[SMEM] + [ANY] * lanes,
        out_specs=ANY,
        scratch_shapes=[pltpu.SemaphoreType.DMA((2,))],
        compiler_params=params(),
        cost_estimate=cost(0, 4 * thirds[0].size),
        name="pick_cross",
    )(steps, *thirds)


def pick_back_kernel(lanes, near_ref, cross_ref, own_in, cross_in, *refs):
    outs, sems = refs[:lanes], refs[lanes]
    plan = ((near_ref, own_in, 0), (cross_ref, cross_in, 1))
    for step_ref, ref, half in plan:
        for j in range(2):
            for step in range(lanes):

                @pl.when(step_ref[j] == step)
                def _():
                    pltpu.make_async_copy(
                        ref.at[j], outs[step].at[half], sems.at[2 * half + j]
                    ).start()

    for step_ref, ref, half in plan:
        for j in range(2):

            @pl.when(step_ref[j] >= 0)
            def _():
                pltpu.make_async_copy(ref.at[j], outs[0].at[half], sems.at[2 * half + j]).wait()


def pick_back(near_steps, cross_steps, own, crossed, lanes):
    shape = jax.ShapeDtypeStruct(own.shape, own.dtype)
    return pl.pallas_call(
        functools.partial(pick_back_kernel, lanes),
        out_shape=(shape,) * lanes,
        in_specs=[SMEM, SMEM, ANY, ANY],
        out_specs=(ANY,) * lanes,
        scratch_shapes=[pltpu.SemaphoreType.DMA((4,))],
        compiler_params=params(),
        cost_estimate=cost(0, 8 * own.size),
        name="pick_back",
    )(near_steps, cross_steps, own, crossed)


def attend_kernel(
    blocks, lanes, slot_ref, third_ref, near_ref, qg_ref, kv_ref, edge_ref, main_ref, cross_ref, *refs
):
    thirds = refs[:lanes]
    out_ref, main_out, third_out, edge_out, sum_ref = refs[lanes : lanes + 5]
    far, far_out, sems, out_sems, third_sems = refs[lanes + 5 :]
    requests = 2 * blocks
    scale = HEAD_DIM ** (-0.5)
    f32, bf16 = jnp.float32, jnp.bfloat16

    def dot(a, b, dims):
        return lax.dot_general(a, b, (dims, ((), ())), preferred_element_type=f32)

    def arrive(r):
        return pltpu.make_async_copy(main_ref.at[0], far.at[r], sems.at[r])

    def leave(r, slot):
        return pltpu.make_async_copy(far_out.at[r], main_out.at[slot], out_sems.at[r])

    def load(r, _):
        @pl.when(slot_ref[r] >= 0)
        def _():
            pltpu.make_async_copy(main_ref.at[slot_ref[r]], far.at[r], sems.at[r]).start()

    lax.fori_loop(0, requests, load, None)
    for j in range(2):
        r = third_ref[j]
        for step in range(1, lanes):

            @pl.when(near_ref[j] == step)
            def _():
                pltpu.make_async_copy(thirds[step].at[0], far.at[r], sems.at[r]).start()

        @pl.when(near_ref[j] < 0)
        def _():
            pltpu.make_async_copy(cross_ref.at[j], far.at[r], sems.at[r]).start()

    def one(n, first):
        q, g = qg_ref[n, 0], qg_ref[n, 1]
        r2, r3 = 2 * n, 2 * n + 1
        if first:
            prev_k, prev_v = edge_ref[0], edge_ref[1]
        else:
            prev_k, prev_v = kv_ref[n - 1, 0], kv_ref[n - 1, 1]
        arrive(r2).wait()
        arrive(r3).wait()
        k = jnp.concatenate([kv_ref[n, 0], prev_k, far[r2, 0], far[r3, 0]], axis=0)
        v = jnp.concatenate([kv_ref[n, 1], prev_v, far[r2, 1], far[r3, 1]], axis=0)
        s = dot(k, q, ((1,), (1,))) * scale
        dp = dot(v, g, ((1,), (1,)))
        w = jnp.exp(s - jnp.max(s, axis=0, keepdims=True))
        p = w * (1.0 / jnp.sum(w, axis=0, keepdims=True))
        p_low = p.astype(bf16)
        delta = jnp.sum(p_low.astype(f32) * dp, axis=0, keepdims=True)
        ds = (p * (dp - delta) * scale).astype(bf16)
        out_ref[n, 0] = dot(p_low, v, ((0,), (0,))).astype(bf16)
        out_ref[n, 1] = dot(ds, k, ((0,), (0,))).astype(bf16)
        dk = dot(ds, q, ((1,), (0,)))
        dv = dot(p_low, g, ((1,), (0,)))
        for which, d in enumerate((dk, dv)):
            sum_ref[n, which] = d[:BLOCK]
            if first:
                edge_out[which] = d[BLOCK : 2 * BLOCK].astype(bf16)
            else:
                sum_ref[n - 1, which] += d[BLOCK : 2 * BLOCK]
            far_out[r2, which] = d[2 * BLOCK : 3 * BLOCK].astype(bf16)
            far_out[r3, which] = d[3 * BLOCK :].astype(bf16)
        for r in (r2, r3):

            @pl.when(slot_ref[r] >= 0)
            def _():
                leave(r, slot_ref[r]).start()

    one(0, True)
    lax.fori_loop(1, blocks, lambda n, _: one(n, False), None)
    lasts = [
        pltpu.make_async_copy(far_out.at[third_ref[j]], third_out.at[j], third_sems.at[j])
        for j in range(2)
    ]
    start_all(lasts)

    def finish(r, _):
        @pl.when(slot_ref[r] >= 0)
        def _():
            leave(r, 0).wait()

    lax.fori_loop(0, requests, finish, None)
    wait_all(lasts)


def attend(slot, third, near, qg, kv, edge, main, cross, thirds):
    blocks = qg.shape[0]
    lanes = len(thirds)
    bf16 = jnp.bfloat16
    far = pltpu.VMEM((2 * blocks,) + kv.shape[1:], bf16)
    return pl.pallas_call(
        functools.partial(attend_kernel, blocks, lanes),
        out_shape=(
            jax.ShapeDtypeStruct(qg.shape, bf16),
            jax.ShapeDtypeStruct(main.shape, bf16),
            jax.ShapeDtypeStruct(cross.shape, bf16),
            jax.ShapeDtypeStruct(edge.shape, bf16),
            jax.ShapeDtypeStruct(kv.shape, jnp.float32),
        ),
        in_specs=[SMEM, SMEM, SMEM, VMEM, VMEM, VMEM] + [ANY] * (2 + lanes),
        out_specs=(VMEM, ANY, ANY, VMEM, VMEM),
        scratch_shapes=[
            far,
            far,
            pltpu.SemaphoreType.DMA((2 * blocks,)),
            pltpu.SemaphoreType.DMA((2 * blocks,)),
            pltpu.SemaphoreType.DMA((2,)),
        ],
        compiler_params=params(),
        cost_estimate=cost(
            5 * 2 * blocks * 4 * BLOCK * BLOCK * HEAD_DIM, 2 * (2 * qg.size + 3 * kv.size + 2 * main.size)
        ),
        name="attend",
    )(slot, third, near, qg, kv, edge, main, cross, *thirds)


def land_kernel(
    slots, blocks, lanes, rank_ref, index_ref, third_ref, sum_ref, back_ref, home_ref, *refs
):
    thirds, out_ref = refs[:lanes], refs[lanes]
    total, late, sems = refs[lanes + 1 :]
    f32 = jnp.float32

    def arrive(at):
        step, half = divmod(at, 2)
        return pltpu.make_async_copy(thirds[step].at[half], late.at[at], sems.at[at])

    for at in range(1, 2 * lanes):

        @pl.when(third_ref[at] >= 0)
        def _():
            arrive(at).start()

    total[...] = sum_ref[...]
    total[blocks - 1] += back_ref[...].astype(f32)

    def one(slot, _):
        @pl.when(slot // 2 != rank_ref[0])
        def _():
            total[index_ref[slot]] += home_ref[slot].astype(f32)

    lax.fori_loop(0, slots, one, None)
    for at in range(1, 2 * lanes):

        @pl.when(third_ref[at] >= 0)
        def _():
            arrive(at).wait()
            total[third_ref[at]] += late[at].astype(f32)

    out_ref[...] = total[...].astype(out_ref.dtype)


def land(rank, index, third_index, sums, back, home, thirds):
    slots = index.shape[0]
    blocks = sums.shape[0]
    lanes = len(thirds)
    return pl.pallas_call(
        functools.partial(land_kernel, slots, blocks, lanes),
        out_shape=jax.ShapeDtypeStruct(sums.shape, jnp.bfloat16),
        in_specs=[SMEM, SMEM, SMEM, VMEM, VMEM, VMEM] + [ANY] * lanes,
        out_specs=VMEM,
        scratch_shapes=[
            pltpu.VMEM(sums.shape, jnp.float32),
            pltpu.VMEM((2 * lanes,) + home.shape[1:], home.dtype),
            pltpu.SemaphoreType.DMA((2 * lanes,)),
        ],
        compiler_params=params(),
        cost_estimate=cost(sums.size * 4, 6 * sums.size + 2 * home.size),
        name="land",
    )(rank, index, third_index, sums, back, home, *thirds)


def plan(key_lists, blocks, ctx_count, lanes):
    i32 = jnp.int32
    me = lax.axis_index("ctx")
    half, lane = me // lanes, me % lanes
    requests = 2 * blocks
    far_all = key_lists[:, 2:].reshape(ctx_count, requests)
    source, inside = far_all // blocks, far_all % blocks
    earlier = (jnp.arange(requests)[None, :] < jnp.arange(requests)[:, None])[None]
    rank = jnp.sum(((source[:, None, :] == source[:, :, None]) & earlier).astype(i32), axis=2)
    is_third = rank == 2
    order = jnp.sum((is_third[:, None, :] & earlier).astype(i32), axis=2)

    pair = jnp.arange(2, dtype=i32)[None, :, None]
    wanted = (source[:, None, :] == me) & (rank[:, None, :] == pair)
    send_main = jnp.sum(jnp.where(wanted, inside[:, None, :], 0), axis=2).reshape(-1)

    from_me = is_third & (source == me)
    third_of = jnp.sum(jnp.where(from_me, inside + 1, 0), axis=1) - 1
    step = jnp.arange(lanes, dtype=i32)[:, None]
    side = jnp.arange(2, dtype=i32)[None, :]
    asker = jnp.where(side == 0, half, 1 - half) * lanes + (lane + step) % lanes
    hit = asker[:, :, None] == jnp.arange(ctx_count, dtype=i32)[None, None, :]
    third_index = jnp.sum(jnp.where(hit, third_of[None, None, :], 0), axis=2).reshape(-1)

    def row(of, array):
        at = jnp.arange(ctx_count, dtype=i32)[:, None] == of
        return jnp.sum(jnp.where(at, array, 0), axis=0)

    slot_of = jnp.where(is_third, -1, source * 2 + rank)
    my_slot = row(me, slot_of)
    is_jth = (is_third[:, None, :] & (order[:, None, :] == pair)).astype(i32)
    third_source = jnp.sum(is_jth * source[:, None, :], axis=2)
    third_request = jnp.sum(is_jth * jnp.arange(requests, dtype=i32), axis=2)

    def steps(of):
        slab = row(of, third_source)
        return jnp.where(slab // lanes == half, (lane - slab % lanes + lanes) % lanes, -1)

    partner = (me + lanes) % ctx_count
    return (
        send_main,
        third_index,
        my_slot,
        row(me, third_request),
        steps(me),
        steps(partner),
    )


def body(queries, keys, values, out_grad, key_lists):
    ctx_count = lax.axis_size("ctx")
    blocks = lax.axis_size("head")
    lanes = ctx_count // 2
    send_main, third_index, my_slot, my_third, near_steps, cross_steps = plan(
        key_lists, blocks, ctx_count, lanes
    )

    def head_exchange(array):
        return lax.all_to_all(array, "head", split_axis=0, concat_axis=0, tiled=True)

    def ctx_exchange(array):
        return lax.all_to_all(array, "ctx", split_axis=0, concat_axis=0, tiled=True)

    def move(array, target):
        return lax.ppermute(array, "ctx", [(i, target(i)) for i in range(ctx_count)])

    def across(array):
        return move(array, lambda i: (i + lanes) % ctx_count)

    def along(arrays, sign):
        def target(step):
            return lambda i: i // lanes * lanes + (i + sign * step) % lanes

        return [arrays[0]] + [move(arrays[s], target(s)) for s in range(1, lanes)]

    kv = head_exchange(split_heads(keys, values))
    qg = head_exchange(split_heads(queries, out_grad))
    thirds = along(pick_third(jnp.maximum(third_index, 0), kv), 1)
    edge = move(kv[blocks - 1], lambda i: (i + 1) % ctx_count)
    to_send, qg, edge, thirds = lax.optimization_barrier(
        (pick_blocks(send_main, kv), qg, edge, thirds)
    )
    main = ctx_exchange(to_send)
    cross = across(pick_cross(cross_steps, thirds))
    out, main_grad, third_grad, edge_grad, sums = attend(
        my_slot, my_third, near_steps, qg, kv, edge, main, cross, thirds
    )
    cross_grad = across(third_grad)
    home = ctx_exchange(main_grad)
    back = move(edge_grad, lambda i: (i - 1) % ctx_count)
    late = along(pick_back(near_steps, cross_steps, third_grad, cross_grad, lanes), -1)
    out, home, back, late = lax.optimization_barrier((out, home, back, late))
    rank = lax.axis_index("ctx").reshape(1)
    attended, query_grad = join_heads(head_exchange(out))
    key_grad, value_grad = join_heads(
        head_exchange(land(rank, send_main, third_index, sums, back, home, late))
    )
    return attended, query_grad, key_grad, value_grad


def solution(mesh):
    tokens = P(("ctx", "head"), None)
    return jax.shard_map(
        body,
        mesh=mesh,
        in_specs=(tokens, tokens, tokens, tokens, P()),
        out_specs=(tokens, tokens, tokens, tokens),
        check_vma=False,
    )
```

```python
import functools

import jax
import jax.numpy as jnp
from jax import lax
from jax.experimental import pallas as pl
from jax.experimental.pallas import tpu as pltpu
from jax.sharding import PartitionSpec as P

HEAD_DIM = 128
BLOCK = 128
VMEM_LIMIT = 48 * 1024 * 1024
ANY = pl.BlockSpec(memory_space=pl.ANY)
HBM = pl.BlockSpec(memory_space=pltpu.HBM)
VMEM = pl.BlockSpec(memory_space=pltpu.VMEM)
SMEM = pl.BlockSpec(memory_space=pltpu.SMEM)


def params():
    return pltpu.CompilerParams(vmem_limit_bytes=VMEM_LIMIT)


def cost(flops, nbytes):
    return pl.CostEstimate(flops=flops, bytes_accessed=nbytes, transcendentals=0)


def split_kernel(heads, first_ref, second_ref, out_ref, sems):
    copies = []
    for which, ref in enumerate((first_ref, second_ref)):
        for head in range(heads):
            copies.append(
                pltpu.make_async_copy(
                    ref.at[:, pl.ds(head * HEAD_DIM, HEAD_DIM)],
                    out_ref.at[head, which],
                    sems.at[which * heads + head],
                )
            )
    for copy in copies:
        copy.start()
    for copy in copies:
        copy.wait()


def split_heads(first, second):
    rows, features = first.shape
    heads = features // HEAD_DIM
    return pl.pallas_call(
        functools.partial(split_kernel, heads),
        out_shape=jax.ShapeDtypeStruct((heads, 2, rows, HEAD_DIM), first.dtype),
        in_specs=[HBM, HBM],
        out_specs=ANY,
        scratch_shapes=[pltpu.SemaphoreType.DMA((2 * heads,))],
        compiler_params=params(),
        cost_estimate=cost(0, 4 * first.size * 2),
        name="split_heads",
    )(first, second)


def join_kernel(heads, in_ref, first_ref, second_ref, sems):
    copies = []
    for which, ref in enumerate((first_ref, second_ref)):
        for head in range(heads):
            copies.append(
                pltpu.make_async_copy(
                    in_ref.at[head, which],
                    ref.at[:, pl.ds(head * HEAD_DIM, HEAD_DIM)],
                    sems.at[which * heads + head],
                )
            )
    for copy in copies:
        copy.start()
    for copy in copies:
        copy.wait()


def join_heads(both):
    heads, _, rows, depth = both.shape
    shape = jax.ShapeDtypeStruct((rows, heads * depth), both.dtype)
    return pl.pallas_call(
        functools.partial(join_kernel, heads),
        out_shape=(shape, shape),
        in_specs=[ANY],
        out_specs=(ANY, ANY),
        scratch_shapes=[pltpu.SemaphoreType.DMA((2 * heads,))],
        compiler_params=params(),
        cost_estimate=cost(0, 2 * both.size * 2),
        name="join_heads",
    )(both)


def start_all(copies):
    for copy in copies:
        copy.start()


def wait_all(copies):
    for copy in copies:
        copy.wait()


def pick_kernel(slots, index_ref, in_ref, out_ref, sems):
    copies = [
        pltpu.make_async_copy(in_ref.at[index_ref[slot]], out_ref.at[slot], sems.at[slot])
        for slot in range(slots)
    ]
    start_all(copies)
    wait_all(copies)


def pick_blocks(index, blocks):
    slots = index.shape[0]
    return pl.pallas_call(
        functools.partial(pick_kernel, slots),
        out_shape=jax.ShapeDtypeStruct((slots,) + blocks.shape[1:], blocks.dtype),
        in_specs=[SMEM, VMEM],
        out_specs=ANY,
        scratch_shapes=[pltpu.SemaphoreType.DMA((slots,))],
        compiler_params=params(),
        cost_estimate=cost(0, 2 * slots * blocks[0].size * 2),
        name="pick_blocks",
    )(index, blocks)


def pick_third_kernel(lanes, index_ref, in_ref, *refs):
    outs, sems = refs[:lanes], refs[lanes]
    copies = [
        pltpu.make_async_copy(
            in_ref.at[index_ref[2 * step + half]], outs[step].at[half], sems.at[2 * step + half]
        )
        for step in range(lanes)
        for half in range(2)
    ]
    start_all(copies)
    wait_all(copies)


def pick_third(index, blocks):
    lanes = index.shape[0] // 2
    shape = jax.ShapeDtypeStruct((2,) + blocks.shape[1:], blocks.dtype)
    return pl.pallas_call(
        functools.partial(pick_third_kernel, lanes),
        out_shape=(shape,) * lanes,
        in_specs=[SMEM, VMEM],
        out_specs=(ANY,) * lanes,
        scratch_shapes=[pltpu.SemaphoreType.DMA((2 * lanes,))],
        compiler_params=params(),
        cost_estimate=cost(0, 4 * lanes * blocks[0].size * 2),
        name="pick_third",
    )(index, blocks)


def pick_cross_kernel(lanes, step_ref, *refs):
    ins, out_ref, sems = refs[:lanes], refs[lanes], refs[lanes + 1]
    for j in range(2):
        for step in range(lanes):

            @pl.when(step_ref[j] == step)
            def _():
                pltpu.make_async_copy(ins[step].at[1], out_ref.at[j], sems.at[j]).start()

    for j in range(2):

        @pl.when(step_ref[j] >= 0)
        def _():
            pltpu.make_async_copy(ins[0].at[1], out_ref.at[j], sems.at[j]).wait()


def pick_cross(steps, thirds):
    lanes = len(thirds)
    return pl.pallas_call(
        functools.partial(pick_cross_kernel, lanes),
        out_shape=jax.ShapeDtypeStruct(thirds[0].shape, thirds[0].dtype),
        in_specs=[SMEM] + [ANY] * lanes,
        out_specs=ANY,
        scratch_shapes=[pltpu.SemaphoreType.DMA((2,))],
        compiler_params=params(),
        cost_estimate=cost(0, 4 * thirds[0].size),
        name="pick_cross",
    )(steps, *thirds)


def pick_back_kernel(lanes, near_ref, cross_ref, own_in, cross_in, *refs):
    outs, sems = refs[:lanes], refs[lanes]
    plan = ((near_ref, own_in, 0), (cross_ref, cross_in, 1))
    for step_ref, ref, half in plan:
        for j in range(2):
            for step in range(lanes):

                @pl.when(step_ref[j] == step)
                def _():
                    pltpu.make_async_copy(
                        ref.at[j], outs[step].at[half], sems.at[2 * half + j]
                    ).start()

    for step_ref, ref, half in plan:
        for j in range(2):

            @pl.when(step_ref[j] >= 0)
            def _():
                pltpu.make_async_copy(ref.at[j], outs[0].at[half], sems.at[2 * half + j]).wait()


def pick_back(near_steps, cross_steps, own, crossed, lanes):
    shape = jax.ShapeDtypeStruct(own.shape, own.dtype)
    return pl.pallas_call(
        functools.partial(pick_back_kernel, lanes),
        out_shape=(shape,) * lanes,
        in_specs=[SMEM, SMEM, ANY, ANY],
        out_specs=(ANY,) * lanes,
        scratch_shapes=[pltpu.SemaphoreType.DMA((4,))],
        compiler_params=params(),
        cost_estimate=cost(0, 8 * own.size),
        name="pick_back",
    )(near_steps, cross_steps, own, crossed)


def attend_kernel(
    blocks, lanes, slot_ref, third_ref, near_ref, qg_ref, kv_ref, edge_ref, main_ref, cross_ref, *refs
):
    thirds = refs[:lanes]
    out, main_out, third_out, edge_out, sum_ref = refs[lanes : lanes + 5]
    far, far_out, out_ref, sems, out_sems, third_sems, done_sems = refs[lanes + 5 :]
    requests = 2 * blocks
    scale = HEAD_DIM ** (-0.5)
    f32, bf16 = jnp.float32, jnp.bfloat16

    def dot(a, b, dims):
        return lax.dot_general(a, b, (dims, ((), ())), preferred_element_type=f32)

    def arrive(r):
        return pltpu.make_async_copy(main_ref.at[0], far.at[r], sems.at[r])

    def leave(r, slot):
        return pltpu.make_async_copy(far_out.at[r], main_out.at[slot], out_sems.at[r])

    def finished(n):
        return pltpu.make_async_copy(out_ref.at[n], out.at[n], done_sems.at[n])

    def load(r, _):
        @pl.when(slot_ref[r] >= 0)
        def _():
            pltpu.make_async_copy(main_ref.at[slot_ref[r]], far.at[r], sems.at[r]).start()

    lax.fori_loop(0, requests, load, None)
    for j in range(2):
        r = third_ref[j]
        for step in range(1, lanes):

            @pl.when(near_ref[j] == step)
            def _():
                pltpu.make_async_copy(thirds[step].at[0], far.at[r], sems.at[r]).start()

        @pl.when(near_ref[j] < 0)
        def _():
            pltpu.make_async_copy(cross_ref.at[j], far.at[r], sems.at[r]).start()

    def one(n, first):
        q, g = qg_ref[n, 0], qg_ref[n, 1]
        r2, r3 = 2 * n, 2 * n + 1
        if first:
            prev_k, prev_v = edge_ref[0], edge_ref[1]
        else:
            prev_k, prev_v = kv_ref[n - 1, 0], kv_ref[n - 1, 1]
        arrive(r2).wait()
        arrive(r3).wait()
        k = jnp.concatenate([kv_ref[n, 0], prev_k, far[r2, 0], far[r3, 0]], axis=0)
        v = jnp.concatenate([kv_ref[n, 1], prev_v, far[r2, 1], far[r3, 1]], axis=0)
        s = dot(k, q, ((1,), (1,))) * scale
        dp = dot(v, g, ((1,), (1,)))
        w = jnp.exp(s - jnp.max(s, axis=0, keepdims=True))
        p = w * (1.0 / jnp.sum(w, axis=0, keepdims=True))
        p_low = p.astype(bf16)
        delta = jnp.sum(p_low.astype(f32) * dp, axis=0, keepdims=True)
        ds = (p * (dp - delta) * scale).astype(bf16)
        out_ref[n, 0] = dot(p_low, v, ((0,), (0,))).astype(bf16)
        out_ref[n, 1] = dot(ds, k, ((0,), (0,))).astype(bf16)
        dk = dot(ds, q, ((1,), (0,)))
        dv = dot(p_low, g, ((1,), (0,)))
        for which, d in enumerate((dk, dv)):
            sum_ref[n, which] = d[:BLOCK]
            if first:
                edge_out[which] = d[BLOCK : 2 * BLOCK].astype(bf16)
            else:
                sum_ref[n - 1, which] += d[BLOCK : 2 * BLOCK]
            far_out[r2, which] = d[2 * BLOCK : 3 * BLOCK].astype(bf16)
            far_out[r3, which] = d[3 * BLOCK :].astype(bf16)
        finished(n).start()
        for r in (r2, r3):

            @pl.when(slot_ref[r] >= 0)
            def _():
                leave(r, slot_ref[r]).start()

    one(0, True)
    lax.fori_loop(1, blocks, lambda n, _: one(n, False), None)
    lasts = [
        pltpu.make_async_copy(far_out.at[third_ref[j]], third_out.at[j], third_sems.at[j])
        for j in range(2)
    ]
    start_all(lasts)

    def finish(r, _):
        @pl.when(slot_ref[r] >= 0)
        def _():
            leave(r, 0).wait()

    lax.fori_loop(0, requests, finish, None)
    lax.fori_loop(0, blocks, lambda n, _: finished(n).wait(), None)
    wait_all(lasts)


def attend(slot, third, near, qg, kv, edge, main, cross, thirds):
    blocks = qg.shape[0]
    lanes = len(thirds)
    bf16 = jnp.bfloat16
    far = pltpu.VMEM((2 * blocks,) + kv.shape[1:], bf16)
    return pl.pallas_call(
        functools.partial(attend_kernel, blocks, lanes),
        out_shape=(
            jax.ShapeDtypeStruct(qg.shape, bf16),
            jax.ShapeDtypeStruct(main.shape, bf16),
            jax.ShapeDtypeStruct(cross.shape, bf16),
            jax.ShapeDtypeStruct(edge.shape, bf16),
            jax.ShapeDtypeStruct(kv.shape, jnp.float32),
        ),
        in_specs=[SMEM, SMEM, SMEM, VMEM, VMEM, VMEM] + [ANY] * (2 + lanes),
        out_specs=(ANY, ANY, ANY, VMEM, VMEM),
        scratch_shapes=[
            far,
            far,
            pltpu.VMEM(qg.shape, bf16),
            pltpu.SemaphoreType.DMA((2 * blocks,)),
            pltpu.SemaphoreType.DMA((2 * blocks,)),
            pltpu.SemaphoreType.DMA((2,)),
            pltpu.SemaphoreType.DMA((blocks,)),
        ],
        compiler_params=params(),
        cost_estimate=cost(
            5 * 2 * blocks * 4 * BLOCK * BLOCK * HEAD_DIM, 2 * (2 * qg.size + 3 * kv.size + 2 * main.size)
        ),
        name="attend",
    )(slot, third, near, qg, kv, edge, main, cross, *thirds)


def land_thirds_kernel(blocks, lanes, third_ref, sum_ref, back_ref, *refs):
    thirds, total = refs[:lanes], refs[lanes]
    late, sems = refs[lanes + 1 :]
    f32 = jnp.float32

    def arrive(at):
        step, half = divmod(at, 2)
        return pltpu.make_async_copy(thirds[step].at[half], late.at[at], sems.at[at])

    for at in range(1, 2 * lanes):

        @pl.when(third_ref[at] >= 0)
        def _():
            arrive(at).start()

    total[...] = sum_ref[...]
    total[blocks - 1] += back_ref[...].astype(f32)
    for at in range(1, 2 * lanes):

        @pl.when(third_ref[at] >= 0)
        def _():
            arrive(at).wait()
            total[third_ref[at]] += late[at].astype(f32)


def land_thirds(third_index, sums, back, thirds):
    blocks = sums.shape[0]
    lanes = len(thirds)
    return pl.pallas_call(
        functools.partial(land_thirds_kernel, blocks, lanes),
        out_shape=jax.ShapeDtypeStruct(sums.shape, jnp.float32),
        in_specs=[SMEM, VMEM, VMEM] + [ANY] * lanes,
        out_specs=VMEM,
        scratch_shapes=[
            pltpu.VMEM((2 * lanes,) + back.shape, back.dtype),
            pltpu.SemaphoreType.DMA((2 * lanes,)),
        ],
        compiler_params=params(),
        cost_estimate=cost(sums.size * 2, 8 * sums.size),
        name="land_thirds",
    )(third_index, sums, back, *thirds)


def land_kernel(
    slots, blocks, rank_ref, index_ref, sums, home, out, total, late, low, sum_sems, home_sems, out_sems
):
    def read(n):
        return pltpu.make_async_copy(sums.at[n], total.at[n], sum_sems.at[n])

    def arrive(slot):
        return pltpu.make_async_copy(home.at[slot], late.at[slot], home_sems.at[slot])

    def write(n):
        return pltpu.make_async_copy(low.at[n], out.at[n], out_sems.at[n])

    start_all([read(n) for n in range(blocks)])
    start_all([arrive(slot) for slot in range(slots)])
    wait_all([read(n) for n in range(blocks)])

    def one(slot, _):
        arrive(slot).wait()

        @pl.when(slot // 2 != rank_ref[0])
        def _():
            total[index_ref[slot]] += late[slot].astype(jnp.float32)

    lax.fori_loop(0, slots, one, None)

    def put(n, _):
        low[n] = total[n].astype(low.dtype)
        write(n).start()

    lax.fori_loop(0, blocks, put, None)
    wait_all([write(n) for n in range(blocks)])


def land(rank, index, sums, home):
    slots = index.shape[0]
    blocks = sums.shape[0]
    bf16 = jnp.bfloat16
    return pl.pallas_call(
        functools.partial(land_kernel, slots, blocks),
        out_shape=jax.ShapeDtypeStruct(sums.shape, bf16),
        in_specs=[SMEM, SMEM, ANY, ANY],
        out_specs=ANY,
        scratch_shapes=[
            pltpu.VMEM(sums.shape, jnp.float32),
            pltpu.VMEM(home.shape, bf16),
            pltpu.VMEM(sums.shape, bf16),
            pltpu.SemaphoreType.DMA((blocks,)),
            pltpu.SemaphoreType.DMA((slots,)),
            pltpu.SemaphoreType.DMA((blocks,)),
        ],
        compiler_params=params(),
        cost_estimate=cost(sums.size * 2, 6 * sums.size + 2 * home.size),
        name="land",
    )(rank, index, sums, home)


def plan(key_lists, blocks, ctx_count, lanes):
    i32 = jnp.int32
    me = lax.axis_index("ctx")
    half, lane = me // lanes, me % lanes
    requests = 2 * blocks
    far_all = key_lists[:, 2:].reshape(ctx_count, requests)
    source, inside = far_all // blocks, far_all % blocks
    earlier = (jnp.arange(requests)[None, :] < jnp.arange(requests)[:, None])[None]
    rank = jnp.sum(((source[:, None, :] == source[:, :, None]) & earlier).astype(i32), axis=2)
    is_third = rank == 2
    order = jnp.sum((is_third[:, None, :] & earlier).astype(i32), axis=2)

    pair = jnp.arange(2, dtype=i32)[None, :, None]
    wanted = (source[:, None, :] == me) & (rank[:, None, :] == pair)
    send_main = jnp.sum(jnp.where(wanted, inside[:, None, :], 0), axis=2).reshape(-1)

    from_me = is_third & (source == me)
    third_of = jnp.sum(jnp.where(from_me, inside + 1, 0), axis=1) - 1
    step = jnp.arange(lanes, dtype=i32)[:, None]
    side = jnp.arange(2, dtype=i32)[None, :]
    asker = jnp.where(side == 0, half, 1 - half) * lanes + (lane + step) % lanes
    hit = asker[:, :, None] == jnp.arange(ctx_count, dtype=i32)[None, None, :]
    third_index = jnp.sum(jnp.where(hit, third_of[None, None, :], 0), axis=2).reshape(-1)

    def row(of, array):
        at = jnp.arange(ctx_count, dtype=i32)[:, None] == of
        return jnp.sum(jnp.where(at, array, 0), axis=0)

    slot_of = jnp.where(is_third, -1, source * 2 + rank)
    my_slot = row(me, slot_of)
    is_jth = (is_third[:, None, :] & (order[:, None, :] == pair)).astype(i32)
    third_source = jnp.sum(is_jth * source[:, None, :], axis=2)
    third_request = jnp.sum(is_jth * jnp.arange(requests, dtype=i32), axis=2)

    def steps(of):
        slab = row(of, third_source)
        return jnp.where(slab // lanes == half, (lane - slab % lanes + lanes) % lanes, -1)

    partner = (me + lanes) % ctx_count
    return (
        send_main,
        third_index,
        my_slot,
        row(me, third_request),
        steps(me),
        steps(partner),
    )


def body(queries, keys, values, out_grad, key_lists):
    ctx_count = lax.axis_size("ctx")
    blocks = lax.axis_size("head")
    lanes = ctx_count // 2
    send_main, third_index, my_slot, my_third, near_steps, cross_steps = plan(
        key_lists, blocks, ctx_count, lanes
    )

    def head_exchange(array):
        return lax.all_to_all(array, "head", split_axis=0, concat_axis=0, tiled=True)

    def ctx_exchange(array):
        return lax.all_to_all(array, "ctx", split_axis=0, concat_axis=0, tiled=True)

    def move(array, target):
        return lax.ppermute(array, "ctx", [(i, target(i)) for i in range(ctx_count)])

    def across(array):
        return move(array, lambda i: (i + lanes) % ctx_count)

    def along(arrays, sign):
        def target(step):
            return lambda i: i // lanes * lanes + (i + sign * step) % lanes

        return [arrays[0]] + [move(arrays[s], target(s)) for s in range(1, lanes)]

    kv = head_exchange(split_heads(keys, values))
    qg = head_exchange(split_heads(queries, out_grad))
    thirds = along(pick_third(jnp.maximum(third_index, 0), kv), 1)
    edge = move(kv[blocks - 1], lambda i: (i + 1) % ctx_count)
    cross = across(pick_cross(cross_steps, thirds))
    to_send, qg, edge, cross = lax.optimization_barrier(
        (pick_blocks(send_main, kv), qg, edge, cross)
    )
    main = ctx_exchange(to_send)
    out, main_grad, third_grad, edge_grad, sums = attend(
        my_slot, my_third, near_steps, qg, kv, edge, main, cross, thirds
    )
    out = head_exchange(out)
    cross_grad = across(third_grad)
    back = move(edge_grad, lambda i: (i - 1) % ctx_count)
    main_grad, out, cross_grad, back = lax.optimization_barrier((main_grad, out, cross_grad, back))
    home = ctx_exchange(main_grad)
    late = along(pick_back(near_steps, cross_steps, third_grad, cross_grad, lanes), -1)
    sums = land_thirds(third_index, sums, back, late)
    rank = lax.axis_index("ctx").reshape(1)
    attended, query_grad = join_heads(out)
    key_grad, value_grad = join_heads(head_exchange(land(rank, send_main, sums, home)))
    return attended, query_grad, key_grad, value_grad


def solution(mesh):
    tokens = P(("ctx", "head"), None)
    return jax.shard_map(
        body,
        mesh=mesh,
        in_specs=(tokens, tokens, tokens, tokens, P()),
        out_specs=(tokens, tokens, tokens, tokens),
        check_vma=False,
    )
```

```python
import functools

import jax
import jax.numpy as jnp
from jax import lax
from jax.experimental import pallas as pl
from jax.experimental.pallas import tpu as pltpu
from jax.sharding import PartitionSpec as P

HEAD_DIM = 128
BLOCK = 128
VMEM_LIMIT = 48 * 1024 * 1024
VMEM_ALL = 60 * 1024 * 1024
ANY = pl.BlockSpec(memory_space=pl.ANY)
VMEM = pl.BlockSpec(memory_space=pltpu.VMEM)
SMEM = pl.BlockSpec(memory_space=pltpu.SMEM)


def params(limit=VMEM_LIMIT):
    return pltpu.CompilerParams(vmem_limit_bytes=limit)


def cost(flops, nbytes):
    return pl.CostEstimate(flops=flops, bytes_accessed=nbytes, transcendentals=0)


def head_copies(heads, packed, arrays, sems, pack):
    copies = []
    for which, array in enumerate(arrays):
        for head in range(heads):
            flat = array.at[:, pl.ds(head * HEAD_DIM, HEAD_DIM)]
            block = packed.at[head, which]
            ends = (flat, block) if pack else (block, flat)
            copies.append(pltpu.make_async_copy(*ends, sems.at[which * heads + head]))
    return copies


def split_kernel(heads, count, *refs):
    copies = head_copies(heads, refs[count], refs[:count], refs[count + 1], True)
    start_all(copies)
    wait_all(copies)


def split_heads(*arrays):
    rows, features = arrays[0].shape
    heads, count = features // HEAD_DIM, len(arrays)
    return pl.pallas_call(
        functools.partial(split_kernel, heads, count),
        out_shape=jax.ShapeDtypeStruct((heads, count, rows, HEAD_DIM), arrays[0].dtype),
        in_specs=[ANY] * count,
        out_specs=ANY,
        scratch_shapes=[pltpu.SemaphoreType.DMA((count * heads,))],
        compiler_params=params(VMEM_ALL),
        cost_estimate=cost(0, 4 * arrays[0].size * count),
        name="split_heads",
    )(*arrays)


def join_kernel(heads, count, packed, *refs):
    copies = head_copies(heads, packed, refs[:count], refs[count], False)
    start_all(copies)
    wait_all(copies)


def join_heads(packed):
    heads, count, rows, depth = packed.shape
    shape = jax.ShapeDtypeStruct((rows, heads * depth), packed.dtype)
    return pl.pallas_call(
        functools.partial(join_kernel, heads, count),
        out_shape=(shape,) * count,
        in_specs=[ANY],
        out_specs=(ANY,) * count,
        scratch_shapes=[pltpu.SemaphoreType.DMA((count * heads,))],
        compiler_params=params(VMEM_ALL),
        cost_estimate=cost(0, 4 * packed.size),
        name="join_heads",
    )(packed)


def start_all(copies):
    for copy in copies:
        copy.start()


def wait_all(copies):
    for copy in copies:
        copy.wait()


def pick_kernel(slots, index_ref, in_ref, out_ref, sems):
    copies = [
        pltpu.make_async_copy(
            in_ref.at[index_ref[slot], pl.ds(0, 2)], out_ref.at[slot], sems.at[slot]
        )
        for slot in range(slots)
    ]
    start_all(copies)
    wait_all(copies)


def pick_blocks(index, blocks):
    slots = index.shape[0]
    return pl.pallas_call(
        functools.partial(pick_kernel, slots),
        out_shape=pltpu.HBM((slots, 2) + blocks.shape[2:], blocks.dtype),
        in_specs=[SMEM, VMEM],
        out_specs=ANY,
        scratch_shapes=[pltpu.SemaphoreType.DMA((slots,))],
        compiler_params=params(),
        cost_estimate=cost(0, 2 * slots * blocks[0].size),
        name="pick_blocks",
    )(index, blocks)


def pick_third_kernel(lanes, index_ref, in_ref, *refs):
    outs, sems = refs[:lanes], refs[lanes]

    def copy(at):
        step, half = divmod(at, 2)
        return pltpu.make_async_copy(
            in_ref.at[jnp.maximum(index_ref[at], 0), pl.ds(0, 2)], outs[step].at[half], sems.at[at]
        )

    for at in range(2 * lanes):

        @pl.when(index_ref[at] >= 0)
        def _():
            copy(at).start()

    for at in range(2 * lanes):

        @pl.when(index_ref[at] >= 0)
        def _():
            copy(at).wait()


def pick_third(index, blocks):
    lanes = index.shape[0] // 2
    shape = jax.ShapeDtypeStruct((2, 2) + blocks.shape[2:], blocks.dtype)
    return pl.pallas_call(
        functools.partial(pick_third_kernel, lanes),
        out_shape=(shape,) * lanes,
        in_specs=[SMEM, VMEM],
        out_specs=(ANY,) * lanes,
        scratch_shapes=[pltpu.SemaphoreType.DMA((2 * lanes,))],
        compiler_params=params(),
        cost_estimate=cost(0, 4 * blocks[0].size),
        name="pick_third",
    )(index, blocks)


def pick_cross_kernel(lanes, step_ref, *refs):
    ins, out_ref, sems = refs[:lanes], refs[lanes], refs[lanes + 1]
    for j in range(2):
        for step in range(lanes):

            @pl.when(step_ref[j] == step)
            def _():
                pltpu.make_async_copy(ins[step].at[1], out_ref.at[j], sems.at[j]).start()

    for j in range(2):

        @pl.when(step_ref[j] >= 0)
        def _():
            pltpu.make_async_copy(ins[0].at[1], out_ref.at[j], sems.at[j]).wait()


def pick_cross(steps, thirds):
    lanes = len(thirds)
    return pl.pallas_call(
        functools.partial(pick_cross_kernel, lanes),
        out_shape=jax.ShapeDtypeStruct(thirds[0].shape, thirds[0].dtype),
        in_specs=[SMEM] + [ANY] * lanes,
        out_specs=ANY,
        scratch_shapes=[pltpu.SemaphoreType.DMA((2,))],
        compiler_params=params(),
        cost_estimate=cost(0, 4 * thirds[0].size),
        name="pick_cross",
    )(steps, *thirds)


def pick_back_kernel(lanes, near_ref, cross_ref, own_in, cross_in, *refs):
    outs, sems = refs[:lanes], refs[lanes]
    plan = ((near_ref, own_in, 0), (cross_ref, cross_in, 1))
    for step_ref, ref, half in plan:
        for j in range(2):
            for step in range(lanes):

                @pl.when(step_ref[j] == step)
                def _():
                    pltpu.make_async_copy(
                        ref.at[j], outs[step].at[half], sems.at[2 * half + j]
                    ).start()

    for step_ref, ref, half in plan:
        for j in range(2):

            @pl.when(step_ref[j] >= 0)
            def _():
                pltpu.make_async_copy(ref.at[j], outs[0].at[half], sems.at[2 * half + j]).wait()


def pick_back(near_steps, cross_steps, own, crossed, lanes):
    shape = jax.ShapeDtypeStruct(own.shape, own.dtype)
    return pl.pallas_call(
        functools.partial(pick_back_kernel, lanes),
        out_shape=(shape,) * lanes,
        in_specs=[SMEM, SMEM, ANY, ANY],
        out_specs=(ANY,) * lanes,
        scratch_shapes=[pltpu.SemaphoreType.DMA((4,))],
        compiler_params=params(),
        cost_estimate=cost(0, 8 * own.size),
        name="pick_back",
    )(near_steps, cross_steps, own, crossed)


def dot(a, b, dims):
    return lax.dot_general(a, b, (dims, ((), ())), preferred_element_type=jnp.float32)


def attention(q, g, k, v):
    scale = HEAD_DIM ** (-0.5)
    s = dot(k, q, ((1,), (1,))) * scale
    dp = dot(v, g, ((1,), (1,)))
    w = jnp.exp(s - jnp.max(s, axis=0, keepdims=True))
    p = w * (1.0 / jnp.sum(w, axis=0, keepdims=True))
    p_low = p.astype(jnp.bfloat16)
    delta = jnp.sum(p_low.astype(jnp.float32) * dp, axis=0, keepdims=True)
    return p_low, (p * (dp - delta) * scale).astype(jnp.bfloat16)


def load_thirds(near_ref, cross_ref, thirds, extra, sems):
    for j in range(2):
        for step in range(1, len(thirds)):

            @pl.when(near_ref[j] == step)
            def _():
                pltpu.make_async_copy(thirds[step].at[0], extra.at[j], sems.at[j]).start()

        @pl.when(near_ref[j] < 0)
        def _():
            pltpu.make_async_copy(cross_ref.at[j], extra.at[j], sems.at[j]).start()

    for j in range(2):
        pltpu.make_async_copy(cross_ref.at[j], extra.at[j], sems.at[j]).wait()


def far_block(r, which, slot_ref, third_ref, main_ref, extra):
    slot = slot_ref[r]
    j = (third_ref[1] == r).astype(jnp.int32)
    return jnp.where(slot >= 0, main_ref[jnp.maximum(slot, 0), which], extra[j, which])


def attend_thirds_kernel(lanes, slot_ref, third_ref, near_ref, x_ref, edge_ref, main_ref, cross_ref, *refs):
    thirds, out_ref = refs[:lanes], refs[lanes]
    extra, sems = refs[lanes + 1 :]
    load_thirds(near_ref, cross_ref, thirds, extra, sems)
    for j in range(2):
        r = third_ref[j]
        n = r // 2
        listed = []
        for which in range(2):
            edge = edge_ref[which]
            before = jnp.where(n == 0, edge, x_ref[jnp.maximum(n - 1, 0), which])
            other = far_block(n * 4 + 1 - r, which, slot_ref, third_ref, main_ref, extra)
            listed.append(jnp.concatenate([extra[j, which], x_ref[n, which], before, other], axis=0))
        q, g = x_ref[n, 2], x_ref[n, 3]
        p_low, ds = attention(q, g, *listed)
        out_ref[j, 0] = dot(ds[:BLOCK], q, ((1,), (0,))).astype(out_ref.dtype)
        out_ref[j, 1] = dot(p_low[:BLOCK], g, ((1,), (0,))).astype(out_ref.dtype)


def attend_thirds(slot, third, near, x, edge, main, cross, thirds):
    lanes = len(thirds)
    return pl.pallas_call(
        functools.partial(attend_thirds_kernel, lanes),
        out_shape=jax.ShapeDtypeStruct(cross.shape, cross.dtype),
        in_specs=[SMEM, SMEM, SMEM, VMEM, VMEM, VMEM] + [ANY] * (1 + lanes),
        out_specs=VMEM,
        scratch_shapes=[pltpu.VMEM(cross.shape, cross.dtype), pltpu.SemaphoreType.DMA((2,))],
        compiler_params=params(),
        cost_estimate=cost(5 * 2 * 2 * 4 * BLOCK * BLOCK * HEAD_DIM, 8 * cross.size),
        name="attend_thirds",
    )(slot, third, near, x, edge, main, cross, *thirds)


def attend_kernel(
    blocks, lanes, slot_ref, third_ref, near_ref, x_ref, edge_ref, main_ref, cross_ref, *refs
):
    thirds = refs[:lanes]
    final, main_out, edge_out, sums = refs[lanes : lanes + 4]
    extra, far_out, out_ref, sum_ref, edge_low = refs[lanes + 4 : lanes + 9]
    sems, far_sems, out_sems, sum_sems, edge_sem = refs[lanes + 9 :]
    bf16 = jnp.bfloat16

    def leave(r, slot):
        return pltpu.make_async_copy(far_out.at[r], main_out.at[slot], far_sems.at[r])

    def finished(n):
        return pltpu.make_async_copy(out_ref.at[n], final.at[n, pl.ds(0, 2)], out_sems.at[n])

    def summed(n):
        return pltpu.make_async_copy(sum_ref.at[n], sums.at[n], sum_sems.at[n])

    edge_done = pltpu.make_async_copy(edge_low, edge_out, edge_sem)
    load_thirds(near_ref, cross_ref, thirds, extra, sems)

    def one(n, first):
        q, g = x_ref[n, 2], x_ref[n, 3]
        r2, r3 = 2 * n, 2 * n + 1
        listed = []
        for which in range(2):
            before = edge_ref[which] if first else x_ref[n - 1, which]
            far = [far_block(r, which, slot_ref, third_ref, main_ref, extra) for r in (r2, r3)]
            listed.append(jnp.concatenate([x_ref[n, which], before] + far, axis=0))
        k, v = listed
        p_low, ds = attention(q, g, k, v)
        out_ref[n, 0] = dot(p_low, v, ((0,), (0,))).astype(bf16)
        out_ref[n, 1] = dot(ds, k, ((0,), (0,))).astype(bf16)
        dk = dot(ds, q, ((1,), (0,)))
        dv = dot(p_low, g, ((1,), (0,)))
        for which, d in enumerate((dk, dv)):
            sum_ref[n, which] = d[:BLOCK]
            if first:
                edge_low[which] = d[BLOCK : 2 * BLOCK].astype(bf16)
            else:
                sum_ref[n - 1, which] += d[BLOCK : 2 * BLOCK]
            far_out[r2, which] = d[2 * BLOCK : 3 * BLOCK].astype(bf16)
            far_out[r3, which] = d[3 * BLOCK :].astype(bf16)
        finished(n).start()
        if first:
            edge_done.start()
        else:
            summed(n - 1).start()
        for r in (r2, r3):

            @pl.when(slot_ref[r] >= 0)
            def _():
                leave(r, slot_ref[r]).start()

    one(0, True)
    lax.fori_loop(1, blocks, lambda n, _: one(n, False), None, unroll=3)
    summed(blocks - 1).start()

    def finish(r, _):
        @pl.when(slot_ref[r] >= 0)
        def _():
            leave(r, 0).wait()

    lax.fori_loop(0, 2 * blocks, finish, None)
    lax.fori_loop(0, blocks, lambda n, _: finished(n).wait(), None)
    lax.fori_loop(0, blocks, lambda n, _: summed(n).wait(), None)
    edge_done.wait()


def attend(slot, third, near, x, edge, main, cross, thirds):
    blocks = x.shape[0]
    lanes = len(thirds)
    bf16 = jnp.bfloat16
    pair = (2,) + x.shape[2:]
    return pl.pallas_call(
        functools.partial(attend_kernel, blocks, lanes),
        out_shape=(
            pltpu.HBM(x.shape, bf16),
            pltpu.HBM(main.shape, bf16),
            pltpu.HBM(edge.shape, bf16),
            pltpu.HBM((blocks,) + pair, jnp.float32),
        ),
        in_specs=[SMEM, SMEM, SMEM, VMEM, VMEM, VMEM] + [ANY] * (1 + lanes),
        out_specs=(ANY, ANY, ANY, ANY),
        scratch_shapes=[
            pltpu.VMEM(cross.shape, bf16),
            pltpu.VMEM((2 * blocks,) + pair, bf16),
            pltpu.VMEM((blocks,) + pair, bf16),
            pltpu.VMEM((blocks,) + pair, jnp.float32),
            pltpu.VMEM(edge.shape, bf16),
            pltpu.SemaphoreType.DMA((2,)),
            pltpu.SemaphoreType.DMA((2 * blocks,)),
            pltpu.SemaphoreType.DMA((blocks,)),
            pltpu.SemaphoreType.DMA((blocks,)),
            pltpu.SemaphoreType.DMA,
        ],
        compiler_params=params(),
        cost_estimate=cost(
            5 * 2 * blocks * 4 * BLOCK * BLOCK * HEAD_DIM, 2 * (3 * x.size + 2 * main.size)
        ),
        name="attend",
    )(slot, third, near, x, edge, main, cross, *thirds)


def land_thirds_kernel(blocks, lanes, third_ref, sum_ref, back_ref, *refs):
    thirds, total = refs[:lanes], refs[lanes]
    late, sems = refs[lanes + 1 :]
    f32 = jnp.float32

    def arrive(at):
        step, half = divmod(at, 2)
        return pltpu.make_async_copy(thirds[step].at[half], late.at[at], sems.at[at])

    for at in range(1, 2 * lanes):

        @pl.when(third_ref[at] >= 0)
        def _():
            arrive(at).start()

    total[...] = sum_ref[...]
    total[blocks - 1] += back_ref[...].astype(f32)
    for at in range(1, 2 * lanes):

        @pl.when(third_ref[at] >= 0)
        def _():
            arrive(at).wait()
            total[third_ref[at]] += late[at].astype(f32)


def land_thirds(third_index, sums, back, thirds):
    blocks = sums.shape[0]
    lanes = len(thirds)
    return pl.pallas_call(
        functools.partial(land_thirds_kernel, blocks, lanes),
        out_shape=jax.ShapeDtypeStruct(sums.shape, jnp.float32),
        in_specs=[SMEM, VMEM, VMEM] + [ANY] * lanes,
        out_specs=VMEM,
        scratch_shapes=[
            pltpu.VMEM((2 * lanes,) + back.shape, back.dtype),
            pltpu.SemaphoreType.DMA((2 * lanes,)),
        ],
        compiler_params=params(),
        cost_estimate=cost(sums.size * 2, 8 * sums.size),
        name="land_thirds",
    )(third_index, sums, back, *thirds)


def land_kernel(
    slots, blocks, rank_ref, index_ref, sums, home, _, out, total, late, low, sum_sems, home_sems, out_sems
):
    def read(n):
        return pltpu.make_async_copy(sums.at[n], total.at[n], sum_sems.at[n])

    def arrive(slot):
        return pltpu.make_async_copy(home.at[slot], late.at[slot], home_sems.at[slot])

    def write(n):
        return pltpu.make_async_copy(low.at[n], out.at[n, pl.ds(2, 2)], out_sems.at[n])

    start_all([read(n) for n in range(blocks)])
    start_all([arrive(slot) for slot in range(slots)])
    wait_all([read(n) for n in range(blocks)])

    def one(slot, _):
        arrive(slot).wait()

        @pl.when(slot // 2 != rank_ref[0])
        def _():
            total[index_ref[slot]] += late[slot].astype(jnp.float32)

    lax.fori_loop(0, slots, one, None)

    def put(n, _):
        low[n] = total[n].astype(low.dtype)
        write(n).start()

    lax.fori_loop(0, blocks, put, None)
    wait_all([write(n) for n in range(blocks)])


def land(rank, index, sums, home, final):
    slots = index.shape[0]
    blocks = sums.shape[0]
    bf16 = jnp.bfloat16
    return pl.pallas_call(
        functools.partial(land_kernel, slots, blocks),
        out_shape=pltpu.HBM(final.shape, bf16),
        in_specs=[SMEM, SMEM, ANY, ANY, ANY],
        out_specs=ANY,
        scratch_shapes=[
            pltpu.VMEM(sums.shape, jnp.float32),
            pltpu.VMEM(home.shape, bf16),
            pltpu.VMEM(sums.shape, bf16),
            pltpu.SemaphoreType.DMA((blocks,)),
            pltpu.SemaphoreType.DMA((slots,)),
            pltpu.SemaphoreType.DMA((blocks,)),
        ],
        input_output_aliases={4: 0},
        compiler_params=params(VMEM_ALL),
        cost_estimate=cost(sums.size * 2, 6 * sums.size + 2 * home.size),
        name="land",
    )(rank, index, sums, home, final)


def plan(key_lists, blocks, ctx_count, lanes):
    i32 = jnp.int32
    me = lax.axis_index("ctx")
    half, lane = me // lanes, me % lanes
    requests = 2 * blocks
    far_all = key_lists[:, 2:].reshape(ctx_count, requests)
    source, inside = far_all // blocks, far_all % blocks
    earlier = (jnp.arange(requests)[None, :] < jnp.arange(requests)[:, None])[None]
    rank = jnp.sum(((source[:, None, :] == source[:, :, None]) & earlier).astype(i32), axis=2)
    is_third = rank == 2
    order = jnp.sum((is_third[:, None, :] & earlier).astype(i32), axis=2)

    pair = jnp.arange(2, dtype=i32)[None, :, None]
    wanted = (source[:, None, :] == me) & (rank[:, None, :] == pair)
    send_main = jnp.sum(jnp.where(wanted, inside[:, None, :], 0), axis=2).reshape(-1)

    from_me = is_third & (source == me)
    third_of = jnp.sum(jnp.where(from_me, inside + 1, 0), axis=1) - 1
    step = jnp.arange(lanes, dtype=i32)[:, None]
    side = jnp.arange(2, dtype=i32)[None, :]
    asker = jnp.where(side == 0, half, 1 - half) * lanes + (lane + step) % lanes
    hit = asker[:, :, None] == jnp.arange(ctx_count, dtype=i32)[None, None, :]
    third_index = jnp.sum(jnp.where(hit, third_of[None, None, :], 0), axis=2).reshape(-1)

    def row(of, array):
        at = jnp.arange(ctx_count, dtype=i32)[:, None] == of
        return jnp.sum(jnp.where(at, array, 0), axis=0)

    slot_of = jnp.where(is_third, -1, source * 2 + rank)
    my_slot = row(me, slot_of)
    is_jth = (is_third[:, None, :] & (order[:, None, :] == pair)).astype(i32)
    third_source = jnp.sum(is_jth * source[:, None, :], axis=2)
    third_request = jnp.sum(is_jth * jnp.arange(requests, dtype=i32), axis=2)

    def steps(of):
        slab = row(of, third_source)
        return jnp.where(slab // lanes == half, (lane - slab % lanes + lanes) % lanes, -1)

    partner = (me + lanes) % ctx_count
    return (
        send_main,
        third_index,
        my_slot,
        row(me, third_request),
        steps(me),
        steps(partner),
    )


def body(queries, keys, values, out_grad, key_lists):
    ctx_count = lax.axis_size("ctx")
    blocks = lax.axis_size("head")
    lanes = ctx_count // 2
    send_main, third_index, my_slot, my_third, near_steps, cross_steps = plan(
        key_lists, blocks, ctx_count, lanes
    )

    def head_exchange(array):
        return lax.all_to_all(array, "head", split_axis=0, concat_axis=0, tiled=True)

    def ctx_exchange(array):
        return lax.all_to_all(array, "ctx", split_axis=0, concat_axis=0, tiled=True)

    def move(array, target):
        return lax.ppermute(array, "ctx", [(i, target(i)) for i in range(ctx_count)])

    def across(array):
        return move(array, lambda i: (i + lanes) % ctx_count)

    def along(arrays, sign):
        def target(step):
            return lambda i: i // lanes * lanes + (i + sign * step) % lanes

        return [arrays[0]] + [move(arrays[s], target(s)) for s in range(1, lanes)]

    x = head_exchange(split_heads(keys, values, queries, out_grad))
    third_blocks = pick_third(third_index, x)
    send_main, third_blocks = lax.optimization_barrier((send_main, third_blocks))
    thirds = along(third_blocks, 1)
    edge = move(x[blocks - 1, :2], lambda i: (i + 1) % ctx_count)
    main = ctx_exchange(pick_blocks(send_main, x))
    cross = across(pick_cross(cross_steps, thirds))
    listed = (my_slot, my_third, near_steps, x, edge, main, cross)
    third_grad = attend_thirds(*listed, thirds)
    cross_grad = across(third_grad)
    my_slot, third_grad = lax.optimization_barrier((my_slot, third_grad))
    final, main_grad, edge_grad, sums = attend(my_slot, *listed[1:], thirds)
    main_grad, edge_grad, cross_grad = lax.optimization_barrier((main_grad, edge_grad, cross_grad))
    home = ctx_exchange(main_grad)
    back = move(edge_grad, lambda i: (i - 1) % ctx_count)
    late = along(pick_back(near_steps, cross_steps, third_grad, cross_grad, lanes), -1)
    sums = land_thirds(third_index, sums, back, late)
    rank = lax.axis_index("ctx").reshape(1)
    final = head_exchange(land(rank, send_main, sums, home, final))
    return join_heads(final)


def solution(mesh):
    tokens = P(("ctx", "head"), None)
    return jax.shard_map(
        body,
        mesh=mesh,
        in_specs=(tokens, tokens, tokens, tokens, P()),
        out_specs=(tokens, tokens, tokens, tokens),
        check_vma=False,
    )
```

```python
import functools

import jax
import jax.numpy as jnp
from jax import lax
from jax.experimental import pallas as pl
from jax.experimental.pallas import tpu as pltpu
from jax.sharding import PartitionSpec as P

HEAD_DIM = 128
BLOCK = 128
ANY = pl.BlockSpec(memory_space=pl.ANY)
VMEM = pl.BlockSpec(memory_space=pltpu.VMEM)
SMEM = pl.BlockSpec(memory_space=pltpu.SMEM)
SPLIT_LIMIT = 58 * 1024 * 1024 + 256 * 1024
HEAD_ORDER = (
    (0, 0), (2, 0), (0, 1), (1, 0), (3, 1), (0, 2), (2, 1), (1, 1),
    (0, 3), (3, 0), (2, 2), (1, 2), (3, 2), (2, 3), (1, 3), (3, 3),
)
FAR_ORDER = (
    (1, 0), (1, 4), (1, 1), (1, 2), (0, 1), (1, 3), (0, 2), (1, 5),
    (0, 3), (1, 6), (0, 4), (1, 7), (0, 5), (0, 6), (0, 7),
)


def call(kernel, out_shape, ins, outs, name, flops, nbytes, scratch=(), limit=16 * 1024 * 1024):
    return pl.pallas_call(
        kernel,
        out_shape=out_shape,
        in_specs=list(ins),
        out_specs=outs,
        scratch_shapes=list(scratch),
        compiler_params=pltpu.CompilerParams(vmem_limit_bytes=limit),
        cost_estimate=pl.CostEstimate(flops=flops, bytes_accessed=nbytes, transcendentals=0),
        name=name,
    )


def dot(a, b, dims):
    return lax.dot_general(a, b, (dims, ((), ())), preferred_element_type=jnp.float32)


def columns(index):
    return pl.ds(pl.multiple_of(index * HEAD_DIM, HEAD_DIM), HEAD_DIM)


def split_kernel(parts, count, to_ref, *refs):
    arrays, outs = refs[:count], refs[count : count + parts]
    held, sems = refs[count + parts :]
    copies = [pltpu.make_async_copy(arrays[w], held.at[w], sems.at[w]) for w in range(count)]
    for copy in copies:
        copy.start()
    for w in range(count):
        copies[w].wait()
        for s in range(parts):
            outs[s][w] = held[w, :, columns(to_ref[s])]


def split_heads(to, *arrays):
    rows, features = arrays[0].shape
    parts, count = features // HEAD_DIM, len(arrays)
    dtype = arrays[0].dtype
    return call(
        functools.partial(split_kernel, parts, count),
        (pltpu.VMEM((count, rows, HEAD_DIM), dtype),) * parts,
        [SMEM] + [ANY] * count,
        (VMEM,) * parts,
        "split_heads",
        0,
        4 * count * arrays[0].size,
        [pltpu.VMEM((count, rows, features), dtype), pltpu.SemaphoreType.DMA((count,))],
        SPLIT_LIMIT,
    )(to, *arrays)


def join_kernel(parts, count, from_ref, *refs):
    ins, outs = refs[:parts], refs[parts : parts + count]
    held, sems = refs[parts + count :]
    copies = [pltpu.make_async_copy(held.at[w], outs[w], sems.at[w]) for w in range(count)]
    for w in range(count):
        for s in range(parts):
            held[w, :, columns(from_ref[s])] = ins[s][w]
        copies[w].start()
    for copy in copies:
        copy.wait()


def join_heads(source, parts):
    count, rows, depth = parts[0].shape
    features, dtype = len(parts) * depth, parts[0].dtype
    return call(
        functools.partial(join_kernel, len(parts), count),
        (jax.ShapeDtypeStruct((rows, features), dtype),) * count,
        [SMEM] + [VMEM] * len(parts),
        (ANY,) * count,
        "join_heads",
        0,
        4 * count * rows * features,
        [pltpu.VMEM((count, rows, features), dtype), pltpu.SemaphoreType.DMA((count,))],
    )(source, *parts)


def spread_kernel(blocks, lanes, from_ref, main_ref, third_ref, *refs):
    ins, x_ref, edge_ref = refs[:blocks], refs[blocks], refs[blocks + 1]
    thirds, mains = refs[blocks + 2 : blocks + 2 + lanes], refs[blocks + 2 + lanes :]
    for s in range(blocks):
        x_ref[from_ref[s]] = ins[s][...]
    edge_ref[...] = x_ref[blocks - 1, pl.ds(0, 2)]
    for step in range(lanes):
        for side in range(2):
            index = third_ref[2 * step + side]

            @pl.when(index >= 0)
            def _():
                thirds[step][side] = x_ref[index, pl.ds(0, 2)]

    for o in range(len(mains)):
        for rank in range(2):
            mains[o][rank] = x_ref[main_ref[2 * o + rank], pl.ds(0, 2)]


def spread(source, main_index, third_index, parts):
    blocks, lanes, routes = len(parts), third_index.shape[0] // 2, main_index.shape[0] // 2
    dtype = parts[0].dtype
    pair = jax.ShapeDtypeStruct((2, 2) + parts[0].shape[1:], dtype)
    outs = call(
        functools.partial(spread_kernel, blocks, lanes),
        (
            jax.ShapeDtypeStruct((blocks,) + parts[0].shape, dtype),
            jax.ShapeDtypeStruct((2,) + parts[0].shape[1:], dtype),
        )
        + (pair,) * (lanes + routes),
        [SMEM] * 3 + [VMEM] * blocks,
        (VMEM,) * (2 + lanes + routes),
        "spread",
        0,
        4 * blocks * parts[0].size,
    )(source, main_index, third_index, *parts)
    return outs[0], outs[1], outs[2 : 2 + lanes], outs[2 + lanes :]


def pick_cross_kernel(lanes, step_ref, *refs):
    ins, out_ref = refs[:lanes], refs[lanes]
    for j in range(2):
        for step in range(lanes):

            @pl.when(step_ref[j] == step)
            def _():
                out_ref[j] = ins[step][1]


def pick_cross(steps, thirds):
    lanes = len(thirds)
    return call(
        functools.partial(pick_cross_kernel, lanes),
        jax.ShapeDtypeStruct(thirds[0].shape, thirds[0].dtype),
        [SMEM] + [VMEM] * lanes,
        VMEM,
        "pick_cross",
        0,
        4 * thirds[0].size,
    )(steps, *thirds)


def pick_back_kernel(lanes, near_ref, cross_ref, own, crossed, *outs):
    for j in range(2):
        for step in range(lanes):

            @pl.when(near_ref[j] == step)
            def _():
                outs[step][0] = own[j]

            @pl.when(cross_ref[j] == step)
            def _():
                outs[step][1] = crossed[j]


def pick_back(near_steps, cross_steps, own, crossed, lanes):
    return call(
        functools.partial(pick_back_kernel, lanes),
        (jax.ShapeDtypeStruct(own.shape, own.dtype),) * lanes,
        [SMEM, SMEM, VMEM, VMEM],
        (VMEM,) * lanes,
        "pick_back",
        0,
        8 * own.size,
    )(near_steps, cross_steps, own, crossed)


def attention(q, g, k, v):
    scale = HEAD_DIM ** (-0.5)
    s = dot(k, q, ((1,), (1,))) * scale
    dp = dot(v, g, ((1,), (1,)))
    w = jnp.exp(s - jnp.max(s, axis=0, keepdims=True))
    p = w * (1.0 / jnp.sum(w, axis=0, keepdims=True))
    p_low = p.astype(jnp.bfloat16)
    delta = jnp.sum(p_low.astype(jnp.float32) * dp, axis=0, keepdims=True)
    return p_low, (p * (dp - delta) * scale).astype(jnp.bfloat16)


def collect_kernel(lanes, routes, request_ref, third_ref, near_ref, x_ref, edge_ref, cross_ref, *refs):
    thirds, mains = refs[:lanes], refs[lanes : lanes + routes]
    far_ref, grad_ref = refs[lanes + routes :]
    for o in range(routes):
        for rank in range(2):
            far_ref[request_ref[2 * o + rank]] = mains[o][rank]
    for j in range(2):
        for step in range(1, lanes):

            @pl.when(near_ref[j] == step)
            def _():
                far_ref[third_ref[j]] = thirds[step][0]

        @pl.when(near_ref[j] < 0)
        def _():
            far_ref[third_ref[j]] = cross_ref[j]

    for j in range(2):
        r = third_ref[j]
        n = r // 2
        other = n * 4 + 1 - r
        listed = []
        for which in range(2):
            before = jnp.where(n == 0, edge_ref[which], x_ref[jnp.maximum(n - 1, 0), which])
            listed.append(
                jnp.concatenate(
                    [far_ref[r, which], x_ref[n, which], before, far_ref[other, which]], axis=0
                )
            )
        q, g = x_ref[n, 2], x_ref[n, 3]
        p_low, ds = attention(q, g, *listed)
        grad_ref[j, 0] = dot(ds[:BLOCK], q, ((1,), (0,))).astype(grad_ref.dtype)
        grad_ref[j, 1] = dot(p_low[:BLOCK], g, ((1,), (0,))).astype(grad_ref.dtype)


def collect(request, third, near, x, edge, cross, thirds, mains):
    lanes, routes = len(thirds), len(mains)
    blocks = x.shape[0]
    return call(
        functools.partial(collect_kernel, lanes, routes),
        (
            jax.ShapeDtypeStruct((2 * blocks, 2) + x.shape[2:], x.dtype),
            jax.ShapeDtypeStruct(cross.shape, cross.dtype),
        ),
        [SMEM] * 3 + [VMEM] * (3 + lanes + routes),
        (VMEM, VMEM),
        "collect",
        5 * 2 * 2 * 4 * BLOCK * BLOCK * HEAD_DIM,
        4 * x.size,
    )(request, third, near, x, edge, cross, *thirds, *mains)


def attend_kernel(blocks, routes, request_ref, x_ref, edge_ref, far_ref, *refs):
    out_ref, sum_ref, edge_out = refs[:3]
    backs, far_out = refs[3 : 3 + routes], refs[3 + routes]
    bf16 = jnp.bfloat16

    def one(n, first):
        q, g = x_ref[n, 2], x_ref[n, 3]
        r2, r3 = 2 * n, 2 * n + 1
        listed = []
        for which in range(2):
            before = edge_ref[which] if first else x_ref[n - 1, which]
            listed.append(
                jnp.concatenate([x_ref[n, which], before, far_ref[r2, which], far_ref[r3, which]], axis=0)
            )
        k, v = listed
        p_low, ds = attention(q, g, k, v)
        out_ref[n, 0] = dot(p_low, v, ((0,), (0,))).astype(bf16)
        out_ref[n, 1] = dot(ds, k, ((0,), (0,))).astype(bf16)
        dk = dot(ds, q, ((1,), (0,)))
        dv = dot(p_low, g, ((1,), (0,)))
        for which, d in enumerate((dk, dv)):
            sum_ref[n, which] = d[:BLOCK]
            if first:
                edge_out[which] = d[BLOCK : 2 * BLOCK].astype(bf16)
            else:
                sum_ref[n - 1, which] += d[BLOCK : 2 * BLOCK]
            far_out[r2, which] = d[2 * BLOCK : 3 * BLOCK].astype(bf16)
            far_out[r3, which] = d[3 * BLOCK :].astype(bf16)

    one(0, True)
    lax.fori_loop(1, blocks, lambda n, _: one(n, False), None, unroll=3)
    for o in range(routes):
        for rank in range(2):
            backs[o][rank] = far_out[request_ref[2 * o + rank]]


def attend(request, x, edge, far):
    blocks, routes = x.shape[0], request.shape[0] // 2
    pair = (2,) + x.shape[2:]
    outs = call(
        functools.partial(attend_kernel, blocks, routes),
        (
            jax.ShapeDtypeStruct((blocks,) + pair, x.dtype),
            jax.ShapeDtypeStruct((blocks,) + pair, jnp.float32),
            jax.ShapeDtypeStruct(edge.shape, x.dtype),
        )
        + (jax.ShapeDtypeStruct((2,) + pair, x.dtype),) * routes,
        [SMEM, VMEM, VMEM, VMEM],
        (VMEM,) * (3 + routes),
        "attend",
        5 * 2 * blocks * 4 * BLOCK * BLOCK * HEAD_DIM,
        2 * (3 * x.size + 2 * far.size),
        [pltpu.VMEM(far.shape, x.dtype)],
    )(request, x, edge, far)
    return outs[0], outs[1], outs[2], outs[3:]


def land_kernel(
    blocks, lanes, routes, to_ref, main_ref, third_ref, own_ref, sum_ref, edge_ref, *refs
):
    thirds, mains = refs[:lanes], refs[lanes : lanes + routes]
    outs, total = refs[lanes + routes : lanes + routes + blocks], refs[lanes + routes + blocks]
    f32 = jnp.float32
    total[...] = sum_ref[...]
    total[blocks - 1] += edge_ref[...].astype(f32)
    for step in range(lanes):
        for side in range(2):
            index = third_ref[2 * step + side]

            @pl.when(index >= 0)
            def _():
                total[index] += thirds[step][side].astype(f32)

    for o in range(routes):
        for rank in range(2):
            total[main_ref[2 * o + rank]] += mains[o][rank].astype(f32)
    for s in range(blocks):
        n = to_ref[s]
        outs[s][pl.ds(0, 2)] = own_ref[n]
        outs[s][pl.ds(2, 2)] = total[n].astype(own_ref.dtype)


def land(to, main_index, third_index, out, sums, edge, thirds, mains):
    blocks, lanes, routes = sums.shape[0], len(thirds), len(mains)
    return call(
        functools.partial(land_kernel, blocks, lanes, routes),
        (jax.ShapeDtypeStruct((4,) + sums.shape[2:], out.dtype),) * blocks,
        [SMEM] * 3 + [VMEM] * (3 + lanes + routes),
        (VMEM,) * blocks,
        "land",
        sums.size * 2,
        10 * sums.size,
        [pltpu.VMEM(sums.shape, jnp.float32)],
    )(to, main_index, third_index, out, sums, edge, *thirds, *mains)


def plan(key_lists, blocks, ctx_count, lanes):
    i32 = jnp.int32
    me = lax.axis_index("ctx")
    half, lane = me // lanes, me % lanes
    requests = 2 * blocks
    slabs = jnp.arange(ctx_count, dtype=i32)
    numbers = jnp.arange(requests, dtype=i32)
    far_all = key_lists[:, 2:].reshape(ctx_count, requests)
    source, inside = far_all // blocks, far_all % blocks
    earlier = (numbers[None, :] < numbers[:, None])[None]
    rank = jnp.sum(((source[:, None, :] == source[:, :, None]) & earlier).astype(i32), axis=2)
    is_third = rank == 2
    order = jnp.sum((is_third[:, None, :] & earlier).astype(i32), axis=2)
    pair = jnp.arange(2, dtype=i32)[None, :, None]

    wanted = (source[:, None, :] == me) & (rank[:, None, :] == pair)
    send_main = jnp.sum(jnp.where(wanted, inside[:, None, :], 0), axis=2)
    from_me = is_third & (source == me)
    third_of = jnp.sum(jnp.where(from_me, inside + 1, 0), axis=1) - 1

    flip = jnp.array([o[0] for o in FAR_ORDER], i32)
    shift = jnp.array([o[1] for o in FAR_ORDER], i32)
    side = jnp.where(flip == 1, 1 - half, half) * lanes
    asker = side + (lane + shift) % lanes
    giver = side + (lane - shift + lanes) % lanes
    asks = (asker[:, None] == slabs[None, :])[:, :, None]
    main_index = jnp.sum(jnp.where(asks, send_main[None], 0), axis=1).reshape(-1)

    step = jnp.arange(lanes, dtype=i32)[:, None]
    third_asker = jnp.concatenate([half * lanes + (lane + step) % lanes, (1 - half) * lanes + (lane + step) % lanes], axis=1)
    hit = third_asker[:, :, None] == slabs[None, None, :]
    third_index = jnp.sum(jnp.where(hit, third_of[None, None, :], 0), axis=2).reshape(-1)

    def row(of, array):
        return jnp.sum(jnp.where(slabs[:, None] == of, array, 0), axis=0)

    my_source, my_rank = row(me, source), row(me, rank)
    serves = (giver[:, None, None] == my_source[None, None, :]) & (pair == my_rank[None, None, :])
    request = jnp.sum(jnp.where(serves, numbers[None, None, :], 0), axis=2).reshape(-1)

    is_jth = (is_third[:, None, :] & (order[:, None, :] == pair)).astype(i32)
    third_source = jnp.sum(is_jth * source[:, None, :], axis=2)
    third_request = jnp.sum(is_jth * numbers, axis=2)

    def steps(of):
        slab = row(of, third_source)
        return jnp.where(slab // lanes == half, (lane - slab % lanes + lanes) % lanes, -1)

    partner = (me + lanes) % ctx_count
    return main_index, third_index, request, row(me, third_request), steps(me), steps(partner)


def body(queries, keys, values, out_grad, key_lists):
    ctx_count = lax.axis_size("ctx")
    blocks = lax.axis_size("head")
    lanes = ctx_count // 2
    side = 4
    main_index, third_index, request, my_third, near_steps, cross_steps = plan(
        key_lists, blocks, ctx_count, lanes
    )
    head = lax.axis_index("head")
    along_z = jnp.array([o[0] for o in HEAD_ORDER], jnp.int32)
    along_x = jnp.array([o[1] for o in HEAD_ORDER], jnp.int32)
    to = (head // side + along_z) % side * side + (head % side + along_x) % side
    source = (head // side - along_z + side) % side * side + (head % side - along_x + side) % side

    def head_exchange(parts):
        def target(shift):
            dz, dx = shift
            return [(i, (i // side + dz) % side * side + (i % side + dx) % side) for i in range(blocks)]

        return [parts[0]] + [
            lax.ppermute(part, "head", target(shift)) for part, shift in zip(parts[1:], HEAD_ORDER[1:])
        ]

    def move(array, flip, shift):
        def target(i):
            return (i // lanes + flip) % 2 * lanes + (i % lanes + shift) % lanes

        return lax.ppermute(array, "ctx", [(i, target(i)) for i in range(ctx_count)])

    def far_exchange(thirds, make_cross, mains, edge, edge_by, sign):
        edge = lax.ppermute(edge, "ctx", [(i, (i + edge_by) % ctx_count) for i in range(ctx_count)])
        got_thirds, got = [thirds[0]], []
        for at in range(len(FAR_ORDER)):
            if at < lanes - 1:
                got_thirds.append(move(thirds[at + 1], 0, sign * (at + 1)))
            if at == lanes and make_cross:
                cross = move(make_cross(got_thirds), 1, 0)
            flip, shift = FAR_ORDER[at]
            got.append(move(mains[at], flip, sign * shift))
        return (edge, got_thirds, got) + ((cross,) if make_cross else ())

    parts = head_exchange(split_heads(to, keys, values, queries, out_grad))
    x, edge, thirds, mains = spread(source, main_index, third_index, parts)
    edge, thirds, mains, cross = far_exchange(
        thirds, lambda got: pick_cross(cross_steps, got), mains, edge, 1, 1
    )
    far, third_grad = collect(request, my_third, near_steps, x, edge, cross, thirds, mains)
    cross_grad = move(third_grad, 1, 0)
    out, sums, edge_grad, backs = attend(request, x, edge, far)
    thirds = pick_back(near_steps, cross_steps, third_grad, cross_grad, lanes)
    edge_grad, thirds, backs = far_exchange(thirds, None, backs, edge_grad, -1, -1)
    parts = land(to, main_index, third_index, out, sums, edge_grad, thirds, backs)
    return join_heads(source, head_exchange(parts))


def solution(mesh):
    tokens = P(("ctx", "head"), None)
    return jax.shard_map(
        body,
        mesh=mesh,
        in_specs=(tokens, tokens, tokens, tokens, P()),
        out_specs=(tokens, tokens, tokens, tokens),
        check_vma=False,
    )
```

```python
import functools

import jax
import jax.numpy as jnp
from jax import lax
from jax.experimental import pallas as pl
from jax.experimental.pallas import tpu as pltpu
from jax.sharding import PartitionSpec as P

HEAD_DIM = 128
BLOCK = 128
ANY = pl.BlockSpec(memory_space=pl.ANY)
VMEM = pl.BlockSpec(memory_space=pltpu.VMEM)
SMEM = pl.BlockSpec(memory_space=pltpu.SMEM)
FULL = 60 * 1024 * 1024


def call(kernel, out_shape, ins, outs, name, flops, nbytes, scratch=(), limit=52 * 1024 * 1024):
    return pl.pallas_call(
        kernel,
        out_shape=out_shape,
        in_specs=list(ins),
        out_specs=outs,
        scratch_shapes=list(scratch),
        compiler_params=pltpu.CompilerParams(vmem_limit_bytes=limit),
        cost_estimate=pl.CostEstimate(flops=flops, bytes_accessed=nbytes, transcendentals=0),
        name=name,
    )


def start_all(copies):
    for copy in copies:
        copy.start()


def wait_all(copies):
    for copy in copies:
        copy.wait()


def dot(a, b, dims):
    return lax.dot_general(a, b, (dims, ((), ())), preferred_element_type=jnp.float32)


def split_kernel(heads, count, *refs):
    arrays, out = refs[:count], refs[count]
    held, packed, sems, out_sems = refs[count + 1 :]
    reads = [pltpu.make_async_copy(arrays[w], held.at[w], sems.at[w]) for w in range(count)]
    writes = [
        pltpu.make_async_copy(packed.at[head], out.at[head], out_sems.at[head]) for head in range(heads)
    ]
    start_all(reads)
    wait_all(reads)
    for head in range(heads):
        for w in range(count):
            packed[head, w] = held[w, :, pl.ds(head * HEAD_DIM, HEAD_DIM)]
        writes[head].start()
    wait_all(writes)


def split_heads(*arrays):
    rows, features = arrays[0].shape
    heads, count = features // HEAD_DIM, len(arrays)
    dtype = arrays[0].dtype
    packed = (heads, count, rows, HEAD_DIM)
    return call(
        functools.partial(split_kernel, heads, count),
        pltpu.HBM(packed, dtype),
        [ANY] * count,
        ANY,
        "split_heads",
        0,
        4 * count * arrays[0].size,
        [
            pltpu.VMEM((count, rows, features), dtype),
            pltpu.VMEM(packed, dtype),
            pltpu.SemaphoreType.DMA((count,)),
            pltpu.SemaphoreType.DMA((heads,)),
        ],
        FULL,
    )(*arrays)


def join_kernel(heads, count, in_ref, *refs):
    outs = refs[:count]
    held, sems = refs[count:]
    writes = [pltpu.make_async_copy(held.at[w], outs[w], sems.at[w]) for w in range(count)]
    for w in range(count):
        for head in range(heads):
            held[w, :, pl.ds(head * HEAD_DIM, HEAD_DIM)] = in_ref[head, w]
        writes[w].start()
    wait_all(writes)


def join_heads(packed):
    heads, count, rows, depth = packed.shape
    features, dtype = heads * depth, packed.dtype
    return call(
        functools.partial(join_kernel, heads, count),
        (pltpu.HBM((rows, features), dtype),) * count,
        [VMEM],
        (ANY,) * count,
        "join_heads",
        0,
        4 * packed.size,
        [pltpu.VMEM((count, rows, features), dtype), pltpu.SemaphoreType.DMA((count,))],
    )(packed)


def pick_third_kernel(blocks, lanes, third_ref, kv_ref, *refs):
    thirds, edge_ref = refs[:lanes], refs[lanes]
    edge_ref[...] = kv_ref[blocks - 1]
    for step in range(lanes):
        for side in range(2):
            index = third_ref[2 * step + side]

            @pl.when(index >= 0)
            def _():
                thirds[step][side] = kv_ref[index]


def pick_third(index, kv):
    lanes = index.shape[0] // 2
    outs = call(
        functools.partial(pick_third_kernel, kv.shape[0], lanes),
        (jax.ShapeDtypeStruct((2,) + kv.shape[1:], kv.dtype),) * lanes
        + (jax.ShapeDtypeStruct(kv.shape[1:], kv.dtype),),
        [SMEM, VMEM],
        (VMEM,) * (lanes + 1),
        "pick_third",
        0,
        8 * kv[0].size,
    )(index, kv)
    return outs[:lanes], outs[lanes]


def pack_kernel(rows, limit, index_ref, in_ref, out, sems):
    copies = [
        pltpu.make_async_copy(in_ref.at[jnp.minimum(index_ref[i], limit)], out.at[i], sems.at[i])
        for i in range(rows)
    ]
    start_all(copies)
    wait_all(copies)


def pack(index, array):
    rows = index.shape[0]
    return call(
        functools.partial(pack_kernel, rows, array.shape[0] - 1),
        pltpu.HBM((rows,) + array.shape[1:], array.dtype),
        [SMEM, VMEM],
        ANY,
        "pack",
        0,
        4 * rows * array[0].size,
        [pltpu.SemaphoreType.DMA((rows,))],
    )(index, array)


def pick_cross_kernel(lanes, step_ref, *refs):
    ins, out_ref = refs[:lanes], refs[lanes]
    for j in range(2):
        for step in range(lanes):

            @pl.when(step_ref[j] == step)
            def _():
                out_ref[j] = ins[step][1]


def pick_cross(steps, thirds):
    lanes = len(thirds)
    return call(
        functools.partial(pick_cross_kernel, lanes),
        jax.ShapeDtypeStruct(thirds[0].shape, thirds[0].dtype),
        [SMEM] + [VMEM] * lanes,
        VMEM,
        "pick_cross",
        0,
        4 * thirds[0].size,
    )(steps, *thirds)


def pick_back_kernel(lanes, near_ref, cross_ref, own, crossed, *outs):
    for j in range(2):
        for step in range(lanes):

            @pl.when(near_ref[j] == step)
            def _():
                outs[step][0] = own[j]

            @pl.when(cross_ref[j] == step)
            def _():
                outs[step][1] = crossed[j]


def pick_back(near_steps, cross_steps, own, crossed, lanes):
    return call(
        functools.partial(pick_back_kernel, lanes),
        (jax.ShapeDtypeStruct(own.shape, own.dtype),) * lanes,
        [SMEM, SMEM, VMEM, VMEM],
        (VMEM,) * lanes,
        "pick_back",
        0,
        8 * own.size,
    )(near_steps, cross_steps, own, crossed)


def attention(q, g, k, v):
    scale = HEAD_DIM ** (-0.5)
    s = dot(k, q, ((1,), (1,))) * scale
    dp = dot(v, g, ((1,), (1,)))
    w = jnp.exp(s - jnp.max(s, axis=0, keepdims=True))
    p = w * (1.0 / jnp.sum(w, axis=0, keepdims=True))
    p_low = p.astype(jnp.bfloat16)
    delta = jnp.sum(p_low.astype(jnp.float32) * dp, axis=0, keepdims=True)
    return p_low, (p * (dp - delta) * scale).astype(jnp.bfloat16)


def collect_kernel(lanes, slots, request_ref, third_ref, near_ref, kv_ref, qg_ref, edge_ref, cross_ref, main_ref, *refs):
    thirds = refs[:lanes]
    far_ref, grad_ref = refs[lanes:]
    for slot in range(slots):
        far_ref[request_ref[slot]] = main_ref[slot]
    for j in range(2):
        for step in range(1, lanes):

            @pl.when(near_ref[j] == step)
            def _():
                far_ref[third_ref[j]] = thirds[step][0]

        @pl.when(near_ref[j] < 0)
        def _():
            far_ref[third_ref[j]] = cross_ref[j]

    for j in range(2):
        r = third_ref[j]
        n = r // 2
        other = n * 4 + 1 - r
        listed = []
        for which in range(2):
            before = jnp.where(n == 0, edge_ref[which], kv_ref[jnp.maximum(n - 1, 0), which])
            listed.append(
                jnp.concatenate(
                    [far_ref[r, which], kv_ref[n, which], before, far_ref[other, which]], axis=0
                )
            )
        q, g = qg_ref[n, 0], qg_ref[n, 1]
        p_low, ds = attention(q, g, *listed)
        grad_ref[j, 0] = dot(ds[:BLOCK], q, ((1,), (0,))).astype(grad_ref.dtype)
        grad_ref[j, 1] = dot(p_low[:BLOCK], g, ((1,), (0,))).astype(grad_ref.dtype)


def collect(request, third, near, kv, qg, edge, cross, main, thirds):
    lanes, slots = len(thirds), main.shape[0]
    return call(
        functools.partial(collect_kernel, lanes, slots),
        (
            jax.ShapeDtypeStruct((slots + 1,) + kv.shape[1:], kv.dtype),
            jax.ShapeDtypeStruct(cross.shape, cross.dtype),
        ),
        [SMEM] * 3 + [VMEM] * (5 + lanes),
        (VMEM, VMEM),
        "collect",
        5 * 2 * 2 * 4 * BLOCK * BLOCK * HEAD_DIM,
        4 * main.size,
    )(request, third, near, kv, qg, edge, cross, main, *thirds)


def attend_kernel(blocks, kv_ref, qg_ref, edge_ref, far_ref, out, sum_ref, edge_out, far_out, out_ref, sems):
    bf16 = jnp.bfloat16

    def finished(n):
        return pltpu.make_async_copy(out_ref.at[n], out.at[n], sems.at[n])

    def one(n, first):
        q, g = qg_ref[n, 0], qg_ref[n, 1]
        r2, r3 = 2 * n, 2 * n + 1
        listed = []
        for which in range(2):
            before = edge_ref[which] if first else kv_ref[n - 1, which]
            listed.append(
                jnp.concatenate([kv_ref[n, which], before, far_ref[r2, which], far_ref[r3, which]], axis=0)
            )
        k, v = listed
        p_low, ds = attention(q, g, k, v)
        out_ref[n, 0] = dot(p_low, v, ((0,), (0,))).astype(bf16)
        out_ref[n, 1] = dot(ds, k, ((0,), (0,))).astype(bf16)
        finished(n).start()
        dk = dot(ds, q, ((1,), (0,)))
        dv = dot(p_low, g, ((1,), (0,)))
        for which, d in enumerate((dk, dv)):
            sum_ref[n, which] = d[:BLOCK]
            if first:
                edge_out[which] = d[BLOCK : 2 * BLOCK].astype(bf16)
            else:
                sum_ref[n - 1, which] += d[BLOCK : 2 * BLOCK]
            far_out[r2, which] = d[2 * BLOCK : 3 * BLOCK].astype(bf16)
            far_out[r3, which] = d[3 * BLOCK :].astype(bf16)

    one(0, True)
    lax.fori_loop(1, blocks, lambda n, _: one(n, False), None, unroll=3)
    wait_all([finished(n) for n in range(blocks)])


def attend(kv, qg, edge, far):
    blocks = kv.shape[0]
    bf16 = kv.dtype
    return call(
        functools.partial(attend_kernel, blocks),
        (
            pltpu.HBM(qg.shape, bf16),
            jax.ShapeDtypeStruct(kv.shape, jnp.float32),
            jax.ShapeDtypeStruct(edge.shape, bf16),
            jax.ShapeDtypeStruct((2 * blocks,) + kv.shape[1:], bf16),
        ),
        [VMEM] * 4,
        (ANY, VMEM, VMEM, VMEM),
        "attend",
        5 * 2 * blocks * 4 * BLOCK * BLOCK * HEAD_DIM,
        2 * (6 * kv.size + 2 * far.size),
        [pltpu.VMEM(qg.shape, bf16), pltpu.SemaphoreType.DMA((blocks,))],
    )(kv, qg, edge, far)


def land_kernel(
    blocks, lanes, slots, main_ref, third_ref, sum_ref, edge_ref, home_ref, *refs
):
    thirds, out = refs[:lanes], refs[lanes]
    total, low, sems = refs[lanes + 1 :]
    f32 = jnp.float32
    total[pl.ds(0, blocks)] = sum_ref[...]
    total[blocks - 1] += edge_ref[...].astype(f32)
    for step in range(lanes):
        for side in range(2):
            index = third_ref[2 * step + side]

            @pl.when(index >= 0)
            def _():
                total[index] += thirds[step][side].astype(f32)

    for slot in range(slots):
        total[main_ref[slot]] += home_ref[slot].astype(f32)
    writes = [pltpu.make_async_copy(low.at[n], out.at[n], sems.at[n]) for n in range(blocks)]
    for n in range(blocks):
        low[n] = total[n].astype(low.dtype)
        writes[n].start()
    wait_all(writes)


def land(main_index, third_index, sums, edge, home, thirds):
    blocks, lanes, slots = sums.shape[0], len(thirds), home.shape[0]
    return call(
        functools.partial(land_kernel, blocks, lanes, slots),
        pltpu.HBM(sums.shape, home.dtype),
        [SMEM] * 2 + [VMEM] * (3 + lanes),
        ANY,
        "land",
        sums.size * 2,
        10 * sums.size,
        [
            pltpu.VMEM((blocks + 1,) + sums.shape[1:], jnp.float32),
            pltpu.VMEM(sums.shape, home.dtype),
            pltpu.SemaphoreType.DMA((blocks,)),
        ],
    )(main_index, third_index, sums, edge, home, *thirds)


def plan(key_lists, blocks, ctx_count, lanes):
    i32 = jnp.int32
    me = lax.axis_index("ctx")
    half, lane = me // lanes, me % lanes
    requests = 2 * blocks
    slabs = jnp.arange(ctx_count, dtype=i32)
    numbers = jnp.arange(requests, dtype=i32)
    far_all = key_lists[:, 2:].reshape(ctx_count, requests)
    source, inside = far_all // blocks, far_all % blocks
    earlier = (numbers[None, :] < numbers[:, None])[None]
    rank = jnp.sum(((source[:, None, :] == source[:, :, None]) & earlier).astype(i32), axis=2)
    is_third = rank == 2
    order = jnp.sum((is_third[:, None, :] & earlier).astype(i32), axis=2)
    pair = jnp.arange(2, dtype=i32)[None, :, None]

    wanted = (source[:, None, :] == me) & (rank[:, None, :] == pair)
    send_main = jnp.sum(jnp.where(wanted, inside[:, None, :], 0), axis=2)
    main_index = jnp.where(slabs[:, None] == me, blocks, send_main).reshape(-1)
    from_me = is_third & (source == me)
    third_of = jnp.sum(jnp.where(from_me, inside + 1, 0), axis=1) - 1

    step = jnp.arange(lanes, dtype=i32)[:, None]
    side = jnp.arange(2, dtype=i32)[None, :]
    third_asker = jnp.where(side == 0, half, 1 - half) * lanes + (lane + step) % lanes
    hit = third_asker[:, :, None] == slabs[None, None, :]
    third_index = jnp.sum(jnp.where(hit, third_of[None, None, :], 0), axis=2).reshape(-1)

    def row(of, array):
        return jnp.sum(jnp.where(slabs[:, None] == of, array, 0), axis=0)

    my_source, my_rank = row(me, source), row(me, rank)
    serves = (slabs[:, None, None] == my_source[None, None, :]) & (pair == my_rank[None, None, :])
    request = jnp.sum(jnp.where(serves, numbers[None, None, :], 0), axis=2)
    request = jnp.where(slabs[:, None] == me, requests, request).reshape(-1)

    is_jth = (is_third[:, None, :] & (order[:, None, :] == pair)).astype(i32)
    third_source = jnp.sum(is_jth * source[:, None, :], axis=2)
    third_request = jnp.sum(is_jth * numbers, axis=2)

    def steps(of):
        slab = row(of, third_source)
        return jnp.where(slab // lanes == half, (lane - slab % lanes + lanes) % lanes, -1)

    partner = (me + lanes) % ctx_count
    return main_index, third_index, request, row(me, third_request), steps(me), steps(partner)


def body(queries, keys, values, out_grad, key_lists):
    ctx_count = lax.axis_size("ctx")
    blocks = lax.axis_size("head")
    lanes = ctx_count // 2
    main_index, third_index, request, my_third, near_steps, cross_steps = plan(
        key_lists, blocks, ctx_count, lanes
    )

    def head_exchange(array):
        return lax.all_to_all(array, "head", split_axis=0, concat_axis=0, tiled=True)

    def ctx_exchange(array):
        return lax.all_to_all(array, "ctx", split_axis=0, concat_axis=0, tiled=True)

    def move(array, target):
        return lax.ppermute(array, "ctx", [(i, target(i)) for i in range(ctx_count)])

    def across(array):
        return move(array, lambda i: (i + lanes) % ctx_count)

    def along(arrays, sign):
        def target(step):
            return lambda i: i // lanes * lanes + (i + sign * step) % lanes

        return [arrays[0]] + [move(arrays[s], target(s)) for s in range(1, lanes)]

    kv = head_exchange(split_heads(keys, values))
    qg = head_exchange(split_heads(queries, out_grad))
    thirds, edge = pick_third(third_index, kv)
    edge = move(edge, lambda i: (i + 1) % ctx_count)
    thirds = along(thirds, 1)
    cross = across(pick_cross(cross_steps, thirds))
    packed, edge, cross = lax.optimization_barrier((pack(main_index, kv), edge, cross))
    main = ctx_exchange(packed)
    far, third_grad = collect(request, my_third, near_steps, kv, qg, edge, cross, main, thirds)
    cross_grad = across(third_grad)
    out, sums, edge_grad, far_grad = attend(kv, qg, edge, far)
    out, cross_grad = lax.optimization_barrier((out, cross_grad))
    out = head_exchange(out)
    edge_grad = move(edge_grad, lambda i: (i - 1) % ctx_count)
    late = along(pick_back(near_steps, cross_steps, third_grad, cross_grad, lanes), -1)
    packed, out, edge_grad, late = lax.optimization_barrier(
        (pack(request, far_grad), out, edge_grad, late)
    )
    home = ctx_exchange(packed)
    attended, query_grad = join_heads(out)
    total = land(main_index, third_index, sums, edge_grad, home, late)
    key_grad, value_grad = join_heads(head_exchange(total))
    return attended, query_grad, key_grad, value_grad


def solution(mesh):
    tokens = P(("ctx", "head"), None)
    return jax.shard_map(
        body,
        mesh=mesh,
        in_specs=(tokens, tokens, tokens, tokens, P()),
        out_specs=(tokens, tokens, tokens, tokens),
        check_vma=False,
    )
```

```python
import functools

import jax
import jax.numpy as jnp
from jax import lax
from jax.experimental import pallas as pl
from jax.experimental.pallas import tpu as pltpu
from jax.sharding import PartitionSpec as P

HEAD_DIM = 128
BLOCK = 128
ANY = pl.BlockSpec(memory_space=pl.ANY)
VMEM = pl.BlockSpec(memory_space=pltpu.VMEM)
SMEM = pl.BlockSpec(memory_space=pltpu.SMEM)
FULL = 60 * 1024 * 1024


def call(kernel, out_shape, ins, outs, name, flops, nbytes, scratch=(), limit=50 * 1024 * 1024):
    return pl.pallas_call(
        kernel,
        out_shape=out_shape,
        in_specs=list(ins),
        out_specs=outs,
        scratch_shapes=list(scratch),
        compiler_params=pltpu.CompilerParams(vmem_limit_bytes=limit),
        cost_estimate=pl.CostEstimate(flops=flops, bytes_accessed=nbytes, transcendentals=0),
        name=name,
    )


def start_all(copies):
    for copy in copies:
        copy.start()


def wait_all(copies):
    for copy in copies:
        copy.wait()


def dot(a, b, dims):
    return lax.dot_general(a, b, (dims, ((), ())), preferred_element_type=jnp.float32)


def split_kernel(heads, count, *refs):
    arrays, out = refs[:count], refs[count]
    held, packed, sems, out_sems = refs[count + 1 :]
    reads = [pltpu.make_async_copy(arrays[w], held.at[w], sems.at[w]) for w in range(count)]
    writes = [
        pltpu.make_async_copy(packed.at[head], out.at[head], out_sems.at[head]) for head in range(heads)
    ]
    start_all(reads)
    wait_all(reads)
    for head in range(heads):
        for w in range(count):
            packed[head, w] = held[w, :, pl.ds(head * HEAD_DIM, HEAD_DIM)]
        writes[head].start()
    wait_all(writes)


def split_heads(*arrays):
    rows, features = arrays[0].shape
    heads, count = features // HEAD_DIM, len(arrays)
    dtype = arrays[0].dtype
    packed = (heads, count, rows, HEAD_DIM)
    return call(
        functools.partial(split_kernel, heads, count),
        pltpu.HBM(packed, dtype),
        [ANY] * count,
        ANY,
        "split_heads",
        0,
        4 * count * arrays[0].size,
        [
            pltpu.VMEM((count, rows, features), dtype),
            pltpu.VMEM(packed, dtype),
            pltpu.SemaphoreType.DMA((count,)),
            pltpu.SemaphoreType.DMA((heads,)),
        ],
        FULL,
    )(*arrays)


def join_kernel(heads, count, in_ref, *refs):
    outs = refs[:count]
    held, sems = refs[count:]
    writes = [pltpu.make_async_copy(held.at[w], outs[w], sems.at[w]) for w in range(count)]
    for w in range(count):
        for head in range(heads):
            held[w, :, pl.ds(head * HEAD_DIM, HEAD_DIM)] = in_ref[head, w]
        writes[w].start()
    wait_all(writes)


def join_heads(packed):
    heads, count, rows, depth = packed.shape
    features, dtype = heads * depth, packed.dtype
    return call(
        functools.partial(join_kernel, heads, count),
        (pltpu.HBM((rows, features), dtype),) * count,
        [VMEM],
        (ANY,) * count,
        "join_heads",
        0,
        4 * packed.size,
        [pltpu.VMEM((count, rows, features), dtype), pltpu.SemaphoreType.DMA((count,))],
    )(packed)


def pick_third_kernel(blocks, lanes, third_ref, kv_ref, *refs):
    thirds, edge_ref = refs[:lanes], refs[lanes]
    edge_ref[...] = kv_ref[blocks - 1]
    for step in range(lanes):
        for side in range(2):
            index = third_ref[2 * step + side]

            @pl.when(index >= 0)
            def _():
                thirds[step][side] = kv_ref[index]


def pick_third(index, kv):
    lanes = index.shape[0] // 2
    outs = call(
        functools.partial(pick_third_kernel, kv.shape[0], lanes),
        (jax.ShapeDtypeStruct((2,) + kv.shape[1:], kv.dtype),) * lanes
        + (jax.ShapeDtypeStruct(kv.shape[1:], kv.dtype),),
        [SMEM, VMEM],
        (VMEM,) * (lanes + 1),
        "pick_third",
        0,
        8 * kv[0].size,
    )(index, kv)
    return outs[:lanes], outs[lanes]


def pack_kernel(rows, limit, index_ref, in_ref, out, sems):
    copies = [
        pltpu.make_async_copy(in_ref.at[jnp.minimum(index_ref[i], limit)], out.at[i], sems.at[i])
        for i in range(rows)
    ]
    start_all(copies)
    wait_all(copies)


def pack(index, array):
    rows = index.shape[0]
    return call(
        functools.partial(pack_kernel, rows, array.shape[0] - 1),
        pltpu.HBM((rows,) + array.shape[1:], array.dtype),
        [SMEM, VMEM],
        ANY,
        "pack",
        0,
        4 * rows * array[0].size,
        [pltpu.SemaphoreType.DMA((rows,))],
    )(index, array)


def pick_cross_kernel(lanes, step_ref, *refs):
    ins, out_ref = refs[:lanes], refs[lanes]
    for j in range(2):
        for step in range(lanes):

            @pl.when(step_ref[j] == step)
            def _():
                out_ref[j] = ins[step][1]


def pick_cross(steps, thirds):
    lanes = len(thirds)
    return call(
        functools.partial(pick_cross_kernel, lanes),
        jax.ShapeDtypeStruct(thirds[0].shape, thirds[0].dtype),
        [SMEM] + [VMEM] * lanes,
        VMEM,
        "pick_cross",
        0,
        4 * thirds[0].size,
    )(steps, *thirds)


def attention(q, g, k, v):
    scale = HEAD_DIM ** (-0.5)
    s = dot(k, q, ((1,), (1,))) * scale
    dp = dot(v, g, ((1,), (1,)))
    w = jnp.exp(s - jnp.max(s, axis=0, keepdims=True))
    p = w * (1.0 / jnp.sum(w, axis=0, keepdims=True))
    p_low = p.astype(jnp.bfloat16)
    delta = jnp.sum(p_low.astype(jnp.float32) * dp, axis=0, keepdims=True)
    return p_low, (p * (dp - delta) * scale).astype(jnp.bfloat16)


def collect_kernel(
    lanes, slot_ref, third_ref, near_ref, kv, qg, edge, cross, main, *refs
):
    thirds, extra, grad_ref = refs[:lanes], refs[lanes], refs[lanes + 1]
    held, asked, sems, far_sems = refs[lanes + 2 :]
    for j in range(2):
        for step in range(1, lanes):

            @pl.when(near_ref[j] == step)
            def _():
                pltpu.make_async_copy(thirds[step].at[0], extra.at[j], far_sems.at[j]).start()

        @pl.when(near_ref[j] < 0)
        def _():
            pltpu.make_async_copy(cross.at[j], extra.at[j], far_sems.at[j]).start()

    for j in range(2):
        n = third_ref[j] // 2
        slot = slot_ref[n * 4 + 1 - third_ref[j]]
        pltpu.make_async_copy(kv.at[n], held.at[j, 0], sems.at[j, 0]).start()
        pltpu.make_async_copy(qg.at[n], asked.at[j], sems.at[j, 3]).start()

        @pl.when(n == 0)
        def _():
            pltpu.make_async_copy(edge, held.at[j, 1], sems.at[j, 1]).start()

        @pl.when(n > 0)
        def _():
            pltpu.make_async_copy(kv.at[n - 1], held.at[j, 1], sems.at[j, 1]).start()

        @pl.when(slot >= 0)
        def _():
            pltpu.make_async_copy(main.at[slot], held.at[j, 2], sems.at[j, 2]).start()

    for j in range(2):
        pltpu.make_async_copy(cross.at[j], extra.at[j], far_sems.at[j]).wait()
    for j in range(2):
        slot = slot_ref[third_ref[j] // 2 * 4 + 1 - third_ref[j]]

        @pl.when(slot < 0)
        def _():
            held[j, 2] = extra[1 - j]

        @pl.when(slot >= 0)
        def _():
            pltpu.make_async_copy(main.at[0], held.at[j, 2], sems.at[j, 2]).wait()

        for at in range(2):
            pltpu.make_async_copy(edge, held.at[j, at], sems.at[j, at]).wait()
        pltpu.make_async_copy(qg.at[0], asked.at[j], sems.at[j, 3]).wait()
        k, v = (
            jnp.concatenate([extra[j, w], held[j, 0, w], held[j, 1, w], held[j, 2, w]], axis=0)
            for w in range(2)
        )
        q, g = asked[j, 0], asked[j, 1]
        p_low, ds = attention(q, g, k, v)
        grad_ref[j, 0] = dot(ds[:BLOCK], q, ((1,), (0,))).astype(grad_ref.dtype)
        grad_ref[j, 1] = dot(p_low[:BLOCK], g, ((1,), (0,))).astype(grad_ref.dtype)


def collect(slot, third, near, kv, qg, edge, cross, main, thirds):
    lanes = len(thirds)
    pair = jax.ShapeDtypeStruct(cross.shape, cross.dtype)
    return call(
        functools.partial(collect_kernel, lanes),
        (pair, pair),
        [SMEM] * 3 + [ANY] * (5 + lanes),
        (VMEM, VMEM),
        "collect",
        5 * 2 * 2 * 4 * BLOCK * BLOCK * HEAD_DIM,
        20 * edge.size,
        [
            pltpu.VMEM((2, 3) + edge.shape, edge.dtype),
            pltpu.VMEM((2,) + edge.shape, edge.dtype),
            pltpu.SemaphoreType.DMA((2, 4)),
            pltpu.SemaphoreType.DMA((2,)),
        ],
    )(slot, third, near, kv, qg, edge, cross, main, *thirds)


def attend_kernel(blocks, slot_ref, third_ref, kv_ref, qg_ref, edge_ref, extra_ref, main, *refs):
    out, sums, edge_out, main_out = refs[:4]
    far_ref, out_ref, sum_ref, far_out, far_sems, done_sems, leave_sems = refs[4:]
    bf16 = jnp.bfloat16

    def arrive(r, slot):
        return pltpu.make_async_copy(main.at[slot], far_ref.at[r], far_sems.at[r])

    def finished(n):
        return pltpu.make_async_copy(out_ref.at[n], out.at[n], done_sems.at[0, n])

    def summed(n):
        return pltpu.make_async_copy(sum_ref.at[n], sums.at[n], done_sems.at[1, n])

    def leave(r, slot):
        return pltpu.make_async_copy(far_out.at[r], main_out.at[slot], leave_sems.at[r])

    def when_main(r, do):
        @pl.when(slot_ref[r] >= 0)
        def _():
            do(r, slot_ref[r])

    def load(r, _):
        when_main(r, lambda r, slot: arrive(r, slot).start())

    lax.fori_loop(0, 2 * blocks, load, None)
    for j in range(2):
        far_ref[third_ref[j]] = extra_ref[j]

    def ready(n):
        for r in (2 * n, 2 * n + 1):
            when_main(r, lambda r, slot: arrive(r, slot).wait())

    def one(n, first):
        q, g = qg_ref[n, 0], qg_ref[n, 1]
        r2, r3 = 2 * n, 2 * n + 1
        listed = []
        for which in range(2):
            before = edge_ref[which] if first else kv_ref[n - 1, which]
            listed.append(
                jnp.concatenate([kv_ref[n, which], before, far_ref[r2, which], far_ref[r3, which]], axis=0)
            )
        k, v = listed
        p_low, ds = attention(q, g, k, v)
        out_ref[n, 0] = dot(p_low, v, ((0,), (0,))).astype(bf16)
        out_ref[n, 1] = dot(ds, k, ((0,), (0,))).astype(bf16)
        dk = dot(ds, q, ((1,), (0,)))
        dv = dot(p_low, g, ((1,), (0,)))
        for which, d in enumerate((dk, dv)):
            sum_ref[n, which] = d[:BLOCK]
            if first:
                edge_out[which] = d[BLOCK : 2 * BLOCK].astype(bf16)
            else:
                sum_ref[n - 1, which] += d[BLOCK : 2 * BLOCK]
            far_out[r2, which] = d[2 * BLOCK : 3 * BLOCK].astype(bf16)
            far_out[r3, which] = d[3 * BLOCK :].astype(bf16)

    def sent(n, first):
        finished(n).start()
        if not first:
            summed(n - 1).start()
        for r in (2 * n, 2 * n + 1):
            when_main(r, lambda r, slot: leave(r, slot).start())

    group = 3
    ready(0)
    one(0, True)
    sent(0, True)

    def several(at, _):
        first = 1 + at * group
        for i in range(group):
            ready(first + i)
        for i in range(group):
            one(first + i, False)
        for i in range(group):
            sent(first + i, False)

    lax.fori_loop(0, (blocks - 1) // group, several, None)
    for n in range(1 + (blocks - 1) // group * group, blocks):
        ready(n)
        one(n, False)
        sent(n, False)
    summed(blocks - 1).start()

    def finish(n, _):
        finished(n).wait()
        summed(n).wait()
        for r in (2 * n, 2 * n + 1):
            when_main(r, lambda r, slot: leave(r, slot).wait())

    lax.fori_loop(0, blocks, finish, None)


def attend(slot, third, kv, qg, edge, extra, main):
    blocks = kv.shape[0]
    bf16, f32 = kv.dtype, jnp.float32
    far = (2 * blocks,) + kv.shape[1:]
    return call(
        functools.partial(attend_kernel, blocks),
        (
            pltpu.HBM(qg.shape, bf16),
            pltpu.HBM(kv.shape, f32),
            jax.ShapeDtypeStruct(edge.shape, bf16),
            pltpu.HBM(main.shape, bf16),
        ),
        [SMEM, SMEM, VMEM, VMEM, VMEM, VMEM, ANY],
        (ANY, ANY, VMEM, ANY),
        "attend",
        5 * 2 * blocks * 4 * BLOCK * BLOCK * HEAD_DIM,
        2 * (6 * kv.size + 2 * main.size),
        [
            pltpu.VMEM(far, bf16),
            pltpu.VMEM(qg.shape, bf16),
            pltpu.VMEM(kv.shape, f32),
            pltpu.VMEM(far, bf16),
            pltpu.SemaphoreType.DMA((2 * blocks,)),
            pltpu.SemaphoreType.DMA((2, blocks)),
            pltpu.SemaphoreType.DMA((2 * blocks,)),
        ],
    )(slot, third, kv, qg, edge, extra, main)


def land_kernel(blocks, slots, thirds, main_ref, late_ref, sum_ref, edge_ref, home_ref, late, out, *refs):
    total, held, low, sems, late_sems = refs
    f32 = jnp.float32

    def arrive(at):
        return pltpu.make_async_copy(late.at[at], held.at[at], late_sems.at[at])

    def load(at, _):
        @pl.when(late_ref[at] >= 0)
        def _():
            arrive(at).start()

    lax.fori_loop(0, thirds, load, None)
    total[pl.ds(0, blocks)] = sum_ref[...]
    total[blocks - 1] += edge_ref[...].astype(f32)
    for slot in range(slots):
        total[main_ref[slot]] += home_ref[slot].astype(f32)

    def add(at, _):
        @pl.when(late_ref[at] >= 0)
        def _():
            arrive(at).wait()
            total[late_ref[at]] += held[at].astype(f32)

    lax.fori_loop(0, thirds, add, None)
    writes = [pltpu.make_async_copy(low.at[n], out.at[n], sems.at[n]) for n in range(blocks)]
    for n in range(blocks):
        low[n] = total[n].astype(low.dtype)
        writes[n].start()
    wait_all(writes)


def land(main_index, late_index, sums, edge, home, late):
    blocks, slots, thirds = sums.shape[0], home.shape[0], late.shape[0]
    return call(
        functools.partial(land_kernel, blocks, slots, thirds),
        pltpu.HBM(sums.shape, home.dtype),
        [SMEM] * 2 + [VMEM] * 3 + [ANY],
        ANY,
        "land",
        sums.size * 2,
        10 * sums.size,
        [
            pltpu.VMEM((blocks + 1,) + sums.shape[1:], jnp.float32),
            pltpu.VMEM(late.shape, home.dtype),
            pltpu.VMEM(sums.shape, home.dtype),
            pltpu.SemaphoreType.DMA((blocks,)),
            pltpu.SemaphoreType.DMA((thirds,)),
        ],
    )(main_index, late_index, sums, edge, home, late)


def plan(key_lists, blocks, ctx_count, lanes):
    i32 = jnp.int32
    me = lax.axis_index("ctx")
    half, lane = me // lanes, me % lanes
    requests = 2 * blocks
    slabs = jnp.arange(ctx_count, dtype=i32)
    numbers = jnp.arange(requests, dtype=i32)
    far_all = key_lists[:, 2:].reshape(ctx_count, requests)
    source, inside = far_all // blocks, far_all % blocks
    earlier = (numbers[None, :] < numbers[:, None])[None]
    rank = jnp.sum(((source[:, None, :] == source[:, :, None]) & earlier).astype(i32), axis=2)
    is_third = rank == 2
    order = jnp.sum((is_third[:, None, :] & earlier).astype(i32), axis=2)
    pair = jnp.arange(2, dtype=i32)[None, :, None]

    wanted = (source[:, None, :] == me) & (rank[:, None, :] == pair)
    send_main = jnp.sum(jnp.where(wanted, inside[:, None, :], 0), axis=2)
    main_index = jnp.where(slabs[:, None] == me, blocks, send_main).reshape(-1)
    from_me = is_third & (source == me)
    third_of = jnp.sum(jnp.where(from_me, inside + 1, 0), axis=1) - 1

    step = jnp.arange(lanes, dtype=i32)[:, None]
    side = jnp.arange(2, dtype=i32)[None, :]
    third_asker = jnp.where(side == 0, half, 1 - half) * lanes + (lane + step) % lanes
    hit = third_asker[:, :, None] == slabs[None, None, :]
    third_index = jnp.sum(jnp.where(hit, third_of[None, None, :], 0), axis=2).reshape(-1)

    def row(of, array):
        return jnp.sum(jnp.where(slabs[:, None] == of, array, 0), axis=0)

    my_slot = row(me, jnp.where(is_third, -1, source * 2 + rank))
    is_jth = (is_third[:, None, :] & (order[:, None, :] == pair)).astype(i32)
    third_source = jnp.sum(is_jth * source[:, None, :], axis=2)
    third_request = jnp.sum(is_jth * numbers, axis=2)
    third_inside = jnp.sum(is_jth * inside[:, None, :], axis=2)
    mine = jnp.where(third_source == me, third_inside, -1).reshape(2, lanes, 2)
    near, far = jnp.where(half == 0, mine[0], mine[1]), jnp.where(half == 0, mine[1], mine[0])
    late_index = jnp.concatenate([near, far], axis=1).reshape(-1)

    def steps(of):
        slab = row(of, third_source)
        return jnp.where(slab // lanes == half, (lane - slab % lanes + lanes) % lanes, -1)

    partner = (me + lanes) % ctx_count
    return (
        main_index, third_index, late_index, my_slot, row(me, third_request), steps(me), steps(partner)
    )


def body(queries, keys, values, out_grad, key_lists):
    ctx_count = lax.axis_size("ctx")
    blocks = lax.axis_size("head")
    lanes = ctx_count // 2
    main_index, third_index, late_index, my_slot, my_third, near_steps, cross_steps = plan(
        key_lists, blocks, ctx_count, lanes
    )

    def head_exchange(array):
        return lax.all_to_all(array, "head", split_axis=0, concat_axis=0, tiled=True)

    def ctx_exchange(array):
        return lax.all_to_all(array, "ctx", split_axis=0, concat_axis=0, tiled=True)

    def move(array, target):
        return lax.ppermute(array, "ctx", [(i, target(i)) for i in range(ctx_count)])

    def across(array):
        return move(array, lambda i: (i + lanes) % ctx_count)

    def along(arrays, sign):
        def target(step):
            return lambda i: i // lanes * lanes + (i + sign * step) % lanes

        return [arrays[0]] + [move(arrays[s], target(s)) for s in range(1, lanes)]

    kv = head_exchange(split_heads(keys, values))
    qg = head_exchange(split_heads(queries, out_grad))
    thirds, edge = pick_third(third_index, kv)
    edge = move(edge, lambda i: (i + 1) % ctx_count)
    thirds = along(thirds, 1)
    thirds[1], edge = lax.optimization_barrier((thirds[1], edge))
    cross = across(pick_cross(cross_steps, thirds))
    packed, cross = lax.optimization_barrier((pack(main_index, kv), cross))
    main = ctx_exchange(packed)
    extra, third_grad = collect(my_slot, my_third, near_steps, kv, qg, edge, cross, main, thirds)
    cross_grad = across(third_grad)
    out, sums, edge_grad, main_grad = attend(my_slot, my_third, kv, qg, edge, extra, main)
    out, cross_grad = lax.optimization_barrier((out, cross_grad))
    late = lax.all_gather(
        jnp.concatenate([third_grad, cross_grad], axis=0),
        "ctx",
        axis_index_groups=[list(range(lanes)), list(range(lanes, ctx_count))],
        tiled=True,
    )
    out = head_exchange(out)
    edge_grad = move(edge_grad, lambda i: (i - 1) % ctx_count)
    main_grad, out, edge_grad, late = lax.optimization_barrier((main_grad, out, edge_grad, late))
    home = ctx_exchange(main_grad)
    attended, query_grad = join_heads(out)
    total = land(main_index, late_index, sums, edge_grad, home, late)
    key_grad, value_grad = join_heads(head_exchange(total))
    return attended, query_grad, key_grad, value_grad


def solution(mesh):
    tokens = P(("ctx", "head"), None)
    return jax.shard_map(
        body,
        mesh=mesh,
        in_specs=(tokens, tokens, tokens, tokens, P()),
        out_specs=(tokens, tokens, tokens, tokens),
        check_vma=False,
    )
```

```python
import functools

import jax
import jax.numpy as jnp
from jax import lax
from jax.experimental import pallas as pl
from jax.experimental.pallas import tpu as pltpu
from jax.sharding import PartitionSpec as P

HEAD_DIM = 128
BLOCK = 128
ANY = pl.BlockSpec(memory_space=pl.ANY)
VMEM = pl.BlockSpec(memory_space=pltpu.VMEM)
SMEM = pl.BlockSpec(memory_space=pltpu.SMEM)
FULL = 60 * 1024 * 1024


def call(kernel, out_shape, ins, outs, name, flops, nbytes, scratch=(), limit=51 * 1024 * 1024):
    return pl.pallas_call(
        kernel,
        out_shape=out_shape,
        in_specs=list(ins),
        out_specs=outs,
        scratch_shapes=list(scratch),
        compiler_params=pltpu.CompilerParams(vmem_limit_bytes=limit),
        cost_estimate=pl.CostEstimate(flops=flops, bytes_accessed=nbytes, transcendentals=0),
        name=name,
    )


def start_all(copies):
    for copy in copies:
        copy.start()


def wait_all(copies):
    for copy in copies:
        copy.wait()


def dot(a, b, dims):
    return lax.dot_general(a, b, (dims, ((), ())), preferred_element_type=jnp.float32)


def split_kernel(heads, count, *refs):
    arrays, out = refs[:count], refs[count]
    held, packed, sems, out_sems = refs[count + 1 :]
    reads = [pltpu.make_async_copy(arrays[w], held.at[w], sems.at[w]) for w in range(count)]
    writes = [
        pltpu.make_async_copy(packed.at[head], out.at[head], out_sems.at[head]) for head in range(heads)
    ]
    start_all(reads)
    wait_all(reads)
    for head in range(heads):
        for w in range(count):
            packed[head, w] = held[w, :, pl.ds(head * HEAD_DIM, HEAD_DIM)]
        writes[head].start()
    wait_all(writes)


def split_heads(*arrays):
    rows, features = arrays[0].shape
    heads, count = features // HEAD_DIM, len(arrays)
    dtype = arrays[0].dtype
    packed = (heads, count, rows, HEAD_DIM)
    return call(
        functools.partial(split_kernel, heads, count),
        pltpu.HBM(packed, dtype),
        [ANY] * count,
        ANY,
        "split_heads",
        0,
        4 * count * arrays[0].size,
        [
            pltpu.VMEM((count, rows, features), dtype),
            pltpu.VMEM(packed, dtype),
            pltpu.SemaphoreType.DMA((count,)),
            pltpu.SemaphoreType.DMA((heads,)),
        ],
        FULL,
    )(*arrays)


def join_kernel(heads, count, in_ref, *refs):
    outs = refs[:count]
    held, sems = refs[count:]
    writes = [pltpu.make_async_copy(held.at[w], outs[w], sems.at[w]) for w in range(count)]
    for w in range(count):
        for head in range(heads):
            held[w, :, pl.ds(head * HEAD_DIM, HEAD_DIM)] = in_ref[head, w]
        writes[w].start()
    wait_all(writes)


def join_heads(packed):
    heads, count, rows, depth = packed.shape
    features, dtype = heads * depth, packed.dtype
    return call(
        functools.partial(join_kernel, heads, count),
        (pltpu.HBM((rows, features), dtype),) * count,
        [VMEM],
        (ANY,) * count,
        "join_heads",
        0,
        4 * packed.size,
        [pltpu.VMEM((count, rows, features), dtype), pltpu.SemaphoreType.DMA((count,))],
    )(packed)


def pick_third_kernel(blocks, lanes, third_ref, kv_ref, *refs):
    thirds, edge_ref = refs[:lanes], refs[lanes]
    edge_ref[...] = kv_ref[blocks - 1]
    for step in range(lanes):
        for side in range(2):
            index = third_ref[2 * step + side]

            @pl.when(index >= 0)
            def _():
                thirds[step][side] = kv_ref[index]


def pick_third(index, kv):
    lanes = index.shape[0] // 2
    outs = call(
        functools.partial(pick_third_kernel, kv.shape[0], lanes),
        (jax.ShapeDtypeStruct((2,) + kv.shape[1:], kv.dtype),) * lanes
        + (jax.ShapeDtypeStruct(kv.shape[1:], kv.dtype),),
        [SMEM, VMEM],
        (VMEM,) * (lanes + 1),
        "pick_third",
        0,
        8 * kv[0].size,
    )(index, kv)
    return outs[:lanes], outs[lanes]


def pack_kernel(rows, limit, index_ref, in_ref, out, sems):
    copies = [
        pltpu.make_async_copy(in_ref.at[jnp.minimum(index_ref[i], limit)], out.at[i], sems.at[i])
        for i in range(rows)
    ]
    start_all(copies)
    wait_all(copies)


def pack(index, array):
    rows = index.shape[0]
    return call(
        functools.partial(pack_kernel, rows, array.shape[0] - 1),
        pltpu.HBM((rows,) + array.shape[1:], array.dtype),
        [SMEM, VMEM],
        ANY,
        "pack",
        0,
        4 * rows * array[0].size,
        [pltpu.SemaphoreType.DMA((rows,))],
    )(index, array)


def pick_cross_kernel(lanes, step_ref, *refs):
    ins, out_ref = refs[:lanes], refs[lanes]
    for j in range(2):
        for step in range(lanes):

            @pl.when(step_ref[j] == step)
            def _():
                out_ref[j] = ins[step][1]


def pick_cross(steps, thirds):
    lanes = len(thirds)
    return call(
        functools.partial(pick_cross_kernel, lanes),
        jax.ShapeDtypeStruct(thirds[0].shape, thirds[0].dtype),
        [SMEM] + [VMEM] * lanes,
        VMEM,
        "pick_cross",
        0,
        4 * thirds[0].size,
    )(steps, *thirds)


def pick_back_kernel(lanes, near_ref, cross_ref, own, crossed, *outs):
    for j in range(2):
        for step in range(lanes):

            @pl.when(near_ref[j] == step)
            def _():
                outs[step][0] = own[j]

            @pl.when(cross_ref[j] == step)
            def _():
                outs[step][1] = crossed[j]


def pick_back(near_steps, cross_steps, own, crossed, lanes):
    return call(
        functools.partial(pick_back_kernel, lanes),
        (jax.ShapeDtypeStruct(own.shape, own.dtype),) * lanes,
        [SMEM, SMEM, VMEM, VMEM],
        (VMEM,) * lanes,
        "pick_back",
        0,
        8 * own.size,
    )(near_steps, cross_steps, own, crossed)


def attention(q, g, k, v):
    scale = HEAD_DIM ** (-0.5)
    s = dot(k, q, ((1,), (1,))) * scale
    dp = dot(v, g, ((1,), (1,)))
    w = jnp.exp(s - jnp.max(s, axis=0, keepdims=True))
    p = w * (1.0 / jnp.sum(w, axis=0, keepdims=True))
    p_low = p.astype(jnp.bfloat16)
    delta = jnp.sum(p_low.astype(jnp.float32) * dp, axis=0, keepdims=True)
    return p_low, (p * (dp - delta) * scale).astype(jnp.bfloat16)


def attend_kernel(
    blocks, lanes, slot_ref, third_ref, near_ref, kv_ref, qg_ref, edge_ref, cross, main, *refs
):
    thirds = refs[:lanes]
    out, sums, edge_out, main_out, third_out = refs[lanes : lanes + 5]
    far_ref, out_ref, sum_ref, far_out, far_sems, done_sems, leave_sems = refs[lanes + 5 :]
    bf16 = jnp.bfloat16

    def arrive(r, slot):
        return pltpu.make_async_copy(main.at[slot], far_ref.at[r], far_sems.at[r])

    def finished(n):
        return pltpu.make_async_copy(out_ref.at[n], out.at[n], done_sems.at[0, n])

    def summed(n):
        return pltpu.make_async_copy(sum_ref.at[n], sums.at[n], done_sems.at[1, n])

    def leave(r, slot):
        return pltpu.make_async_copy(far_out.at[r], main_out.at[slot], leave_sems.at[r])

    def when_main(r, do):
        @pl.when(slot_ref[r] >= 0)
        def _():
            do(r, slot_ref[r])

    def load(r, _):
        when_main(r, lambda r, slot: arrive(r, slot).start())

    lax.fori_loop(0, 2 * blocks, load, None)
    for j in range(2):
        r = third_ref[j]
        for step in range(1, lanes):

            @pl.when(near_ref[j] == step)
            def _():
                pltpu.make_async_copy(thirds[step].at[0], far_ref.at[r], far_sems.at[r]).start()

        @pl.when(near_ref[j] < 0)
        def _():
            pltpu.make_async_copy(cross.at[j], far_ref.at[r], far_sems.at[r]).start()

    def ready(n):
        for r in (2 * n, 2 * n + 1):
            arrive(r, 0).wait()

    def one(n, first):
        q, g = qg_ref[n, 0], qg_ref[n, 1]
        r2, r3 = 2 * n, 2 * n + 1
        listed = []
        for which in range(2):
            before = edge_ref[which] if first else kv_ref[n - 1, which]
            listed.append(
                jnp.concatenate([kv_ref[n, which], before, far_ref[r2, which], far_ref[r3, which]], axis=0)
            )
        k, v = listed
        p_low, ds = attention(q, g, k, v)
        out_ref[n, 0] = dot(p_low, v, ((0,), (0,))).astype(bf16)
        out_ref[n, 1] = dot(ds, k, ((0,), (0,))).astype(bf16)
        dk = dot(ds, q, ((1,), (0,)))
        dv = dot(p_low, g, ((1,), (0,)))
        for which, d in enumerate((dk, dv)):
            sum_ref[n, which] = d[:BLOCK]
            if first:
                edge_out[which] = d[BLOCK : 2 * BLOCK].astype(bf16)
            else:
                sum_ref[n - 1, which] += d[BLOCK : 2 * BLOCK]
            far_out[r2, which] = d[2 * BLOCK : 3 * BLOCK].astype(bf16)
            far_out[r3, which] = d[3 * BLOCK :].astype(bf16)

    def sent(n, first):
        finished(n).start()
        if not first:
            summed(n - 1).start()
        for r in (2 * n, 2 * n + 1):
            when_main(r, lambda r, slot: leave(r, slot).start())

    group = 3
    ready(0)
    one(0, True)
    sent(0, True)

    def several(at, _):
        first = 1 + at * group
        for i in range(group):
            ready(first + i)
        for i in range(group):
            one(first + i, False)
        for i in range(group):
            sent(first + i, False)

    lax.fori_loop(0, (blocks - 1) // group, several, None)
    for n in range(1 + (blocks - 1) // group * group, blocks):
        ready(n)
        one(n, False)
        sent(n, False)
    summed(blocks - 1).start()
    for j in range(2):
        third_out[j] = far_out[third_ref[j]]

    def finish(n, _):
        finished(n).wait()
        summed(n).wait()
        for r in (2 * n, 2 * n + 1):
            when_main(r, lambda r, slot: leave(r, slot).wait())

    lax.fori_loop(0, blocks, finish, None)


def attend(slot, third, near, kv, qg, edge, cross, main, thirds):
    blocks, lanes = kv.shape[0], len(thirds)
    bf16, f32 = kv.dtype, jnp.float32
    far = (2 * blocks,) + kv.shape[1:]
    return call(
        functools.partial(attend_kernel, blocks, lanes),
        (
            pltpu.HBM(qg.shape, bf16),
            pltpu.HBM(kv.shape, f32),
            jax.ShapeDtypeStruct(edge.shape, bf16),
            pltpu.HBM(main.shape, bf16),
            jax.ShapeDtypeStruct(cross.shape, bf16),
        ),
        [SMEM] * 3 + [VMEM] * 3 + [ANY] * (2 + lanes),
        (ANY, ANY, VMEM, ANY, VMEM),
        "attend",
        5 * 2 * blocks * 4 * BLOCK * BLOCK * HEAD_DIM,
        2 * (6 * kv.size + 2 * main.size),
        [
            pltpu.VMEM(far, bf16),
            pltpu.VMEM(qg.shape, bf16),
            pltpu.VMEM(kv.shape, f32),
            pltpu.VMEM(far, bf16),
            pltpu.SemaphoreType.DMA((2 * blocks,)),
            pltpu.SemaphoreType.DMA((2, blocks)),
            pltpu.SemaphoreType.DMA((2 * blocks,)),
        ],
    )(slot, third, near, kv, qg, edge, cross, main, *thirds)


def land_kernel(
    blocks, lanes, slots, main_ref, third_ref, sum_ref, edge_ref, home_ref, *refs
):
    thirds, out = refs[:lanes], refs[lanes]
    total, low, sems = refs[lanes + 1 :]
    f32 = jnp.float32
    total[pl.ds(0, blocks)] = sum_ref[...]
    total[blocks - 1] += edge_ref[...].astype(f32)
    for step in range(lanes):
        for side in range(2):
            index = third_ref[2 * step + side]

            @pl.when(index >= 0)
            def _():
                total[index] += thirds[step][side].astype(f32)

    for slot in range(slots):
        total[main_ref[slot]] += home_ref[slot].astype(f32)
    writes = [pltpu.make_async_copy(low.at[n], out.at[n], sems.at[n]) for n in range(blocks)]
    for n in range(blocks):
        low[n] = total[n].astype(low.dtype)
        writes[n].start()
    wait_all(writes)


def land(main_index, third_index, sums, edge, home, thirds):
    blocks, lanes, slots = sums.shape[0], len(thirds), home.shape[0]
    return call(
        functools.partial(land_kernel, blocks, lanes, slots),
        pltpu.HBM(sums.shape, home.dtype),
        [SMEM] * 2 + [VMEM] * (3 + lanes),
        ANY,
        "land",
        sums.size * 2,
        10 * sums.size,
        [
            pltpu.VMEM((blocks + 1,) + sums.shape[1:], jnp.float32),
            pltpu.VMEM(sums.shape, home.dtype),
            pltpu.SemaphoreType.DMA((blocks,)),
        ],
    )(main_index, third_index, sums, edge, home, *thirds)


def plan(key_lists, blocks, ctx_count, lanes):
    i32 = jnp.int32
    me = lax.axis_index("ctx")
    half, lane = me // lanes, me % lanes
    requests = 2 * blocks
    slabs = jnp.arange(ctx_count, dtype=i32)
    numbers = jnp.arange(requests, dtype=i32)
    far_all = key_lists[:, 2:].reshape(ctx_count, requests)
    source, inside = far_all // blocks, far_all % blocks
    earlier = (numbers[None, :] < numbers[:, None])[None]
    rank = jnp.sum(((source[:, None, :] == source[:, :, None]) & earlier).astype(i32), axis=2)
    is_third = rank == 2
    order = jnp.sum((is_third[:, None, :] & earlier).astype(i32), axis=2)
    pair = jnp.arange(2, dtype=i32)[None, :, None]

    wanted = (source[:, None, :] == me) & (rank[:, None, :] == pair)
    send_main = jnp.sum(jnp.where(wanted, inside[:, None, :], 0), axis=2)
    main_index = jnp.where(slabs[:, None] == me, blocks, send_main).reshape(-1)
    from_me = is_third & (source == me)
    third_of = jnp.sum(jnp.where(from_me, inside + 1, 0), axis=1) - 1

    step = jnp.arange(lanes, dtype=i32)[:, None]
    side = jnp.arange(2, dtype=i32)[None, :]
    third_asker = jnp.where(side == 0, half, 1 - half) * lanes + (lane + step) % lanes
    hit = third_asker[:, :, None] == slabs[None, None, :]
    third_index = jnp.sum(jnp.where(hit, third_of[None, None, :], 0), axis=2).reshape(-1)

    def row(of, array):
        return jnp.sum(jnp.where(slabs[:, None] == of, array, 0), axis=0)

    my_slot = row(me, jnp.where(is_third, -1, source * 2 + rank))
    is_jth = (is_third[:, None, :] & (order[:, None, :] == pair)).astype(i32)
    third_source = jnp.sum(is_jth * source[:, None, :], axis=2)
    third_request = jnp.sum(is_jth * numbers, axis=2)

    def steps(of):
        slab = row(of, third_source)
        return jnp.where(slab // lanes == half, (lane - slab % lanes + lanes) % lanes, -1)

    partner = (me + lanes) % ctx_count
    return main_index, third_index, my_slot, row(me, third_request), steps(me), steps(partner)


def body(queries, keys, values, out_grad, key_lists):
    ctx_count = lax.axis_size("ctx")
    blocks = lax.axis_size("head")
    lanes = ctx_count // 2
    main_index, third_index, my_slot, my_third, near_steps, cross_steps = plan(
        key_lists, blocks, ctx_count, lanes
    )

    def head_exchange(array):
        return lax.all_to_all(array, "head", split_axis=0, concat_axis=0, tiled=True)

    def ctx_exchange(array):
        return lax.all_to_all(array, "ctx", split_axis=0, concat_axis=0, tiled=True)

    def move(array, target):
        return lax.ppermute(array, "ctx", [(i, target(i)) for i in range(ctx_count)])

    def across(array):
        return move(array, lambda i: (i + lanes) % ctx_count)

    def along(arrays, sign):
        def target(step):
            return lambda i: i // lanes * lanes + (i + sign * step) % lanes

        return [arrays[0]] + [move(arrays[s], target(s)) for s in range(1, lanes)]

    kv = head_exchange(split_heads(keys, values))
    qg = head_exchange(split_heads(queries, out_grad))
    thirds, edge = pick_third(third_index, kv)
    edge = move(edge, lambda i: (i + 1) % ctx_count)
    thirds = along(thirds, 1)
    thirds[1], packed = lax.optimization_barrier((thirds[1], pack(main_index, kv)))
    cross = across(pick_cross(cross_steps, thirds))
    packed, edge, cross = lax.optimization_barrier((packed, edge, cross))
    main = ctx_exchange(packed)
    out, sums, edge_grad, main_grad, third_grad = attend(
        my_slot, my_third, near_steps, kv, qg, edge, cross, main, thirds
    )
    out = head_exchange(out)
    cross_grad = across(third_grad)
    edge_grad = move(edge_grad, lambda i: (i - 1) % ctx_count)
    main_grad, out, cross_grad, edge_grad = lax.optimization_barrier(
        (main_grad, out, cross_grad, edge_grad)
    )
    home = ctx_exchange(main_grad)
    late = along(pick_back(near_steps, cross_steps, third_grad, cross_grad, lanes), -1)
    attended, query_grad = join_heads(out)
    total = land(main_index, third_index, sums, edge_grad, home, late)
    key_grad, value_grad = join_heads(head_exchange(total))
    return attended, query_grad, key_grad, value_grad


def solution(mesh):
    tokens = P(("ctx", "head"), None)
    return jax.shard_map(
        body,
        mesh=mesh,
        in_specs=(tokens, tokens, tokens, tokens, P()),
        out_specs=(tokens, tokens, tokens, tokens),
        check_vma=False,
    )
```

```python
import functools

import jax
import jax.numpy as jnp
from jax import lax
from jax.experimental import pallas as pl
from jax.experimental.pallas import tpu as pltpu
from jax.sharding import PartitionSpec as P

HEAD_DIM = 128
BLOCK = 128
ANY = pl.BlockSpec(memory_space=pl.ANY)
VMEM = pl.BlockSpec(memory_space=pltpu.VMEM)
SMEM = pl.BlockSpec(memory_space=pltpu.SMEM)
FULL = 60 * 1024 * 1024


def call(kernel, out_shape, ins, outs, name, flops, nbytes, scratch=(), limit=51 * 1024 * 1024):
    return pl.pallas_call(
        kernel,
        out_shape=out_shape,
        in_specs=list(ins),
        out_specs=outs,
        scratch_shapes=list(scratch),
        compiler_params=pltpu.CompilerParams(vmem_limit_bytes=limit),
        cost_estimate=pl.CostEstimate(flops=flops, bytes_accessed=nbytes, transcendentals=0),
        name=name,
    )


def start_all(copies):
    for copy in copies:
        copy.start()


def wait_all(copies):
    for copy in copies:
        copy.wait()


def dot(a, b, dims):
    return lax.dot_general(a, b, (dims, ((), ())), preferred_element_type=jnp.float32)


def split_kernel(heads, count, *refs):
    arrays, out = refs[:count], refs[count]
    held, packed, sems, out_sems = refs[count + 1 :]
    reads = [pltpu.make_async_copy(arrays[w], held.at[w], sems.at[w]) for w in range(count)]
    writes = [
        pltpu.make_async_copy(packed.at[head], out.at[head], out_sems.at[head]) for head in range(heads)
    ]
    start_all(reads)
    wait_all(reads)
    for head in range(heads):
        for w in range(count):
            packed[head, w] = held[w, :, pl.ds(head * HEAD_DIM, HEAD_DIM)]
        writes[head].start()
    wait_all(writes)


def split_heads(*arrays):
    rows, features = arrays[0].shape
    heads, count = features // HEAD_DIM, len(arrays)
    dtype = arrays[0].dtype
    packed = (heads, count, rows, HEAD_DIM)
    return call(
        functools.partial(split_kernel, heads, count),
        pltpu.HBM(packed, dtype),
        [ANY] * count,
        ANY,
        "split_heads",
        0,
        4 * count * arrays[0].size,
        [
            pltpu.VMEM((count, rows, features), dtype),
            pltpu.VMEM(packed, dtype),
            pltpu.SemaphoreType.DMA((count,)),
            pltpu.SemaphoreType.DMA((heads,)),
        ],
        FULL,
    )(*arrays)


def join_kernel(heads, count, in_ref, *refs):
    outs = refs[:count]
    held, sems = refs[count:]
    writes = [pltpu.make_async_copy(held.at[w], outs[w], sems.at[w]) for w in range(count)]
    for w in range(count):
        for head in range(heads):
            held[w, :, pl.ds(head * HEAD_DIM, HEAD_DIM)] = in_ref[head, w]
        writes[w].start()
    wait_all(writes)


def join_heads(packed):
    heads, count, rows, depth = packed.shape
    features, dtype = heads * depth, packed.dtype
    return call(
        functools.partial(join_kernel, heads, count),
        (pltpu.HBM((rows, features), dtype),) * count,
        [VMEM],
        (ANY,) * count,
        "join_heads",
        0,
        4 * packed.size,
        [pltpu.VMEM((count, rows, features), dtype), pltpu.SemaphoreType.DMA((count,))],
    )(packed)


def pick_third_kernel(blocks, lanes, third_ref, kv_ref, *refs):
    thirds, edge_ref = refs[:lanes], refs[lanes]
    edge_ref[...] = kv_ref[blocks - 1]
    for step in range(lanes):
        for side in range(2):
            index = third_ref[2 * step + side]

            @pl.when(index >= 0)
            def _():
                thirds[step][side] = kv_ref[index]


def pick_third(index, kv):
    lanes = index.shape[0] // 2
    outs = call(
        functools.partial(pick_third_kernel, kv.shape[0], lanes),
        (jax.ShapeDtypeStruct((2,) + kv.shape[1:], kv.dtype),) * lanes
        + (jax.ShapeDtypeStruct(kv.shape[1:], kv.dtype),),
        [SMEM, VMEM],
        (VMEM,) * (lanes + 1),
        "pick_third",
        0,
        8 * kv[0].size,
    )(index, kv)
    return outs[:lanes], outs[lanes]


def pack_kernel(rows, limit, index_ref, in_ref, out, sems):
    copies = [
        pltpu.make_async_copy(in_ref.at[jnp.minimum(index_ref[i], limit)], out.at[i], sems.at[i])
        for i in range(rows)
    ]
    start_all(copies)
    wait_all(copies)


def pack(index, array):
    rows = index.shape[0]
    return call(
        functools.partial(pack_kernel, rows, array.shape[0] - 1),
        pltpu.HBM((rows,) + array.shape[1:], array.dtype),
        [SMEM, VMEM],
        ANY,
        "pack",
        0,
        4 * rows * array[0].size,
        [pltpu.SemaphoreType.DMA((rows,))],
    )(index, array)


def pick_cross_kernel(lanes, step_ref, *refs):
    ins, out_ref = refs[:lanes], refs[lanes]
    for j in range(2):
        for step in range(lanes):

            @pl.when(step_ref[j] == step)
            def _():
                out_ref[j] = ins[step][1]


def pick_cross(steps, thirds):
    lanes = len(thirds)
    return call(
        functools.partial(pick_cross_kernel, lanes),
        jax.ShapeDtypeStruct(thirds[0].shape, thirds[0].dtype),
        [SMEM] + [VMEM] * lanes,
        VMEM,
        "pick_cross",
        0,
        4 * thirds[0].size,
    )(steps, *thirds)


def pick_back_kernel(lanes, near_ref, cross_ref, own, crossed, *outs):
    for j in range(2):
        for step in range(lanes):

            @pl.when(near_ref[j] == step)
            def _():
                outs[step][0] = own[j]

            @pl.when(cross_ref[j] == step)
            def _():
                outs[step][1] = crossed[j]


def pick_back(near_steps, cross_steps, own, crossed, lanes):
    return call(
        functools.partial(pick_back_kernel, lanes),
        (jax.ShapeDtypeStruct(own.shape, own.dtype),) * lanes,
        [SMEM, SMEM, VMEM, VMEM],
        (VMEM,) * lanes,
        "pick_back",
        0,
        8 * own.size,
    )(near_steps, cross_steps, own, crossed)


def attention(q, g, k, v):
    scale = HEAD_DIM ** (-0.5)
    s = dot(k, q, ((1,), (1,))) * scale
    dp = dot(v, g, ((1,), (1,)))
    w = jnp.exp(s - jnp.max(s, axis=0, keepdims=True))
    p = w * (1.0 / jnp.sum(w, axis=0, keepdims=True))
    p_low = p.astype(jnp.bfloat16)
    delta = jnp.sum(p_low.astype(jnp.float32) * dp, axis=0, keepdims=True)
    return p_low, (p * (dp - delta) * scale).astype(jnp.bfloat16)


def attend_kernel(
    blocks, lanes, slot_ref, third_ref, near_ref, kv_ref, qg_ref, edge_ref, cross, main, *refs
):
    thirds = refs[:lanes]
    out, sums, edge_out, main_out, third_out = refs[lanes : lanes + 5]
    far_ref, out_ref, sum_ref, far_out, far_sems, done_sems, leave_sems = refs[lanes + 5 :]
    bf16 = jnp.bfloat16

    def arrive(r, slot):
        return pltpu.make_async_copy(main.at[slot], far_ref.at[r], far_sems.at[r])

    def finished(n):
        return pltpu.make_async_copy(out_ref.at[n], out.at[n], done_sems.at[0, n])

    def summed(n):
        return pltpu.make_async_copy(sum_ref.at[n], sums.at[n], done_sems.at[1, n])

    def leave(r, slot):
        return pltpu.make_async_copy(far_out.at[r], main_out.at[slot], leave_sems.at[r])

    def when_main(r, do):
        @pl.when(slot_ref[r] >= 0)
        def _():
            do(r, slot_ref[r])

    def load(r, _):
        when_main(r, lambda r, slot: arrive(r, slot).start())

    lax.fori_loop(0, 2 * blocks, load, None)
    for j in range(2):
        r = third_ref[j]
        for step in range(1, lanes):

            @pl.when(near_ref[j] == step)
            def _():
                pltpu.make_async_copy(thirds[step].at[0], far_ref.at[r], far_sems.at[r]).start()

        @pl.when(near_ref[j] < 0)
        def _():
            pltpu.make_async_copy(cross.at[j], far_ref.at[r], far_sems.at[r]).start()

    def ready(n):
        for r in (2 * n, 2 * n + 1):
            arrive(r, 0).wait()

    def one(n, first):
        q, g = qg_ref[n, 0], qg_ref[n, 1]
        r2, r3 = 2 * n, 2 * n + 1
        listed = []
        for which in range(2):
            before = edge_ref[which] if first else kv_ref[n - 1, which]
            listed.append(
                jnp.concatenate([kv_ref[n, which], before, far_ref[r2, which], far_ref[r3, which]], axis=0)
            )
        k, v = listed
        p_low, ds = attention(q, g, k, v)
        out_ref[n, 0] = dot(p_low, v, ((0,), (0,))).astype(bf16)
        out_ref[n, 1] = dot(ds, k, ((0,), (0,))).astype(bf16)
        dk = dot(ds, q, ((1,), (0,)))
        dv = dot(p_low, g, ((1,), (0,)))
        for which, d in enumerate((dk, dv)):
            sum_ref[n, which] = d[:BLOCK]
            if first:
                edge_out[which] = d[BLOCK : 2 * BLOCK].astype(bf16)
            else:
                sum_ref[n - 1, which] += d[BLOCK : 2 * BLOCK]
            far_out[r2, which] = d[2 * BLOCK : 3 * BLOCK].astype(bf16)
            far_out[r3, which] = d[3 * BLOCK :].astype(bf16)

    def sent(n, first):
        finished(n).start()
        if not first:
            summed(n - 1).start()
        for r in (2 * n, 2 * n + 1):
            when_main(r, lambda r, slot: leave(r, slot).start())

    group = 3
    ready(0)
    one(0, True)
    sent(0, True)

    def several(at, _):
        first = 1 + at * group
        for i in range(group):
            ready(first + i)
        for i in range(group):
            one(first + i, False)
        for i in range(group):
            sent(first + i, False)

    lax.fori_loop(0, (blocks - 1) // group, several, None)
    for n in range(1 + (blocks - 1) // group * group, blocks):
        ready(n)
        one(n, False)
        sent(n, False)
    summed(blocks - 1).start()
    for j in range(2):
        third_out[j] = far_out[third_ref[j]]

    def finish(n, _):
        finished(n).wait()
        summed(n).wait()
        for r in (2 * n, 2 * n + 1):
            when_main(r, lambda r, slot: leave(r, slot).wait())

    lax.fori_loop(0, blocks, finish, None)


def attend(slot, third, near, kv, qg, edge, cross, main, thirds):
    blocks, lanes = kv.shape[0], len(thirds)
    bf16, f32 = kv.dtype, jnp.float32
    far = (2 * blocks,) + kv.shape[1:]
    return call(
        functools.partial(attend_kernel, blocks, lanes),
        (
            pltpu.HBM(qg.shape, bf16),
            pltpu.HBM(kv.shape, f32),
            jax.ShapeDtypeStruct(edge.shape, bf16),
            pltpu.HBM(main.shape, bf16),
            jax.ShapeDtypeStruct(cross.shape, bf16),
        ),
        [SMEM] * 3 + [VMEM] * 3 + [ANY] * (2 + lanes),
        (ANY, ANY, VMEM, ANY, VMEM),
        "attend",
        5 * 2 * blocks * 4 * BLOCK * BLOCK * HEAD_DIM,
        2 * (6 * kv.size + 2 * main.size),
        [
            pltpu.VMEM(far, bf16),
            pltpu.VMEM(qg.shape, bf16),
            pltpu.VMEM(kv.shape, f32),
            pltpu.VMEM(far, bf16),
            pltpu.SemaphoreType.DMA((2 * blocks,)),
            pltpu.SemaphoreType.DMA((2, blocks)),
            pltpu.SemaphoreType.DMA((2 * blocks,)),
        ],
    )(slot, third, near, kv, qg, edge, cross, main, *thirds)


def land_kernel(blocks, slots, main_ref, sum_ref, edge_ref, home_ref, total):
    f32 = jnp.float32
    total[...] = sum_ref[...]
    total[blocks - 1] += edge_ref[...].astype(f32)
    for slot in range(slots):
        row = main_ref[slot]

        @pl.when(row < blocks)
        def _():
            total[row] += home_ref[slot].astype(f32)


def land(main_index, sums, edge, home):
    blocks, slots = sums.shape[0], home.shape[0]
    return call(
        functools.partial(land_kernel, blocks, slots),
        jax.ShapeDtypeStruct(sums.shape, jnp.float32),
        [SMEM] + [VMEM] * 3,
        VMEM,
        "land",
        sums.size * 2,
        12 * sums.size,
    )(main_index, sums, edge, home)


def land_thirds_kernel(blocks, lanes, third_ref, total, *refs):
    thirds, out = refs[:lanes], refs[lanes]
    held, low, in_sems, sems, late, late_sems = refs[lanes + 1 :]
    reads = [pltpu.make_async_copy(total.at[n], held.at[n], in_sems.at[n]) for n in range(blocks)]
    writes = [pltpu.make_async_copy(low.at[n], out.at[n], sems.at[n]) for n in range(blocks)]
    start_all(reads)

    def arrive(at):
        step, side = divmod(at, 2)
        return pltpu.make_async_copy(thirds[step].at[side], late.at[at], late_sems.at[at])

    for at in range(2 * lanes):

        @pl.when(third_ref[at] >= 0)
        def _():
            arrive(at).start()

    wait_all(reads)
    for at in range(2 * lanes):

        @pl.when(third_ref[at] >= 0)
        def _():
            arrive(at).wait()
            held[third_ref[at]] += late[at].astype(jnp.float32)

    for n in range(blocks):
        low[n] = held[n].astype(low.dtype)
        writes[n].start()
    wait_all(writes)


def land_thirds(third_index, total, thirds):
    blocks, lanes = total.shape[0], len(thirds)
    dtype = thirds[0].dtype
    return call(
        functools.partial(land_thirds_kernel, blocks, lanes),
        pltpu.HBM(total.shape, dtype),
        [SMEM] + [ANY] * (1 + lanes),
        ANY,
        "land_thirds",
        total.size,
        6 * total.size,
        [
            pltpu.VMEM(total.shape, jnp.float32),
            pltpu.VMEM(total.shape, dtype),
            pltpu.SemaphoreType.DMA((blocks,)),
            pltpu.SemaphoreType.DMA((blocks,)),
            pltpu.VMEM((2 * lanes,) + total.shape[1:], dtype),
            pltpu.SemaphoreType.DMA((2 * lanes,)),
        ],
    )(third_index, total, *thirds)


def plan(key_lists, blocks, ctx_count, lanes):
    i32 = jnp.int32
    me = lax.axis_index("ctx")
    half, lane = me // lanes, me % lanes
    requests = 2 * blocks
    slabs = jnp.arange(ctx_count, dtype=i32)
    numbers = jnp.arange(requests, dtype=i32)
    far_all = key_lists[:, 2:].reshape(ctx_count, requests)
    source, inside = far_all // blocks, far_all % blocks
    earlier = (numbers[None, :] < numbers[:, None])[None]
    rank = jnp.sum(((source[:, None, :] == source[:, :, None]) & earlier).astype(i32), axis=2)
    is_third = rank == 2
    order = jnp.sum((is_third[:, None, :] & earlier).astype(i32), axis=2)
    pair = jnp.arange(2, dtype=i32)[None, :, None]

    wanted = (source[:, None, :] == me) & (rank[:, None, :] == pair)
    send_main = jnp.sum(jnp.where(wanted, inside[:, None, :], 0), axis=2)
    main_index = jnp.where(slabs[:, None] == me, blocks, send_main).reshape(-1)
    from_me = is_third & (source == me)
    third_of = jnp.sum(jnp.where(from_me, inside + 1, 0), axis=1) - 1

    step = jnp.arange(lanes, dtype=i32)[:, None]
    side = jnp.arange(2, dtype=i32)[None, :]
    third_asker = jnp.where(side == 0, half, 1 - half) * lanes + (lane + step) % lanes
    hit = third_asker[:, :, None] == slabs[None, None, :]
    third_index = jnp.sum(jnp.where(hit, third_of[None, None, :], 0), axis=2).reshape(-1)

    def row(of, array):
        return jnp.sum(jnp.where(slabs[:, None] == of, array, 0), axis=0)

    my_slot = row(me, jnp.where(is_third, -1, source * 2 + rank))
    is_jth = (is_third[:, None, :] & (order[:, None, :] == pair)).astype(i32)
    third_source = jnp.sum(is_jth * source[:, None, :], axis=2)
    third_request = jnp.sum(is_jth * numbers, axis=2)

    def steps(of):
        slab = row(of, third_source)
        return jnp.where(slab // lanes == half, (lane - slab % lanes + lanes) % lanes, -1)

    partner = (me + lanes) % ctx_count
    return main_index, third_index, my_slot, row(me, third_request), steps(me), steps(partner)


def body(queries, keys, values, out_grad, key_lists):
    ctx_count = lax.axis_size("ctx")
    blocks = lax.axis_size("head")
    lanes = ctx_count // 2
    main_index, third_index, my_slot, my_third, near_steps, cross_steps = plan(
        key_lists, blocks, ctx_count, lanes
    )

    def head_exchange(array):
        return lax.all_to_all(array, "head", split_axis=0, concat_axis=0, tiled=True)

    def ctx_exchange(array):
        return lax.all_to_all(array, "ctx", split_axis=0, concat_axis=0, tiled=True)

    def move(array, target):
        return lax.ppermute(array, "ctx", [(i, target(i)) for i in range(ctx_count)])

    def across(array):
        return move(array, lambda i: (i + lanes) % ctx_count)

    def along(arrays, sign):
        def target(step):
            return lambda i: i // lanes * lanes + (i + sign * step) % lanes

        return [arrays[0]] + [move(arrays[s], target(s)) for s in range(1, lanes)]

    kv = head_exchange(split_heads(keys, values))
    qg = head_exchange(split_heads(queries, out_grad))
    thirds, edge = pick_third(third_index, kv)
    edge = move(edge, lambda i: (i + 1) % ctx_count)
    thirds = along(thirds, 1)
    thirds[1], packed = lax.optimization_barrier((thirds[1], pack(main_index, kv)))
    cross = across(pick_cross(cross_steps, thirds))
    packed, edge, cross = lax.optimization_barrier((packed, edge, cross))
    main = ctx_exchange(packed)
    out, sums, edge_grad, main_grad, third_grad = attend(
        my_slot, my_third, near_steps, kv, qg, edge, cross, main, thirds
    )
    home = ctx_exchange(main_grad)
    cross_grad = across(third_grad)
    edge_grad = move(edge_grad, lambda i: (i - 1) % ctx_count)
    out, home, cross_grad, edge_grad = lax.optimization_barrier((out, home, cross_grad, edge_grad))
    out = head_exchange(out)
    late = along(pick_back(near_steps, cross_steps, third_grad, cross_grad, lanes), -1)
    total = land(main_index, sums, edge_grad, home)
    total, out = lax.optimization_barrier((total, out))
    total = land_thirds(third_index, total, late)
    attended, query_grad = join_heads(out)
    key_grad, value_grad = join_heads(head_exchange(total))
    return attended, query_grad, key_grad, value_grad


def solution(mesh):
    tokens = P(("ctx", "head"), None)
    return jax.shard_map(
        body,
        mesh=mesh,
        in_specs=(tokens, tokens, tokens, tokens, P()),
        out_specs=(tokens, tokens, tokens, tokens),
        check_vma=False,
    )
```

```python
import functools

import jax
import jax.numpy as jnp
from jax import lax
from jax.experimental import pallas as pl
from jax.experimental.pallas import tpu as pltpu
from jax.sharding import PartitionSpec as P

HEAD_DIM = 128
BLOCK = 128
ANY = pl.BlockSpec(memory_space=pl.ANY)
VMEM = pl.BlockSpec(memory_space=pltpu.VMEM)
SMEM = pl.BlockSpec(memory_space=pltpu.SMEM)
FULL = 60 * 1024 * 1024


def call(kernel, out_shape, ins, outs, name, flops, nbytes, scratch=(), limit=51 * 1024 * 1024, aliases=None):
    return pl.pallas_call(
        kernel,
        out_shape=out_shape,
        in_specs=list(ins),
        out_specs=outs,
        scratch_shapes=list(scratch),
        input_output_aliases=aliases or {},
        compiler_params=pltpu.CompilerParams(vmem_limit_bytes=limit),
        cost_estimate=pl.CostEstimate(flops=flops, bytes_accessed=nbytes, transcendentals=0),
        name=name,
    )


def start_all(copies):
    for copy in copies:
        copy.start()


def wait_all(copies):
    for copy in copies:
        copy.wait()


def dot(a, b, dims):
    return lax.dot_general(a, b, (dims, ((), ())), preferred_element_type=jnp.float32)


def split_kernel(heads, count, *refs):
    arrays, out = refs[:count], refs[count]
    held, packed, sems, out_sems = refs[count + 1 :]
    reads = [pltpu.make_async_copy(arrays[w], held.at[w], sems.at[w]) for w in range(count)]
    writes = []
    start_all(reads)
    for w in range(count):
        reads[w].wait()
        for head in range(heads):
            packed[head, w] = held[w, :, pl.ds(head * HEAD_DIM, HEAD_DIM)]
            sem = out_sems.at[w * heads + head]
            writes.append(pltpu.make_async_copy(packed.at[head, w], out.at[head, w], sem))
            writes[-1].start()
    wait_all(writes)


def split_heads(*arrays):
    rows, features = arrays[0].shape
    heads, count = features // HEAD_DIM, len(arrays)
    dtype = arrays[0].dtype
    packed = (heads, count, rows, HEAD_DIM)
    return call(
        functools.partial(split_kernel, heads, count),
        pltpu.HBM(packed, dtype),
        [ANY] * count,
        ANY,
        "split_heads",
        0,
        4 * count * arrays[0].size,
        [
            pltpu.VMEM((count, rows, features), dtype),
            pltpu.VMEM(packed, dtype),
            pltpu.SemaphoreType.DMA((count,)),
            pltpu.SemaphoreType.DMA((count * heads,)),
        ],
        FULL,
    )(*arrays)


def join_kernel(heads, count, in_ref, *refs):
    outs = refs[:count]
    held, sems = refs[count:]
    writes = [pltpu.make_async_copy(held.at[w], outs[w], sems.at[w]) for w in range(count)]
    for w in range(count):
        for head in range(heads):
            held[w, :, pl.ds(head * HEAD_DIM, HEAD_DIM)] = in_ref[head, w]
        writes[w].start()
    wait_all(writes)


def join_heads(packed):
    heads, count, rows, depth = packed.shape
    features, dtype = heads * depth, packed.dtype
    return call(
        functools.partial(join_kernel, heads, count),
        (pltpu.HBM((rows, features), dtype),) * count,
        [VMEM],
        (ANY,) * count,
        "join_heads",
        0,
        4 * packed.size,
        [pltpu.VMEM((count, rows, features), dtype), pltpu.SemaphoreType.DMA((count,))],
    )(packed)


def pick_third_kernel(blocks, lanes, third_ref, kv_ref, *refs):
    thirds, edge_ref = refs[:lanes], refs[lanes]
    edge_ref[...] = kv_ref[blocks - 1]
    for step in range(lanes):
        for side in range(2):
            index = third_ref[2 * step + side]

            @pl.when(index >= 0)
            def _():
                thirds[step][side] = kv_ref[index]


def pick_third(index, kv):
    lanes = index.shape[0] // 2
    outs = call(
        functools.partial(pick_third_kernel, kv.shape[0], lanes),
        (jax.ShapeDtypeStruct((2,) + kv.shape[1:], kv.dtype),) * lanes
        + (jax.ShapeDtypeStruct(kv.shape[1:], kv.dtype),),
        [SMEM, VMEM],
        (VMEM,) * (lanes + 1),
        "pick_third",
        0,
        8 * kv[0].size,
    )(index, kv)
    return outs[:lanes], outs[lanes]


def pack_kernel(rows, limit, index_ref, in_ref, out, sems):
    copies = [
        pltpu.make_async_copy(in_ref.at[jnp.minimum(index_ref[i], limit)], out.at[i], sems.at[i])
        for i in range(rows)
    ]
    start_all(copies)
    wait_all(copies)


def pack(index, array):
    rows = index.shape[0]
    return call(
        functools.partial(pack_kernel, rows, array.shape[0] - 1),
        pltpu.HBM((rows,) + array.shape[1:], array.dtype),
        [SMEM, VMEM],
        ANY,
        "pack",
        0,
        4 * rows * array[0].size,
        [pltpu.SemaphoreType.DMA((rows,))],
    )(index, array)


def pick_cross_kernel(lanes, step_ref, *refs):
    ins, out_ref = refs[:lanes], refs[lanes]
    for j in range(2):
        for step in range(lanes):

            @pl.when(step_ref[j] == step)
            def _():
                out_ref[j] = ins[step][1]


def pick_cross(steps, thirds):
    lanes = len(thirds)
    return call(
        functools.partial(pick_cross_kernel, lanes),
        jax.ShapeDtypeStruct(thirds[0].shape, thirds[0].dtype),
        [SMEM] + [VMEM] * lanes,
        VMEM,
        "pick_cross",
        0,
        4 * thirds[0].size,
    )(steps, *thirds)


def pick_back_kernel(lanes, near_ref, cross_ref, own, crossed, *outs):
    for j in range(2):
        for step in range(lanes):

            @pl.when(near_ref[j] == step)
            def _():
                outs[step][0] = own[j]

            @pl.when(cross_ref[j] == step)
            def _():
                outs[step][1] = crossed[j]


def pick_back(near_steps, cross_steps, own, crossed, lanes):
    return call(
        functools.partial(pick_back_kernel, lanes),
        (jax.ShapeDtypeStruct(own.shape, own.dtype),) * lanes,
        [SMEM, SMEM, VMEM, VMEM],
        (VMEM,) * lanes,
        "pick_back",
        0,
        8 * own.size,
    )(near_steps, cross_steps, own, crossed)


def attention(q, g, k, v):
    scale = HEAD_DIM ** (-0.5)
    s = dot(k, q, ((1,), (1,))) * scale
    dp = dot(v, g, ((1,), (1,)))
    w = jnp.exp(s - jnp.max(s, axis=0, keepdims=True))
    p = w * (1.0 / jnp.sum(w, axis=0, keepdims=True))
    p_low = p.astype(jnp.bfloat16)
    delta = jnp.sum(p_low.astype(jnp.float32) * dp, axis=0, keepdims=True)
    return p_low, (p * (dp - delta) * scale).astype(jnp.bfloat16)


def attend_kernel(
    blocks, lanes, slot_ref, third_ref, near_ref, kv_ref, qg_ref, edge_ref, cross, main, *refs
):
    thirds = refs[:lanes]
    out, sum_ref, edge_out, main_out, third_out = refs[lanes : lanes + 5]
    far_ref, out_ref, far_out, far_sems, done_sems, leave_sems = refs[lanes + 5 :]
    bf16 = jnp.bfloat16

    def arrive(r, slot):
        return pltpu.make_async_copy(main.at[slot], far_ref.at[r], far_sems.at[r])

    def finished(n):
        return pltpu.make_async_copy(out_ref.at[n], out.at[n], done_sems.at[n])

    def leave(r, slot):
        return pltpu.make_async_copy(far_out.at[r], main_out.at[slot], leave_sems.at[r])

    def when_main(r, do):
        @pl.when(slot_ref[r] >= 0)
        def _():
            do(r, slot_ref[r])

    def load(r, _):
        when_main(r, lambda r, slot: arrive(r, slot).start())

    lax.fori_loop(0, 2 * blocks, load, None)
    for j in range(2):
        r = third_ref[j]
        for step in range(1, lanes):

            @pl.when(near_ref[j] == step)
            def _():
                pltpu.make_async_copy(thirds[step].at[0], far_ref.at[r], far_sems.at[r]).start()

        @pl.when(near_ref[j] < 0)
        def _():
            pltpu.make_async_copy(cross.at[j], far_ref.at[r], far_sems.at[r]).start()

    def ready(n):
        for r in (2 * n, 2 * n + 1):
            arrive(r, 0).wait()

    def one(n, first):
        q, g = qg_ref[n, 0], qg_ref[n, 1]
        r2, r3 = 2 * n, 2 * n + 1
        listed = []
        for which in range(2):
            before = edge_ref[which] if first else kv_ref[n - 1, which]
            listed.append(
                jnp.concatenate([kv_ref[n, which], before, far_ref[r2, which], far_ref[r3, which]], axis=0)
            )
        k, v = listed
        p_low, ds = attention(q, g, k, v)
        out_ref[n, 0] = dot(p_low, v, ((0,), (0,))).astype(bf16)
        out_ref[n, 1] = dot(ds, k, ((0,), (0,))).astype(bf16)
        dk = dot(ds, q, ((1,), (0,)))
        dv = dot(p_low, g, ((1,), (0,)))
        for which, d in enumerate((dk, dv)):
            sum_ref[n, which] = d[:BLOCK]
            if first:
                edge_out[which] = d[BLOCK : 2 * BLOCK].astype(bf16)
            else:
                sum_ref[n - 1, which] += d[BLOCK : 2 * BLOCK]
            far_out[r2, which] = d[2 * BLOCK : 3 * BLOCK].astype(bf16)
            far_out[r3, which] = d[3 * BLOCK :].astype(bf16)

    def sent(n):
        finished(n).start()
        for r in (2 * n, 2 * n + 1):
            when_main(r, lambda r, slot: leave(r, slot).start())

    group = 3
    ready(0)
    one(0, True)
    sent(0)

    def several(at, _):
        first = 1 + at * group
        for i in range(group):
            ready(first + i)
        for i in range(group):
            one(first + i, False)
        for i in range(group):
            sent(first + i)

    lax.fori_loop(0, (blocks - 1) // group, several, None)
    for n in range(1 + (blocks - 1) // group * group, blocks):
        ready(n)
        one(n, False)
        sent(n)
    for j in range(2):
        third_out[j] = far_out[third_ref[j]]

    def finish(n, _):
        finished(n).wait()
        for r in (2 * n, 2 * n + 1):
            when_main(r, lambda r, slot: leave(r, slot).wait())

    lax.fori_loop(0, blocks, finish, None)


def attend(slot, third, near, kv, qg, edge, cross, main, thirds):
    blocks, lanes = kv.shape[0], len(thirds)
    bf16, f32 = kv.dtype, jnp.float32
    far = (2 * blocks,) + kv.shape[1:]
    return call(
        functools.partial(attend_kernel, blocks, lanes),
        (
            pltpu.HBM(qg.shape, bf16),
            jax.ShapeDtypeStruct(kv.shape, f32),
            jax.ShapeDtypeStruct(edge.shape, bf16),
            pltpu.HBM(main.shape, bf16),
            jax.ShapeDtypeStruct(cross.shape, bf16),
        ),
        [SMEM] * 3 + [VMEM] * 3 + [ANY] * (2 + lanes),
        (ANY, VMEM, VMEM, ANY, VMEM),
        "attend",
        5 * 2 * blocks * 4 * BLOCK * BLOCK * HEAD_DIM,
        2 * (6 * kv.size + 2 * main.size),
        [
            pltpu.VMEM(far, bf16),
            pltpu.VMEM(qg.shape, bf16),
            pltpu.VMEM(far, bf16),
            pltpu.SemaphoreType.DMA((2 * blocks,)),
            pltpu.SemaphoreType.DMA((blocks,)),
            pltpu.SemaphoreType.DMA((2 * blocks,)),
        ],
    )(slot, third, near, kv, qg, edge, cross, main, *thirds)


def land_kernel(blocks, slots, main_ref, sum_ref, edge_ref, home_ref, total, low):
    f32 = jnp.float32
    total[...] = sum_ref[...]
    total[blocks - 1] += edge_ref[...].astype(f32)
    for slot in range(slots):
        row = main_ref[slot]

        @pl.when(row < blocks)
        def _():
            total[row] += home_ref[slot].astype(f32)

    low[...] = total[...].astype(low.dtype)


def land(main_index, sums, edge, home):
    blocks, slots = sums.shape[0], home.shape[0]
    return call(
        functools.partial(land_kernel, blocks, slots),
        (pltpu.HBM(sums.shape, jnp.float32), pltpu.HBM(sums.shape, home.dtype)),
        [SMEM] + [VMEM] * 3,
        (VMEM, VMEM),
        "land",
        sums.size * 2,
        12 * sums.size,
    )(main_index, sums, edge, home)


def land_thirds_kernel(lanes, third_ref, once_ref, total, _, *refs):
    thirds, out = refs[:lanes], refs[lanes]
    held, low, late, in_sems, late_sems, sems = refs[lanes + 1 :]

    def read(at):
        row = once_ref[at]
        return pltpu.make_async_copy(total.at[row], held.at[row], in_sems.at[at])

    def arrive(at):
        step, side = divmod(at, 2)
        return pltpu.make_async_copy(thirds[step].at[side], late.at[at], late_sems.at[at])

    def write(at):
        row = once_ref[at]
        return pltpu.make_async_copy(low.at[row], out.at[row], sems.at[at])

    def add(at):
        held[third_ref[at]] += late[at].astype(jnp.float32)

    def put(at):
        row = once_ref[at]
        low[row] = held[row].astype(low.dtype)
        write(at).start()

    stages = (
        (third_ref, lambda at: arrive(at).start()),
        (once_ref, lambda at: read(at).start()),
        (third_ref, lambda at: arrive(at).wait()),
        (once_ref, lambda at: read(at).wait()),
        (third_ref, add),
        (once_ref, put),
        (once_ref, lambda at: write(at).wait()),
    )
    for table, do in stages:
        for at in range(2 * lanes):
            pl.when(table[at] >= 0)(functools.partial(do, at))


def land_thirds(third_index, once, total, low, thirds):
    lanes = len(thirds)
    dtype = low.dtype
    return call(
        functools.partial(land_thirds_kernel, lanes),
        pltpu.HBM(low.shape, dtype),
        [SMEM] * 2 + [ANY] * (2 + lanes),
        ANY,
        "land_thirds",
        total.size,
        total.size,
        [
            pltpu.VMEM(total.shape, jnp.float32),
            pltpu.VMEM(low.shape, dtype),
            pltpu.VMEM((2 * lanes,) + low.shape[1:], dtype),
            pltpu.SemaphoreType.DMA((2 * lanes,)),
            pltpu.SemaphoreType.DMA((2 * lanes,)),
            pltpu.SemaphoreType.DMA((2 * lanes,)),
        ],
        aliases={3: 0},
    )(third_index, once, total, low, *thirds)


def plan(key_lists, blocks, ctx_count, lanes):
    i32 = jnp.int32
    me = lax.axis_index("ctx")
    half, lane = me // lanes, me % lanes
    requests = 2 * blocks
    slabs = jnp.arange(ctx_count, dtype=i32)
    numbers = jnp.arange(requests, dtype=i32)
    far_all = key_lists[:, 2:].reshape(ctx_count, requests)
    source, inside = far_all // blocks, far_all % blocks
    earlier = (numbers[None, :] < numbers[:, None])[None]
    rank = jnp.sum(((source[:, None, :] == source[:, :, None]) & earlier).astype(i32), axis=2)
    is_third = rank == 2
    order = jnp.sum((is_third[:, None, :] & earlier).astype(i32), axis=2)
    pair = jnp.arange(2, dtype=i32)[None, :, None]

    wanted = (source[:, None, :] == me) & (rank[:, None, :] == pair)
    send_main = jnp.sum(jnp.where(wanted, inside[:, None, :], 0), axis=2)
    main_index = jnp.where(slabs[:, None] == me, blocks, send_main).reshape(-1)
    from_me = is_third & (source == me)
    third_of = jnp.sum(jnp.where(from_me, inside + 1, 0), axis=1) - 1

    step = jnp.arange(lanes, dtype=i32)[:, None]
    side = jnp.arange(2, dtype=i32)[None, :]
    third_asker = jnp.where(side == 0, half, 1 - half) * lanes + (lane + step) % lanes
    hit = third_asker[:, :, None] == slabs[None, None, :]
    third_index = jnp.sum(jnp.where(hit, third_of[None, None, :], 0), axis=2).reshape(-1)

    def row(of, array):
        return jnp.sum(jnp.where(slabs[:, None] == of, array, 0), axis=0)

    my_slot = row(me, jnp.where(is_third, -1, source * 2 + rank))
    is_jth = (is_third[:, None, :] & (order[:, None, :] == pair)).astype(i32)
    third_source = jnp.sum(is_jth * source[:, None, :], axis=2)
    third_request = jnp.sum(is_jth * numbers, axis=2)

    def steps(of):
        slab = row(of, third_source)
        return jnp.where(slab // lanes == half, (lane - slab % lanes + lanes) % lanes, -1)

    partner = (me + lanes) % ctx_count
    places = jnp.arange(2 * lanes, dtype=i32)
    same = (third_index[:, None] == third_index[None, :]) & (places[None, :] < places[:, None])
    once = jnp.where(jnp.any(same, axis=1), -1, third_index)
    return main_index, third_index, once, my_slot, row(me, third_request), steps(me), steps(partner)


def body(queries, keys, values, out_grad, key_lists):
    ctx_count = lax.axis_size("ctx")
    blocks = lax.axis_size("head")
    lanes = ctx_count // 2
    main_index, third_index, once, my_slot, my_third, near_steps, cross_steps = plan(
        key_lists, blocks, ctx_count, lanes
    )

    def head_exchange(array):
        return lax.all_to_all(array, "head", split_axis=0, concat_axis=0, tiled=True)

    def ctx_exchange(array):
        return lax.all_to_all(array, "ctx", split_axis=0, concat_axis=0, tiled=True)

    def move(array, target):
        return lax.ppermute(array, "ctx", [(i, target(i)) for i in range(ctx_count)])

    def across(array):
        return move(array, lambda i: (i + lanes) % ctx_count)

    def along(arrays, sign):
        def target(step):
            return lambda i: i // lanes * lanes + (i + sign * step) % lanes

        return [arrays[0]] + [move(arrays[s], target(s)) for s in range(1, lanes)]

    kv = head_exchange(split_heads(keys, values))
    qg = head_exchange(split_heads(queries, out_grad))
    thirds, edge = pick_third(third_index, kv)
    edge = move(edge, lambda i: (i + 1) % ctx_count)
    thirds = along(thirds, 1)
    thirds[1], packed = lax.optimization_barrier((thirds[1], pack(main_index, kv)))
    packed, edge, cross = lax.optimization_barrier((packed, edge, pick_cross(cross_steps, thirds)))
    cross = across(cross)
    main = ctx_exchange(packed)
    out, sums, edge_grad, main_grad, third_grad = attend(
        my_slot, my_third, near_steps, kv, qg, edge, cross, main, thirds
    )
    home = ctx_exchange(main_grad)
    cross_grad = across(third_grad)
    edge_grad = move(edge_grad, lambda i: (i - 1) % ctx_count)
    out, home, cross_grad, edge_grad = lax.optimization_barrier((out, home, cross_grad, edge_grad))
    out = head_exchange(out)
    late = along(pick_back(near_steps, cross_steps, third_grad, cross_grad, lanes), -1)
    total, low = land(main_index, sums, edge_grad, home)
    total, low, out = lax.optimization_barrier((total, low, out))
    low = land_thirds(third_index, once, total, low, late)
    attended, query_grad = join_heads(out)
    key_grad, value_grad = join_heads(head_exchange(low))
    return attended, query_grad, key_grad, value_grad


def solution(mesh):
    tokens = P(("ctx", "head"), None)
    return jax.shard_map(
        body,
        mesh=mesh,
        in_specs=(tokens, tokens, tokens, tokens, P()),
        out_specs=(tokens, tokens, tokens, tokens),
        check_vma=False,
    )
```

```python
import functools

import jax
import jax.numpy as jnp
from jax import lax
from jax.experimental import pallas as pl
from jax.experimental.pallas import tpu as pltpu
from jax.sharding import PartitionSpec as P

HEAD_DIM = 128
BLOCK = 128
ANY = pl.BlockSpec(memory_space=pl.ANY)
VMEM = pl.BlockSpec(memory_space=pltpu.VMEM)
SMEM = pl.BlockSpec(memory_space=pltpu.SMEM)
FULL = 60 * 1024 * 1024


def call(kernel, out_shape, ins, outs, name, flops, nbytes, scratch=(), limit=51 * 1024 * 1024, aliases=None):
    return pl.pallas_call(
        kernel,
        out_shape=out_shape,
        in_specs=list(ins),
        out_specs=outs,
        scratch_shapes=list(scratch),
        input_output_aliases=aliases or {},
        compiler_params=pltpu.CompilerParams(vmem_limit_bytes=limit),
        cost_estimate=pl.CostEstimate(flops=flops, bytes_accessed=nbytes, transcendentals=0),
        name=name,
    )


def start_all(copies):
    for copy in copies:
        copy.start()


def wait_all(copies):
    for copy in copies:
        copy.wait()


def dot(a, b, dims):
    return lax.dot_general(a, b, (dims, ((), ())), preferred_element_type=jnp.float32)


def split_kernel(heads, count, *refs):
    arrays, out = refs[:count], refs[count]
    held, packed, sems, out_sems = refs[count + 1 :]
    reads = [pltpu.make_async_copy(arrays[w], held.at[w], sems.at[w]) for w in range(count)]
    writes = []
    start_all(reads)
    for w in range(count):
        reads[w].wait()
        for head in range(heads):
            packed[head, w] = held[w, :, pl.ds(head * HEAD_DIM, HEAD_DIM)]
            sem = out_sems.at[w * heads + head]
            writes.append(pltpu.make_async_copy(packed.at[head, w], out.at[head, w], sem))
            writes[-1].start()
    wait_all(writes)


def split_heads(*arrays):
    rows, features = arrays[0].shape
    heads, count = features // HEAD_DIM, len(arrays)
    dtype = arrays[0].dtype
    packed = (heads, count, rows, HEAD_DIM)
    return call(
        functools.partial(split_kernel, heads, count),
        pltpu.HBM(packed, dtype),
        [ANY] * count,
        ANY,
        "split_heads",
        0,
        4 * count * arrays[0].size,
        [
            pltpu.VMEM((count, rows, features), dtype),
            pltpu.VMEM(packed, dtype),
            pltpu.SemaphoreType.DMA((count,)),
            pltpu.SemaphoreType.DMA((count * heads,)),
        ],
        FULL,
    )(*arrays)


def join_kernel(heads, count, in_ref, *refs):
    outs = refs[:count]
    held, sems = refs[count:]
    writes = [pltpu.make_async_copy(held.at[w], outs[w], sems.at[w]) for w in range(count)]
    for w in range(count):
        for head in range(heads):
            held[w, :, pl.ds(head * HEAD_DIM, HEAD_DIM)] = in_ref[head, w]
        writes[w].start()
    wait_all(writes)


def join_heads(packed):
    heads, count, rows, depth = packed.shape
    features, dtype = heads * depth, packed.dtype
    return call(
        functools.partial(join_kernel, heads, count),
        (pltpu.HBM((rows, features), dtype),) * count,
        [VMEM],
        (ANY,) * count,
        "join_heads",
        0,
        4 * packed.size,
        [pltpu.VMEM((count, rows, features), dtype), pltpu.SemaphoreType.DMA((count,))],
    )(packed)


def pick_third_kernel(blocks, lanes, third_ref, kv_ref, *refs):
    thirds, edge_ref = refs[:lanes], refs[lanes]
    edge_ref[...] = kv_ref[blocks - 1]
    for step in range(lanes):
        for side in range(2):
            index = third_ref[2 * step + side]

            @pl.when(index >= 0)
            def _():
                thirds[step][side] = kv_ref[index]


def pick_third(index, kv):
    lanes = index.shape[0] // 2
    outs = call(
        functools.partial(pick_third_kernel, kv.shape[0], lanes),
        (jax.ShapeDtypeStruct((2,) + kv.shape[1:], kv.dtype),) * lanes
        + (jax.ShapeDtypeStruct(kv.shape[1:], kv.dtype),),
        [SMEM, VMEM],
        (VMEM,) * (lanes + 1),
        "pick_third",
        0,
        8 * kv[0].size,
    )(index, kv)
    return outs[:lanes], outs[lanes]


def pack_kernel(rows, limit, index_ref, in_ref, out, sems):
    copies = [
        pltpu.make_async_copy(in_ref.at[jnp.minimum(index_ref[i], limit)], out.at[i], sems.at[i])
        for i in range(rows)
    ]
    start_all(copies)
    wait_all(copies)


def pack(index, array):
    rows = index.shape[0]
    return call(
        functools.partial(pack_kernel, rows, array.shape[0] - 1),
        pltpu.HBM((rows,) + array.shape[1:], array.dtype),
        [SMEM, VMEM],
        ANY,
        "pack",
        0,
        4 * rows * array[0].size,
        [pltpu.SemaphoreType.DMA((rows,))],
    )(index, array)


def pick_cross_kernel(lanes, step_ref, *refs):
    ins, out_ref = refs[:lanes], refs[lanes]
    for j in range(2):
        for step in range(lanes):

            @pl.when(step_ref[j] == step)
            def _():
                out_ref[j] = ins[step][1]


def pick_cross(steps, thirds):
    lanes = len(thirds)
    return call(
        functools.partial(pick_cross_kernel, lanes),
        jax.ShapeDtypeStruct(thirds[0].shape, thirds[0].dtype),
        [SMEM] + [VMEM] * lanes,
        VMEM,
        "pick_cross",
        0,
        4 * thirds[0].size,
    )(steps, *thirds)


def pick_back_kernel(lanes, near_ref, cross_ref, own, crossed, *outs):
    for j in range(2):
        for step in range(lanes):

            @pl.when(near_ref[j] == step)
            def _():
                outs[step][0] = own[j]

            @pl.when(cross_ref[j] == step)
            def _():
                outs[step][1] = crossed[j]


def pick_back(near_steps, cross_steps, own, crossed, lanes):
    return call(
        functools.partial(pick_back_kernel, lanes),
        (jax.ShapeDtypeStruct(own.shape, own.dtype),) * lanes,
        [SMEM, SMEM, VMEM, VMEM],
        (VMEM,) * lanes,
        "pick_back",
        0,
        8 * own.size,
    )(near_steps, cross_steps, own, crossed)


def attention(q, g, k, v):
    scale = HEAD_DIM ** (-0.5)
    s = dot(k, q, ((1,), (1,))) * scale
    dp = dot(v, g, ((1,), (1,)))
    w = jnp.exp(s - jnp.max(s, axis=0, keepdims=True))
    p = w * (1.0 / jnp.sum(w, axis=0, keepdims=True))
    p_low = p.astype(jnp.bfloat16)
    delta = jnp.sum(p_low.astype(jnp.float32) * dp, axis=0, keepdims=True)
    return p_low, (p * (dp - delta) * scale).astype(jnp.bfloat16)


def attend_kernel(
    blocks, lanes, slot_ref, third_ref, near_ref, kv_ref, qg_ref, edge_ref, cross, main, *refs
):
    thirds = refs[:lanes]
    out, sums, edge_out, main_out, third_out = refs[lanes : lanes + 5]
    far_ref, out_ref, sum_ref, far_out, far_sems, done_sems, leave_sems = refs[lanes + 5 :]
    bf16 = jnp.bfloat16

    def arrive(r, slot):
        return pltpu.make_async_copy(main.at[slot], far_ref.at[r], far_sems.at[r])

    def finished(n):
        return pltpu.make_async_copy(out_ref.at[n], out.at[n], done_sems.at[0, n])

    def summed(n):
        return pltpu.make_async_copy(sum_ref.at[n], sums.at[n], done_sems.at[1, n])

    def leave(r, slot):
        return pltpu.make_async_copy(far_out.at[r], main_out.at[slot], leave_sems.at[r])

    def when_main(r, do):
        @pl.when(slot_ref[r] >= 0)
        def _():
            do(r, slot_ref[r])

    def load(r, _):
        when_main(r, lambda r, slot: arrive(r, slot).start())

    lax.fori_loop(0, 2 * blocks, load, None)
    for j in range(2):
        r = third_ref[j]
        for step in range(1, lanes):

            @pl.when(near_ref[j] == step)
            def _():
                pltpu.make_async_copy(thirds[step].at[0], far_ref.at[r], far_sems.at[r]).start()

        @pl.when(near_ref[j] < 0)
        def _():
            pltpu.make_async_copy(cross.at[j], far_ref.at[r], far_sems.at[r]).start()

    def ready(n):
        for r in (2 * n, 2 * n + 1):
            arrive(r, 0).wait()

    def one(n, first):
        q, g = qg_ref[n, 0], qg_ref[n, 1]
        r2, r3 = 2 * n, 2 * n + 1
        listed = []
        for which in range(2):
            before = edge_ref[which] if first else kv_ref[n - 1, which]
            listed.append(
                jnp.concatenate([kv_ref[n, which], before, far_ref[r2, which], far_ref[r3, which]], axis=0)
            )
        k, v = listed
        p_low, ds = attention(q, g, k, v)
        out_ref[n, 0] = dot(p_low, v, ((0,), (0,))).astype(bf16)
        out_ref[n, 1] = dot(ds, k, ((0,), (0,))).astype(bf16)
        dk = dot(ds, q, ((1,), (0,)))
        dv = dot(p_low, g, ((1,), (0,)))
        for which, d in enumerate((dk, dv)):
            sum_ref[n, which] = d[:BLOCK]
            if first:
                edge_out[which] = d[BLOCK : 2 * BLOCK].astype(bf16)
            else:
                sum_ref[n - 1, which] += d[BLOCK : 2 * BLOCK]
            far_out[r2, which] = d[2 * BLOCK : 3 * BLOCK].astype(bf16)
            far_out[r3, which] = d[3 * BLOCK :].astype(bf16)

    def sent(n, first):
        finished(n).start()
        if not first:
            summed(n - 1).start()
        for r in (2 * n, 2 * n + 1):
            when_main(r, lambda r, slot: leave(r, slot).start())

    group = 5
    ready(0)
    one(0, True)
    sent(0, True)

    def several(at, _):
        first = 1 + at * group
        for i in range(group):
            ready(first + i)
        for i in range(group):
            one(first + i, False)
        for i in range(group):
            sent(first + i, False)

    lax.fori_loop(0, (blocks - 1) // group, several, None)
    for n in range(1 + (blocks - 1) // group * group, blocks):
        ready(n)
        one(n, False)
        sent(n, False)
    summed(blocks - 1).start()
    for j in range(2):
        third_out[j] = far_out[third_ref[j]]

    def finish(n, _):
        finished(n).wait()
        summed(n).wait()
        for r in (2 * n, 2 * n + 1):
            when_main(r, lambda r, slot: leave(r, slot).wait())

    lax.fori_loop(0, blocks, finish, None)


def attend(slot, third, near, kv, qg, edge, cross, main, thirds):
    blocks, lanes = kv.shape[0], len(thirds)
    bf16, f32 = kv.dtype, jnp.float32
    far = (2 * blocks,) + kv.shape[1:]
    return call(
        functools.partial(attend_kernel, blocks, lanes),
        (
            pltpu.HBM(qg.shape, bf16),
            pltpu.HBM(kv.shape, f32),
            jax.ShapeDtypeStruct(edge.shape, bf16),
            pltpu.HBM(main.shape, bf16),
            jax.ShapeDtypeStruct(cross.shape, bf16),
        ),
        [SMEM] * 3 + [VMEM] * 3 + [ANY] * (2 + lanes),
        (ANY, ANY, VMEM, ANY, VMEM),
        "attend",
        5 * 2 * blocks * 4 * BLOCK * BLOCK * HEAD_DIM,
        2 * (6 * kv.size + 2 * main.size),
        [
            pltpu.VMEM(far, bf16),
            pltpu.VMEM(qg.shape, bf16),
            pltpu.VMEM(kv.shape, f32),
            pltpu.VMEM(far, bf16),
            pltpu.SemaphoreType.DMA((2 * blocks,)),
            pltpu.SemaphoreType.DMA((2, blocks)),
            pltpu.SemaphoreType.DMA((2 * blocks,)),
        ],
    )(slot, third, near, kv, qg, edge, cross, main, *thirds)


def land_kernel(blocks, slots, main_ref, sum_ref, edge_ref, home_ref, total, low):
    f32 = jnp.float32
    total[...] = sum_ref[...]
    total[blocks - 1] += edge_ref[...].astype(f32)
    for slot in range(slots):
        row = main_ref[slot]

        @pl.when(row < blocks)
        def _():
            total[row] += home_ref[slot].astype(f32)

    low[...] = total[...].astype(low.dtype)


def land(main_index, sums, edge, home):
    blocks, slots = sums.shape[0], home.shape[0]
    return call(
        functools.partial(land_kernel, blocks, slots),
        (pltpu.HBM(sums.shape, jnp.float32), pltpu.HBM(sums.shape, home.dtype)),
        [SMEM] + [VMEM] * 3,
        (VMEM, VMEM),
        "land",
        sums.size * 2,
        12 * sums.size,
    )(main_index, sums, edge, home)


def land_thirds_kernel(lanes, third_ref, once_ref, total, _, *refs):
    thirds, out = refs[:lanes], refs[lanes]
    held, low, late, in_sems, late_sems, sems = refs[lanes + 1 :]

    def read(at):
        row = once_ref[at]
        return pltpu.make_async_copy(total.at[row], held.at[row], in_sems.at[at])

    def arrive(at):
        step, side = divmod(at, 2)
        return pltpu.make_async_copy(thirds[step].at[side], late.at[at], late_sems.at[at])

    def write(at):
        row = once_ref[at]
        return pltpu.make_async_copy(low.at[row], out.at[row], sems.at[at])

    def add(at):
        held[third_ref[at]] += late[at].astype(jnp.float32)

    def put(at):
        row = once_ref[at]
        low[row] = held[row].astype(low.dtype)
        write(at).start()

    stages = (
        (third_ref, lambda at: arrive(at).start()),
        (once_ref, lambda at: read(at).start()),
        (third_ref, lambda at: arrive(at).wait()),
        (once_ref, lambda at: read(at).wait()),
        (third_ref, add),
        (once_ref, put),
        (once_ref, lambda at: write(at).wait()),
    )
    for table, do in stages:
        for at in range(2 * lanes):
            pl.when(table[at] >= 0)(functools.partial(do, at))


def land_thirds(third_index, once, total, low, thirds):
    lanes = len(thirds)
    dtype = low.dtype
    return call(
        functools.partial(land_thirds_kernel, lanes),
        pltpu.HBM(low.shape, dtype),
        [SMEM] * 2 + [ANY] * (2 + lanes),
        ANY,
        "land_thirds",
        total.size,
        total.size,
        [
            pltpu.VMEM(total.shape, jnp.float32),
            pltpu.VMEM(low.shape, dtype),
            pltpu.VMEM((2 * lanes,) + low.shape[1:], dtype),
            pltpu.SemaphoreType.DMA((2 * lanes,)),
            pltpu.SemaphoreType.DMA((2 * lanes,)),
            pltpu.SemaphoreType.DMA((2 * lanes,)),
        ],
        aliases={3: 0},
    )(third_index, once, total, low, *thirds)


def plan(key_lists, blocks, ctx_count, lanes):
    i32 = jnp.int32
    me = lax.axis_index("ctx")
    half, lane = me // lanes, me % lanes
    requests = 2 * blocks
    slabs = jnp.arange(ctx_count, dtype=i32)
    numbers = jnp.arange(requests, dtype=i32)
    far_all = key_lists[:, 2:].reshape(ctx_count, requests)
    source, inside = far_all // blocks, far_all % blocks
    earlier = (numbers[None, :] < numbers[:, None])[None]
    rank = jnp.sum(((source[:, None, :] == source[:, :, None]) & earlier).astype(i32), axis=2)
    is_third = rank == 2
    order = jnp.sum((is_third[:, None, :] & earlier).astype(i32), axis=2)
    pair = jnp.arange(2, dtype=i32)[None, :, None]

    wanted = (source[:, None, :] == me) & (rank[:, None, :] == pair)
    send_main = jnp.sum(jnp.where(wanted, inside[:, None, :], 0), axis=2)
    main_index = jnp.where(slabs[:, None] == me, blocks, send_main).reshape(-1)
    from_me = is_third & (source == me)
    third_of = jnp.sum(jnp.where(from_me, inside + 1, 0), axis=1) - 1

    step = jnp.arange(lanes, dtype=i32)[:, None]
    side = jnp.arange(2, dtype=i32)[None, :]
    third_asker = jnp.where(side == 0, half, 1 - half) * lanes + (lane + step) % lanes
    hit = third_asker[:, :, None] == slabs[None, None, :]
    third_index = jnp.sum(jnp.where(hit, third_of[None, None, :], 0), axis=2).reshape(-1)

    def row(of, array):
        return jnp.sum(jnp.where(slabs[:, None] == of, array, 0), axis=0)

    my_slot = row(me, jnp.where(is_third, -1, source * 2 + rank))
    is_jth = (is_third[:, None, :] & (order[:, None, :] == pair)).astype(i32)
    third_source = jnp.sum(is_jth * source[:, None, :], axis=2)
    third_request = jnp.sum(is_jth * numbers, axis=2)

    def steps(of):
        slab = row(of, third_source)
        return jnp.where(slab // lanes == half, (lane - slab % lanes + lanes) % lanes, -1)

    partner = (me + lanes) % ctx_count
    places = jnp.arange(2 * lanes, dtype=i32)
    same = (third_index[:, None] == third_index[None, :]) & (places[None, :] < places[:, None])
    once = jnp.where(jnp.any(same, axis=1), -1, third_index)
    return main_index, third_index, once, my_slot, row(me, third_request), steps(me), steps(partner)


def body(queries, keys, values, out_grad, key_lists):
    ctx_count = lax.axis_size("ctx")
    blocks = lax.axis_size("head")
    lanes = ctx_count // 2
    main_index, third_index, once, my_slot, my_third, near_steps, cross_steps = plan(
        key_lists, blocks, ctx_count, lanes
    )

    def head_exchange(array):
        return lax.all_to_all(array, "head", split_axis=0, concat_axis=0, tiled=True)

    def ctx_exchange(array):
        return lax.all_to_all(array, "ctx", split_axis=0, concat_axis=0, tiled=True)

    def move(array, target):
        return lax.ppermute(array, "ctx", [(i, target(i)) for i in range(ctx_count)])

    def across(array):
        return move(array, lambda i: (i + lanes) % ctx_count)

    def along(arrays, sign):
        def target(step):
            return lambda i: i // lanes * lanes + (i + sign * step) % lanes

        return [arrays[0]] + [move(arrays[s], target(s)) for s in range(1, lanes)]

    kv = head_exchange(split_heads(keys, values))
    qg = head_exchange(split_heads(queries, out_grad))
    thirds, edge = pick_third(third_index, kv)
    edge = move(edge, lambda i: (i + 1) % ctx_count)
    thirds = along(thirds, 1)
    thirds[1], packed = lax.optimization_barrier((thirds[1], pack(main_index, kv)))
    cross = across(pick_cross(cross_steps, thirds))
    packed, edge, cross = lax.optimization_barrier((packed, edge, cross))
    main = ctx_exchange(packed)
    out, sums, edge_grad, main_grad, third_grad = attend(
        my_slot, my_third, near_steps, kv, qg, edge, cross, main, thirds
    )
    home = ctx_exchange(main_grad)
    cross_grad = across(third_grad)
    edge_grad = move(edge_grad, lambda i: (i - 1) % ctx_count)
    out, home, cross_grad, edge_grad = lax.optimization_barrier((out, home, cross_grad, edge_grad))
    out = head_exchange(out)
    late = along(pick_back(near_steps, cross_steps, third_grad, cross_grad, lanes), -1)
    total, low = land(main_index, sums, edge_grad, home)
    total, low, out = lax.optimization_barrier((total, low, out))
    low = land_thirds(third_index, once, total, low, late)
    attended, query_grad = join_heads(out)
    key_grad, value_grad = join_heads(head_exchange(low))
    return attended, query_grad, key_grad, value_grad


def solution(mesh):
    tokens = P(("ctx", "head"), None)
    return jax.shard_map(
        body,
        mesh=mesh,
        in_specs=(tokens, tokens, tokens, tokens, P()),
        out_specs=(tokens, tokens, tokens, tokens),
        check_vma=False,
    )
```
